32 devices in a mesh: rows: 4 (over y, x), cols: 8 (over z, core).
Axes of the slice: x: 2, y: 2, z: 4, core: 2. Of those that a mesh axis runs over, the one named last changes fastest.
Arguments:
- dosage: int32 [512, 12288], P('cols', 'rows'), may hold values from 0 to 2
- present: int32 [512, 12288], P('cols', 'rows'), may hold values from 0 to 1, as said below
- components: float32 [32, 12288], P(None, 'rows'), may hold values from -8 to 8
Outputs:
- kinship: float32 [12288, 12288], P('rows', 'cols')
The draws below stay inside these ranges and needn't reach their ends.
Inputs may be any that keep to these rules, and one draw needn't show every extreme that they name: `present`: markers whose index is a multiple of 8 are observed for every person.
All inputs are finite; a program needn't handle non-finite values.
Results may differ from the reference program's by a relative error of at most 0.0036.
Values may be sent and summed in bfloat16 or wider, within the bound.
No kernel may reach another device: no remote copies, remote signals or barrier semaphores. Data moves between devices by JAX's collectives and lax.ppermute only.
A program may use at most 128 MiB of HBM per device.

```python
import jax
import jax.numpy as jnp
from jax import lax

MARKERS = 512
COMPS = 32
PEOPLE_DEV = 3072
PEOPLE = 12288


def ancestry_groups(key):
    return jax.random.randint(jax.random.fold_in(key, 101), (PEOPLE,), 0, 4)


def draw_dosage(key, part):
    groups = ancestry_groups(key)
    percent = jax.random.randint(jax.random.fold_in(key, 102), (MARKERS, 4), 1, 100)
    level = percent[:, groups]
    first = jax.random.randint(jax.random.fold_in(key, 103), (MARKERS, PEOPLE), 0, 100)
    second = jax.random.randint(jax.random.fold_in(key, 104), (MARKERS, PEOPLE), 0, 100)
    return ((first < level).astype(jnp.int32) + (second < level).astype(jnp.int32)).astype(jnp.int32)


def draw_present(key, part):
    roll = jax.random.randint(jax.random.fold_in(key, 201), (MARKERS, PEOPLE), 0, 10)
    marker_index = jnp.arange(MARKERS, dtype=jnp.int32)[:, None]
    always = (marker_index % 8 == 0).astype(jnp.int32)
    return jnp.maximum((roll >= 1).astype(jnp.int32), always).astype(jnp.int32)


def draw_components(key, part):
    groups = ancestry_groups(key)
    centers = 1.5 * jax.random.normal(jax.random.fold_in(key, 105), (COMPS, 4), jnp.float32)
    noise = jax.random.normal(jax.random.fold_in(key, 106), (COMPS, PEOPLE), jnp.float32)
    return jnp.clip(centers[:, groups] + noise, -8.0, 8.0).astype(jnp.float32)


def setup_inputs(seed: int = 0) -> dict:
    key_of = jax.random.split(jax.random.key(seed), 4)
    return {
        "dosage": draw_dosage(jax.random.fold_in(key_of[3], 71), 0),
        "present": draw_present(jax.random.fold_in(key_of[3], 71), 0),
        "components": draw_components(jax.random.fold_in(key_of[3], 71), 0),
    }


def solve_normal(gram, moment):
    width = gram.shape[0]
    index_col = jnp.arange(width, dtype=jnp.int32)[:, None]
    columns = []
    for j in range(width):
        column = gram[:, j, :]
        if j > 0:
            stacked = jnp.stack(columns, axis=1)
            column = column - lax.optimization_barrier(jnp.sum(stacked * stacked[j][None, :, :], axis=1))
        pivot = jnp.sqrt(column[j])
        columns.append(jnp.where(index_col >= j, column / pivot[None, :], jnp.zeros_like(column)))
    factor = jnp.stack(columns, axis=1)
    forward = []
    for j in range(width):
        value = moment[j]
        for k in range(j):
            value = value - factor[j, k] * forward[k]
        forward.append(value / factor[j, j])
    backward = [None] * width
    for j in range(width - 1, -1, -1):
        value = forward[j]
        for k in range(j + 1, width):
            value = value - factor[k, j] * backward[k]
        backward[j] = value / factor[j, j]
    return jnp.stack(backward, axis=0)

def fit_panel(dosage, present, components):
    design = jnp.concatenate([jnp.ones((1, components.shape[1]), jnp.float32), components.astype(jnp.float32)], axis=0)
    width = design.shape[0]
    observed = present.astype(jnp.float32)
    target = 0.5 * dosage.astype(jnp.float32) * observed
    outer_rows = (design[:, None, :] * design[None, :, :]).reshape(width * width, design.shape[1])
    gram_flat = jnp.dot(outer_rows, observed.T, precision=lax.Precision.HIGHEST, preferred_element_type=jnp.float32)
    moment = jnp.dot(design, target.T, precision=lax.Precision.HIGHEST, preferred_element_type=jnp.float32)
    markers_here = observed.shape[0]
    gram = gram_flat.reshape(width, width, markers_here)
    coef = solve_normal(gram, moment)
    fitted = jnp.dot(coef.T, design, precision=lax.Precision.HIGHEST, preferred_element_type=jnp.float32)
    freq = jnp.clip(fitted, 0.01, 0.99)
    resid = (observed * (dosage.astype(jnp.float32) - 2.0 * freq)).astype(jnp.bfloat16)
    sdev = (observed * jnp.sqrt(freq * (1.0 - freq))).astype(jnp.bfloat16)
    return (resid, sdev)

def reference(dosage, present, components):
    resid, sdev = fit_panel(dosage, present, components)
    contract = (((0,), (0,)), ((), ()))
    block = PEOPLE_DEV
    count = PEOPLE // block

    def one_block(index):
        start = (index * block).astype(jnp.int32)
        left_r = lax.dynamic_slice_in_dim(resid, start, block, 1)
        left_s = lax.dynamic_slice_in_dim(sdev, start, block, 1)
        numer = lax.dot_general(left_r, resid, contract, preferred_element_type=jnp.float32)
        denom = lax.dot_general(left_s, sdev, contract, preferred_element_type=jnp.float32)
        return numer / (4.0 * denom)
    tiles = lax.map(one_block, jnp.arange(count, dtype=jnp.int32))
    return tiles.reshape(PEOPLE, PEOPLE)
```

```python
import functools

import jax
import jax.numpy as jnp
from jax import lax
from jax.experimental import pallas as pl
from jax.experimental.pallas import tpu as pltpu
from jax.sharding import PartitionSpec as P

F32, BF16 = jnp.float32, jnp.bfloat16
VMEM_LIMIT = 56 * 1024 * 1024
SUB = 8


def split3(x):
    high = x.astype(BF16)
    rest = x - high.astype(F32)
    mid = rest.astype(BF16)
    low = (rest - mid.astype(F32)).astype(BF16)
    return high, mid, low


def group_starts(comps):
    starts, at = [], 0
    for j in range(comps):
        first = j // SUB * SUB
        starts.append((at, first))
        at += comps - first
    return starts, at


def gram_kernel(dosage_ref, present_ref, comps_ref, out_ref, lhs_ref):
    comps, people = comps_ref.shape
    markers = dosage_ref.shape[0]
    starts, total = group_starts(comps)
    chunk = 512 if people % 512 == 0 else people
    acc = None
    for at in range(0, people, chunk):
        span = slice(at, at + chunk)
        obs = present_ref[:, span].astype(F32)
        tgt = 0.5 * dosage_ref[:, span].astype(F32) * obs
        rhs = jnp.concatenate([obs, tgt], axis=0).astype(BF16)
        x = comps_ref[:, span]
        for j, (start, first) in enumerate(starts):
            lhs_ref[start : start + comps - first, :] = x[first:, :] * x[j : j + 1, :]
        lhs_ref[total : total + comps, :] = x
        tail = lhs_ref.shape[0] - total - comps
        lhs_ref[total + comps :, :] = jnp.ones((tail, chunk), F32)
        for part in split3(lhs_ref[...]):
            term = lax.dot_general(part, rhs, (((1,), (1,)), ((), ())), preferred_element_type=F32)
            acc = term if acc is None else acc + term
    half = total // 2
    out_ref[0:half, :] = jnp.concatenate([acc[0:half, 0:markers], acc[half:total, 0:markers]], axis=1)
    out_ref[half:, :] = acc[total : total + comps + SUB, :]


def gram_call(dosage, present, components):
    markers, people = dosage.shape
    comps = components.shape[0]
    total = group_starts(comps)[1]
    chunk = 512 if people % 512 == 0 else people
    return pl.pallas_call(
        gram_kernel,
        out_shape=jax.ShapeDtypeStruct((total // 2 + comps + SUB, 2 * markers), F32),
        scratch_shapes=[pltpu.VMEM((total + comps + 2 * SUB, chunk), F32)],
        compiler_params=pltpu.CompilerParams(vmem_limit_bytes=VMEM_LIMIT),
        name="gram",
    )(dosage, present, components)


def coef_rows(comps):
    return 6 * comps + 2 * SUB


def below(old, first, new):
    return new if first == 0 else jnp.concatenate([old[:first], new], axis=0)


def solve_kernel(comps, markers, *refs):
    out_ref = refs[-1]
    summed = refs[0][...]
    for ref in refs[1:-1]:
        summed = summed + ref[...]
    starts, total = group_starts(comps)
    half = total // 2
    left, right = summed[:, 0:markers], summed[:, markers : 2 * markers]

    def rows_of(start, count):
        if start + count <= half:
            return left[start : start + count]
        if start >= half:
            return right[start - half : start - half + count]
        return jnp.concatenate([left[start:half], right[0 : start + count - half]], axis=0)

    columns = [rows_of(start, comps - first) for start, first in starts]
    firsts = [first for _, first in starts]
    edge = left[half : half + comps]
    count = left[half + comps : half + comps + 1]
    moment = right[half : half + comps]
    moment_one = right[half + comps : half + comps + 1]
    factor, edge_f, moment_f = [], [], []
    for j in range(comps):
        first = firsts[j]
        column = columns[j]
        inv = 1.0 / column[j - first : j - first + 1]
        scaled = column * inv
        edge_j = edge[j : j + 1]
        moment_j = moment[j : j + 1]
        edge_s, moment_s = edge_j * inv, moment_j * inv
        row = lax.broadcasted_iota(jnp.int32, column.shape, 0) + first
        factor.append(jnp.where(row > j, scaled, 0.0))
        edge_f.append(edge_s)
        moment_f.append(moment_s)
        count = count - edge_s * edge_j
        moment_one = moment_one - edge_s * moment_j
        if j + 1 < comps:
            edge = below(edge, first, edge[first:] - column * edge_s)
            moment = below(moment, first, moment[first:] - column * moment_s)
        for k in range(j + 1, comps):
            offset = firsts[k] - first
            columns[k] = columns[k] - scaled[offset:] * column[k - first : k - first + 1]
    last = moment_one / count
    index = lax.broadcasted_iota(jnp.int32, (SUB, markers), 0)
    groups = [jnp.zeros((SUB, markers), F32) for _ in range(comps // SUB)]
    for j in range(comps - 1, -1, -1):
        first = firsts[j]
        value = moment_f[j] - edge_f[j] * last
        total_term = None
        for g in range(first // SUB, comps // SUB):
            term = factor[j][g * SUB - first : (g + 1) * SUB - first] * groups[g]
            total_term = term if total_term is None else total_term + term
        value = value - jnp.sum(total_term, axis=0, keepdims=True)
        g = j // SUB
        groups[g] = jnp.where(index == j - first, value, groups[g])
    coef = jnp.concatenate(groups, axis=0)
    c1, c2, c3 = [part.astype(F32) for part in split3(coef)]
    l1, l2, l3 = [part.astype(F32) for part in split3(last)]
    index = lax.broadcasted_iota(jnp.int32, (2 * SUB, markers), 0)
    ones = jnp.where(index == 0, l1, jnp.where(index == 1, l2, jnp.where(index == 2, l3, 0.0)))
    stacked = jnp.concatenate([c1, c1, c2, c2, c1, c3, ones], axis=0).astype(BF16)
    eye = (
        lax.broadcasted_iota(jnp.int32, (markers, markers), 0)
        == lax.broadcasted_iota(jnp.int32, (markers, markers), 1)
    ).astype(F32).astype(BF16)
    turned = lax.dot_general(eye, stacked, (((1,), (1,)), ((), ())), preferred_element_type=F32)
    out_ref[...] = turned.astype(BF16)


def solve_call(parts, comps, markers):
    return pl.pallas_call(
        functools.partial(solve_kernel, comps, markers),
        out_shape=jax.ShapeDtypeStruct((markers, coef_rows(comps)), BF16),
        compiler_params=pltpu.CompilerParams(vmem_limit_bytes=VMEM_LIMIT),
        name="solve",
    )(*parts)


def design_parts(x):
    d1, d2, d3 = split3(x)
    ones = jnp.ones((2 * SUB, x.shape[1]), BF16)
    return jnp.concatenate([d1, d2, d1, d2, d3, d1, ones], axis=0)


def panel(coef, x, dosage, present):
    fitted = lax.dot_general(
        coef, design_parts(x), (((1,), (0,)), ((), ())), preferred_element_type=F32
    )
    freq = jnp.clip(fitted, 0.01, 0.99)
    observed = present.astype(F32)
    resid = observed * (dosage.astype(F32) - 2.0 * freq)
    sdev = observed * jnp.sqrt(freq * (1.0 - freq))
    return resid.astype(BF16), (2.0 * sdev).astype(BF16)


def kin_kernel(rows, ratio, cols, raw_ref, comps_ref, col_comps_ref, *refs):
    coef_refs = refs[:cols]
    piece_refs = refs[cols : cols + rows * ratio]
    out_ref, coef, raw_cols, col_r, col_s, sems = refs[cols + rows * ratio :]
    here = coef_refs[0].shape[0]
    width = out_ref.shape[1]

    @pl.when(pl.program_id(0) == 0)
    def _():
        r = lax.axis_index("rows")
        q = lax.axis_index("cols")
        copies = []
        for d in range(cols):
            place = pl.multiple_of((q ^ d) * here, here)
            copies.append(
                pltpu.make_async_copy(coef_refs[d], coef.at[pl.ds(place, here), :], sems.at[len(copies)])
            )
        for d in range(rows):
            for k in range(ratio):
                owner = (r ^ d) * ratio + lax.rem(lax.rem(q, ratio) + ratio - k, ratio)
                place = pl.multiple_of(owner * here, here)
                copies.append(
                    pltpu.make_async_copy(
                        piece_refs[d * ratio + k],
                        raw_cols.at[:, pl.ds(place, here), :],
                        sems.at[len(copies)],
                    )
                )
        for copy in copies:
            copy.start()
        for copy in copies:
            copy.wait()
        step = 256 if width % 256 == 0 else width
        for at in range(0, width, step):
            span = slice(at, at + step)
            resid, sdev = panel(
                coef[...], col_comps_ref[:, span], raw_cols[0, :, span], raw_cols[1, :, span]
            )
            col_r[:, span] = resid
            col_s[:, span] = sdev

    resid, sdev = panel(coef[...], comps_ref[...], raw_ref[0], raw_ref[1])
    contract = (((0,), (0,)), ((), ()))
    step = 512 if width % 512 == 0 else width
    for at in range(0, width, step):
        span = slice(at, at + step)
        numer = lax.dot_general(resid, col_r[:, span], contract, preferred_element_type=F32)
        denom = lax.dot_general(sdev, col_s[:, span], contract, preferred_element_type=F32)
        out_ref[:, span] = numer / denom


def kin_call(rows, ratio, cols, raw, components, col_comps, coefs, pieces):
    _, markers, people = raw.shape
    comps, width = col_comps.shape
    tile = 512 if people % 512 == 0 else people
    anywhere = pl.BlockSpec(memory_space=pl.ANY)
    return pl.pallas_call(
        functools.partial(kin_kernel, rows, ratio, cols),
        grid=(people // tile,),
        in_specs=[
            pl.BlockSpec((2, markers, tile), lambda i: (0, 0, i)),
            pl.BlockSpec((comps, tile), lambda i: (0, i)),
            pl.BlockSpec((comps, width), lambda i: (0, 0)),
        ]
        + [anywhere] * (len(coefs) + len(pieces)),
        out_specs=pl.BlockSpec((tile, width), lambda i: (i, 0)),
        out_shape=jax.ShapeDtypeStruct((people, width), F32),
        scratch_shapes=[
            pltpu.VMEM((markers, coef_rows(comps)), BF16),
            pltpu.VMEM((2, markers, width), BF16),
            pltpu.VMEM((markers, width), BF16),
            pltpu.VMEM((markers, width), BF16),
            pltpu.SemaphoreType.DMA((len(coefs) + len(pieces),)),
        ],
        compiler_params=pltpu.CompilerParams(vmem_limit_bytes=VMEM_LIMIT),
        name="kinship",
    )(raw, components, col_comps, *coefs, *pieces)


def per_device(dosage, present, components):
    rows, cols = lax.axis_size("rows"), lax.axis_size("cols")
    ratio = cols // rows
    markers, people = dosage.shape
    comps = components.shape[0]
    width = people // ratio
    col = lax.axis_index("cols")
    raw = jnp.stack([dosage.astype(BF16), present.astype(BF16)])
    raw_rows = lax.all_gather(raw, "cols", axis=1, tiled=True)

    def across(x, axis, size):
        return [x] + [lax.ppermute(x, axis, [(i, i ^ d) for i in range(size)]) for d in range(1, size)]

    both = ("rows", "cols")
    pieces = []
    for k in range(ratio):
        part = (col % ratio + k) % ratio
        mine = lax.dynamic_slice_in_dim(raw, part * width, width, 2)
        moves = [
            (r * cols + z * ratio + c, z * cols + r * ratio + (c + k) % ratio)
            for r in range(rows)
            for z in range(rows)
            for c in range(ratio)
        ]
        pieces.append(lax.ppermute(mine, both, moves) if len(moves) > 1 else mine)
        if k == 0:
            mine = lax.dynamic_slice_in_dim(components, part * width, width, 1)
            col_comps = lax.ppermute(mine, both, moves) if len(moves) > 1 else mine
    spread = [across(piece, "rows", rows) for piece in pieces]
    pieces = [spread[k][d] for d in range(rows) for k in range(ratio)]

    gram = gram_call(dosage, present, components)
    coef = solve_call(across(gram, "rows", rows), comps, markers)
    coefs = across(coef, "cols", cols)
    return kin_call(rows, ratio, cols, raw_rows, components, col_comps, coefs, pieces)


def solution(mesh):
    placed = (P("cols", "rows"), P("cols", "rows"), P(None, "rows"))
    return jax.shard_map(
        per_device, mesh=mesh, in_specs=placed, out_specs=P("rows", "cols"), check_vma=False
    )
```

```python
import functools

import jax
import jax.numpy as jnp
from jax import lax
from jax.experimental import pallas as pl
from jax.experimental.pallas import tpu as pltpu
from jax.sharding import PartitionSpec as P

F32, BF16 = jnp.float32, jnp.bfloat16
VMEM_LIMIT = 56 * 1024 * 1024
SUB = 8
CHUNKS = 2


def split3(x):
    high = x.astype(BF16)
    rest = x - high.astype(F32)
    mid = rest.astype(BF16)
    low = (rest - mid.astype(F32)).astype(BF16)
    return high, mid, low


def group_starts(comps):
    starts, at = [], 0
    for j in range(comps):
        first = j // SUB * SUB
        starts.append((at, first))
        at += comps - first
    return starts, at


def gram_kernel(dosage_ref, present_ref, comps_ref, out_ref, lhs_ref):
    comps, people = comps_ref.shape
    markers = dosage_ref.shape[0]
    starts, total = group_starts(comps)
    chunk = 512 if people % 512 == 0 else people
    acc = None
    for at in range(0, people, chunk):
        span = slice(at, at + chunk)
        obs = present_ref[:, span].astype(F32)
        tgt = 0.5 * dosage_ref[:, span].astype(F32) * obs
        rhs = jnp.concatenate([obs, tgt], axis=0).astype(BF16)
        x = comps_ref[:, span]
        for j, (start, first) in enumerate(starts):
            lhs_ref[start : start + comps - first, :] = x[first:, :] * x[j : j + 1, :]
        lhs_ref[total : total + comps, :] = x
        tail = lhs_ref.shape[0] - total - comps
        lhs_ref[total + comps :, :] = jnp.ones((tail, chunk), F32)
        for part in split3(lhs_ref[...]):
            term = lax.dot_general(part, rhs, (((1,), (1,)), ((), ())), preferred_element_type=F32)
            acc = term if acc is None else acc + term
    half = total // 2
    out_ref[0:half, :] = jnp.concatenate([acc[0:half, 0:markers], acc[half:total, 0:markers]], axis=1)
    out_ref[half:, :] = acc[total : total + comps + SUB, :]


def gram_call(dosage, present, components):
    markers, people = dosage.shape
    comps = components.shape[0]
    total = group_starts(comps)[1]
    chunk = 512 if people % 512 == 0 else people
    return pl.pallas_call(
        gram_kernel,
        out_shape=jax.ShapeDtypeStruct((total // 2 + comps + SUB, 2 * markers), F32),
        scratch_shapes=[pltpu.VMEM((total + comps + 2 * SUB, chunk), F32)],
        compiler_params=pltpu.CompilerParams(vmem_limit_bytes=VMEM_LIMIT),
        name="gram",
    )(dosage, present, components)


def coef_rows(comps):
    return 6 * comps + 2 * SUB


def below(old, first, new):
    return new if first == 0 else jnp.concatenate([old[:first], new], axis=0)


def solve_kernel(comps, markers, *refs):
    out_ref = refs[-1]
    summed = refs[0][...]
    for ref in refs[1:-1]:
        summed = summed + ref[...]
    starts, total = group_starts(comps)
    half = total // 2
    left, right = summed[:, 0:markers], summed[:, markers : 2 * markers]

    def rows_of(start, count):
        if start + count <= half:
            return left[start : start + count]
        if start >= half:
            return right[start - half : start - half + count]
        return jnp.concatenate([left[start:half], right[0 : start + count - half]], axis=0)

    columns = [rows_of(start, comps - first) for start, first in starts]
    firsts = [first for _, first in starts]
    edge = left[half : half + comps]
    count = left[half + comps : half + comps + 1]
    moment = right[half : half + comps]
    moment_one = right[half + comps : half + comps + 1]
    factor, edge_f, moment_f = [], [], []
    for j in range(comps):
        first = firsts[j]
        column = columns[j]
        inv = 1.0 / column[j - first : j - first + 1]
        scaled = column * inv
        edge_j = edge[j : j + 1]
        moment_j = moment[j : j + 1]
        edge_s, moment_s = edge_j * inv, moment_j * inv
        row = lax.broadcasted_iota(jnp.int32, column.shape, 0) + first
        factor.append(jnp.where(row > j, scaled, 0.0))
        edge_f.append(edge_s)
        moment_f.append(moment_s)
        count = count - edge_s * edge_j
        moment_one = moment_one - edge_s * moment_j
        if j + 1 < comps:
            edge = below(edge, first, edge[first:] - column * edge_s)
            moment = below(moment, first, moment[first:] - column * moment_s)
        for k in range(j + 1, comps):
            offset = firsts[k] - first
            columns[k] = columns[k] - scaled[offset:] * column[k - first : k - first + 1]
    last = moment_one / count
    index = lax.broadcasted_iota(jnp.int32, (SUB, markers), 0)
    groups = [jnp.zeros((SUB, markers), F32) for _ in range(comps // SUB)]
    for j in range(comps - 1, -1, -1):
        first = firsts[j]
        value = moment_f[j] - edge_f[j] * last
        total_term = None
        for g in range(first // SUB, comps // SUB):
            term = factor[j][g * SUB - first : (g + 1) * SUB - first] * groups[g]
            total_term = term if total_term is None else total_term + term
        value = value - jnp.sum(total_term, axis=0, keepdims=True)
        g = j // SUB
        groups[g] = jnp.where(index == j - first, value, groups[g])
    coef = jnp.concatenate(groups, axis=0)
    c1, c2, c3 = [part.astype(F32) for part in split3(coef)]
    l1, l2, l3 = [part.astype(F32) for part in split3(last)]
    index = lax.broadcasted_iota(jnp.int32, (2 * SUB, markers), 0)
    ones = jnp.where(index == 0, l1, jnp.where(index == 1, l2, jnp.where(index == 2, l3, 0.0)))
    stacked = jnp.concatenate([c1, c1, c2, c2, c1, c3, ones], axis=0).astype(BF16)
    eye = (
        lax.broadcasted_iota(jnp.int32, (markers, markers), 0)
        == lax.broadcasted_iota(jnp.int32, (markers, markers), 1)
    ).astype(F32).astype(BF16)
    turned = lax.dot_general(eye, stacked, (((1,), (1,)), ((), ())), preferred_element_type=F32)
    out_ref[...] = turned.astype(BF16)


def solve_call(parts, comps, markers):
    return pl.pallas_call(
        functools.partial(solve_kernel, comps, markers),
        out_shape=jax.ShapeDtypeStruct((markers, coef_rows(comps)), BF16),
        compiler_params=pltpu.CompilerParams(vmem_limit_bytes=VMEM_LIMIT),
        name="solve",
    )(*parts)


def design_parts(x):
    d1, d2, d3 = split3(x)
    ones = jnp.ones((2 * SUB, x.shape[1]), BF16)
    return jnp.concatenate([d1, d2, d1, d2, d3, d1, ones], axis=0)


def panel(coef, x, dosage, present):
    fitted = lax.dot_general(
        coef, design_parts(x), (((1,), (0,)), ((), ())), preferred_element_type=F32
    )
    freq = jnp.clip(fitted, 0.01, 0.99)
    observed = present.astype(F32)
    resid = observed * (dosage.astype(F32) - 2.0 * freq)
    sdev = observed * jnp.sqrt(freq * (1.0 - freq))
    return resid.astype(BF16), (2.0 * sdev).astype(BF16)


def reversed_bits(value, size):
    bits = size.bit_length() - 1
    return sum(((value >> i) & 1) << (bits - 1 - i) for i in range(bits))


def line_of(plane, source, size):
    return source ^ reversed_bits(plane, size)


def columns_kernel(rows, ratio, cols, col_comps_ref, *refs):
    coef_refs = refs[:cols]
    piece_refs = refs[cols : cols + rows * ratio]
    coef_out, col_r, col_s, coef, raw_cols, sems = refs[cols + rows * ratio :]
    here = coef_refs[0].shape[0]
    width = col_r.shape[1]
    r = lax.axis_index("rows")
    q = lax.axis_index("cols")
    copies = []
    for d in range(cols):
        place = pl.multiple_of((q ^ d) * here, here)
        copies.append(
            pltpu.make_async_copy(coef_refs[d], coef.at[pl.ds(place, here), :], sems.at[len(copies)])
        )
    for d in range(rows):
        for k in range(ratio):
            source = line_of(q // ratio, r ^ d, rows)
            owner = source * ratio + lax.rem(lax.rem(q, ratio) + ratio - k, ratio)
            place = pl.multiple_of(owner * here, here)
            copies.append(
                pltpu.make_async_copy(
                    piece_refs[d * ratio + k],
                    raw_cols.at[:, pl.ds(place, here), :],
                    sems.at[len(copies)],
                )
            )
    for copy in copies:
        copy.start()
    for copy in copies:
        copy.wait()
    coef_out[...] = coef[...]
    step = 256 if width % 256 == 0 else width
    for at in range(0, width, step):
        span = slice(at, at + step)
        resid, sdev = panel(
            coef[...], col_comps_ref[:, span], raw_cols[0, :, span], raw_cols[1, :, span]
        )
        col_r[:, span] = resid
        col_s[:, span] = sdev


def columns_call(rows, ratio, cols, col_comps, coefs, pieces):
    comps, width = col_comps.shape
    markers = coefs[0].shape[0] * cols
    anywhere = pl.BlockSpec(memory_space=pl.ANY)
    return pl.pallas_call(
        functools.partial(columns_kernel, rows, ratio, cols),
        in_specs=[pl.BlockSpec(memory_space=pltpu.VMEM)] + [anywhere] * (len(coefs) + len(pieces)),
        out_shape=(
            jax.ShapeDtypeStruct((markers, coef_rows(comps)), BF16),
            jax.ShapeDtypeStruct((markers, width), BF16),
            jax.ShapeDtypeStruct((markers, width), BF16),
        ),
        scratch_shapes=[
            pltpu.VMEM((markers, coef_rows(comps)), BF16),
            pltpu.VMEM((2, markers, width), BF16),
            pltpu.SemaphoreType.DMA((len(coefs) + len(pieces),)),
        ],
        compiler_params=pltpu.CompilerParams(vmem_limit_bytes=VMEM_LIMIT),
        name="columns",
    )(col_comps, *coefs, *pieces)


def kin_kernel(raw_ref, comps_ref, coef_ref, col_r, col_s, *refs):
    out_ref = refs[-1]
    width = out_ref.shape[1]
    resid, sdev = panel(coef_ref[...], comps_ref[...], raw_ref[0], raw_ref[1])
    contract = (((0,), (0,)), ((), ()))
    step = 512 if width % 512 == 0 else width
    for at in range(0, width, step):
        span = slice(at, at + step)
        numer = lax.dot_general(resid, col_r[:, span], contract, preferred_element_type=F32)
        denom = lax.dot_general(sdev, col_s[:, span], contract, preferred_element_type=F32)
        out_ref[:, span] = numer / denom


def kin_call(start, raw, components, coef, col_r, col_s, before):
    _, markers, count = raw.shape
    comps, people = components.shape
    width = col_r.shape[1]
    tile = 512 if count % 512 == 0 else count
    first = start // tile
    whole = lambda i: (0, 0)
    in_specs = [
        pl.BlockSpec((2, markers, tile), lambda i: (0, 0, i)),
        pl.BlockSpec((comps, tile), lambda i: (0, i + first)),
        pl.BlockSpec(coef.shape, whole),
        pl.BlockSpec((markers, width), whole),
        pl.BlockSpec((markers, width), whole),
    ]
    operands = [raw, components, coef, col_r, col_s]
    aliases = {}
    if before is not None:
        in_specs.append(pl.BlockSpec(memory_space=pl.ANY))
        aliases = {len(operands): 0}
        operands.append(before)
    return pl.pallas_call(
        kin_kernel,
        grid=(count // tile,),
        in_specs=in_specs,
        out_specs=pl.BlockSpec((tile, width), lambda i: (i + first, 0)),
        out_shape=jax.ShapeDtypeStruct((people, width), F32),
        input_output_aliases=aliases,
        compiler_params=pltpu.CompilerParams(vmem_limit_bytes=VMEM_LIMIT),
        name="kinship",
    )(*operands)


def per_device(dosage, present, components):
    rows, cols = lax.axis_size("rows"), lax.axis_size("cols")
    ratio = cols // rows
    markers, people = dosage.shape
    comps = components.shape[0]
    width = people // ratio
    col = lax.axis_index("cols")
    raw = jnp.stack([dosage.astype(BF16), present.astype(BF16)])

    def across(x, axis, size):
        return [x] + [lax.ppermute(x, axis, [(i, i ^ d) for i in range(size)]) for d in range(1, size)]

    both = ("rows", "cols")
    pieces = []
    for k in range(ratio):
        part = (col % ratio + k) % ratio
        mine = lax.dynamic_slice_in_dim(raw, part * width, width, 2)
        moves = [
            (r * cols + z * ratio + c, line_of(r, z, rows) * cols + r * ratio + (c + k) % ratio)
            for r in range(rows)
            for z in range(rows)
            for c in range(ratio)
        ]
        pieces.append(lax.ppermute(mine, both, moves) if len(moves) > 1 else mine)
        if k == 0:
            mine = lax.dynamic_slice_in_dim(components, part * width, width, 1)
            col_comps = lax.ppermute(mine, both, moves) if len(moves) > 1 else mine
    raw, *pieces = lax.optimization_barrier((raw, *pieces))
    starts = [people * i // CHUNKS for i in range(CHUNKS + 1)]
    raw_rows = [
        lax.all_gather(raw[:, :, a:b], "cols", axis=1, tiled=True) for a, b in zip(starts, starts[1:])
    ]
    spread = [across(piece, "rows", rows) for piece in pieces]
    pieces = [spread[k][d] for d in range(rows) for k in range(ratio)]

    gram = gram_call(dosage, present, components)
    coef = solve_call(across(gram, "rows", rows), comps, markers)
    coefs = across(coef, "cols", cols)
    coef, col_r, col_s = columns_call(rows, ratio, cols, col_comps, coefs, pieces)
    out = None
    for start, part in zip(starts, raw_rows):
        out = kin_call(start, part, components, coef, col_r, col_s, out)
    return out


def solution(mesh):
    placed = (P("cols", "rows"), P("cols", "rows"), P(None, "rows"))
    return jax.shard_map(
        per_device, mesh=mesh, in_specs=placed, out_specs=P("rows", "cols"), check_vma=False
    )
```

```python
import functools

import jax
import jax.numpy as jnp
from jax import lax
from jax.experimental import pallas as pl
from jax.experimental.pallas import tpu as pltpu
from jax.sharding import PartitionSpec as P

F32, BF16 = jnp.float32, jnp.bfloat16
VMEM_LIMIT = 56 * 1024 * 1024
SUB = 8
CHUNKS = 1


def split3(x):
    high = x.astype(BF16)
    rest = x - high.astype(F32)
    mid = rest.astype(BF16)
    low = (rest - mid.astype(F32)).astype(BF16)
    return high, mid, low


def group_starts(comps):
    starts, at = [], 0
    for j in range(comps):
        first = j // SUB * SUB
        starts.append((at, first))
        at += comps - first
    return starts, at


def gram_kernel(dosage_ref, present_ref, comps_ref, out_ref, lhs_ref):
    comps, people = comps_ref.shape
    markers = dosage_ref.shape[0]
    starts, total = group_starts(comps)
    chunk = 512 if people % 512 == 0 else people
    acc = None
    for at in range(0, people, chunk):
        span = slice(at, at + chunk)
        obs = present_ref[:, span].astype(F32)
        tgt = 0.5 * dosage_ref[:, span].astype(F32) * obs
        rhs = jnp.concatenate([obs, tgt], axis=0).astype(BF16)
        x = comps_ref[:, span]
        for j, (start, first) in enumerate(starts):
            lhs_ref[start : start + comps - first, :] = x[first:, :] * x[j : j + 1, :]
        lhs_ref[total : total + comps, :] = x
        tail = lhs_ref.shape[0] - total - comps
        lhs_ref[total + comps :, :] = jnp.ones((tail, chunk), F32)
        for part in split3(lhs_ref[...]):
            term = lax.dot_general(part, rhs, (((1,), (1,)), ((), ())), preferred_element_type=F32)
            acc = term if acc is None else acc + term
    half = total // 2
    out_ref[0:half, :] = jnp.concatenate([acc[0:half, 0:markers], acc[half:total, 0:markers]], axis=1)
    out_ref[half:, :] = acc[total : total + comps + SUB, :]


def gram_call(dosage, present, components):
    markers, people = dosage.shape
    comps = components.shape[0]
    total = group_starts(comps)[1]
    chunk = 512 if people % 512 == 0 else people
    return pl.pallas_call(
        gram_kernel,
        out_shape=jax.ShapeDtypeStruct((total // 2 + comps + SUB, 2 * markers), F32),
        scratch_shapes=[pltpu.VMEM((total + comps + 2 * SUB, chunk), F32)],
        compiler_params=pltpu.CompilerParams(vmem_limit_bytes=VMEM_LIMIT),
        name="gram",
    )(dosage, present, components)


def coef_rows(comps):
    return 6 * comps + 2 * SUB


def below(old, first, new):
    return new if first == 0 else jnp.concatenate([old[:first], new], axis=0)


def solve_kernel(comps, markers, *refs):
    out_ref = refs[-1]
    summed = refs[0][...]
    for ref in refs[1:-1]:
        summed = summed + ref[...]
    starts, total = group_starts(comps)
    half = total // 2
    left, right = summed[:, 0:markers], summed[:, markers : 2 * markers]

    def rows_of(start, count):
        if start + count <= half:
            return left[start : start + count]
        if start >= half:
            return right[start - half : start - half + count]
        return jnp.concatenate([left[start:half], right[0 : start + count - half]], axis=0)

    columns = [rows_of(start, comps - first) for start, first in starts]
    firsts = [first for _, first in starts]
    edge = left[half : half + comps]
    count = left[half + comps : half + comps + 1]
    moment = right[half : half + comps]
    moment_one = right[half + comps : half + comps + 1]
    factor, edge_f, moment_f = [], [], []
    for j in range(comps):
        first = firsts[j]
        column = columns[j]
        inv = 1.0 / column[j - first : j - first + 1]
        scaled = column * inv
        edge_j = edge[j : j + 1]
        moment_j = moment[j : j + 1]
        edge_s, moment_s = edge_j * inv, moment_j * inv
        row = lax.broadcasted_iota(jnp.int32, column.shape, 0) + first
        factor.append(jnp.where(row > j, scaled, 0.0))
        edge_f.append(edge_s)
        moment_f.append(moment_s)
        count = count - edge_s * edge_j
        moment_one = moment_one - edge_s * moment_j
        if j + 1 < comps:
            edge = below(edge, first, edge[first:] - column * edge_s)
            moment = below(moment, first, moment[first:] - column * moment_s)
        for k in range(j + 1, comps):
            offset = firsts[k] - first
            columns[k] = columns[k] - scaled[offset:] * column[k - first : k - first + 1]
    last = moment_one / count
    index = lax.broadcasted_iota(jnp.int32, (SUB, markers), 0)
    groups = [jnp.zeros((SUB, markers), F32) for _ in range(comps // SUB)]
    for j in range(comps - 1, -1, -1):
        first = firsts[j]
        value = moment_f[j] - edge_f[j] * last
        total_term = None
        for g in range(first // SUB, comps // SUB):
            term = factor[j][g * SUB - first : (g + 1) * SUB - first] * groups[g]
            total_term = term if total_term is None else total_term + term
        value = value - jnp.sum(total_term, axis=0, keepdims=True)
        g = j // SUB
        groups[g] = jnp.where(index == j - first, value, groups[g])
    coef = jnp.concatenate(groups, axis=0)
    c1, c2, c3 = [part.astype(F32) for part in split3(coef)]
    l1, l2, l3 = [part.astype(F32) for part in split3(last)]
    index = lax.broadcasted_iota(jnp.int32, (2 * SUB, markers), 0)
    ones = jnp.where(index == 0, l1, jnp.where(index == 1, l2, jnp.where(index == 2, l3, 0.0)))
    stacked = jnp.concatenate([c1, c1, c2, c2, c1, c3, ones], axis=0).astype(BF16)
    eye = (
        lax.broadcasted_iota(jnp.int32, (markers, markers), 0)
        == lax.broadcasted_iota(jnp.int32, (markers, markers), 1)
    ).astype(F32).astype(BF16)
    turned = lax.dot_general(eye, stacked, (((1,), (1,)), ((), ())), preferred_element_type=F32)
    out_ref[...] = turned.astype(BF16)


def solve_call(parts, comps, markers):
    return pl.pallas_call(
        functools.partial(solve_kernel, comps, markers),
        out_shape=jax.ShapeDtypeStruct((markers, coef_rows(comps)), BF16),
        compiler_params=pltpu.CompilerParams(vmem_limit_bytes=VMEM_LIMIT),
        name="solve",
    )(*parts)


def design_parts(x):
    d1, d2, d3 = split3(x)
    ones = jnp.ones((2 * SUB, x.shape[1]), BF16)
    return jnp.concatenate([d1, d2, d1, d2, d3, d1, ones], axis=0)


def panel(coef, x, dosage, present):
    fitted = lax.dot_general(
        coef, design_parts(x), (((1,), (0,)), ((), ())), preferred_element_type=F32
    )
    freq = jnp.clip(fitted, 0.01, 0.99)
    observed = present.astype(F32)
    resid = observed * (dosage.astype(F32) - 2.0 * freq)
    sdev = observed * jnp.sqrt(freq * (1.0 - freq))
    return resid.astype(BF16), (2.0 * sdev).astype(BF16)


def columns_kernel(rows, ratio, cols, col_comps_ref, *refs):
    coef_refs = refs[:cols]
    piece_refs = refs[cols : cols + rows]
    coef_out, col_r, col_s, coef, raw_cols, sems = refs[cols + rows :]
    here = coef_refs[0].shape[0]
    width = col_r.shape[1]
    r = lax.axis_index("rows")
    q = lax.axis_index("cols")
    copies = []
    for d in range(cols):
        place = pl.multiple_of((q ^ d) * here, here)
        copies.append(
            pltpu.make_async_copy(coef_refs[d], coef.at[pl.ds(place, here), :], sems.at[len(copies)])
        )
    height = piece_refs[0].shape[1]
    for d in range(rows):
        begin = (r ^ d) * height
        k, part, inside = begin // (2 * here), lax.rem(begin // here, 2), lax.rem(begin, here)
        for e in range(rows):
            owner = ((q // ratio) ^ e) * ratio + lax.rem(q + ratio - k, ratio)
            place = pl.multiple_of(owner * here + inside, height)
            copies.append(
                pltpu.make_async_copy(
                    piece_refs[d].at[e], raw_cols.at[part, pl.ds(place, height), :], sems.at[len(copies)]
                )
            )
    for copy in copies:
        copy.start()
    for copy in copies:
        copy.wait()
    coef_out[...] = coef[...]
    step = 256 if width % 256 == 0 else width
    for at in range(0, width, step):
        span = slice(at, at + step)
        resid, sdev = panel(
            coef[...], col_comps_ref[:, span], raw_cols[0, :, span], raw_cols[1, :, span]
        )
        col_r[:, span] = resid
        col_s[:, span] = sdev


def columns_call(rows, ratio, cols, col_comps, coefs, pieces):
    comps, width = col_comps.shape
    markers = coefs[0].shape[0] * cols
    anywhere = pl.BlockSpec(memory_space=pl.ANY)
    return pl.pallas_call(
        functools.partial(columns_kernel, rows, ratio, cols),
        in_specs=[pl.BlockSpec(memory_space=pltpu.VMEM)] + [anywhere] * (len(coefs) + len(pieces)),
        out_shape=(
            jax.ShapeDtypeStruct((markers, coef_rows(comps)), BF16),
            jax.ShapeDtypeStruct((markers, width), BF16),
            jax.ShapeDtypeStruct((markers, width), BF16),
        ),
        scratch_shapes=[
            pltpu.VMEM((markers, coef_rows(comps)), BF16),
            pltpu.VMEM((2, markers, width), BF16),
            pltpu.SemaphoreType.DMA((cols + rows * rows,)),
        ],
        compiler_params=pltpu.CompilerParams(vmem_limit_bytes=VMEM_LIMIT),
        name="columns",
    )(col_comps, *coefs, *pieces)


def kin_kernel(raw_ref, comps_ref, coef_ref, col_r, col_s, *refs):
    out_ref = refs[-1]
    width = out_ref.shape[1]
    resid, sdev = panel(coef_ref[...], comps_ref[...], raw_ref[0], raw_ref[1])
    contract = (((0,), (0,)), ((), ()))
    step = 512 if width % 512 == 0 else width
    for at in range(0, width, step):
        span = slice(at, at + step)
        numer = lax.dot_general(resid, col_r[:, span], contract, preferred_element_type=F32)
        denom = lax.dot_general(sdev, col_s[:, span], contract, preferred_element_type=F32)
        out_ref[:, span] = numer / denom


def kin_call(start, raw, components, coef, col_r, col_s, before):
    _, markers, count = raw.shape
    comps, people = components.shape
    width = col_r.shape[1]
    tile = 512 if count % 512 == 0 else count
    first = start // tile
    whole = lambda i: (0, 0)
    in_specs = [
        pl.BlockSpec((2, markers, tile), lambda i: (0, 0, i)),
        pl.BlockSpec((comps, tile), lambda i: (0, i + first)),
        pl.BlockSpec(coef.shape, whole),
        pl.BlockSpec((markers, width), whole),
        pl.BlockSpec((markers, width), whole),
    ]
    operands = [raw, components, coef, col_r, col_s]
    aliases = {}
    if before is not None:
        in_specs.append(pl.BlockSpec(memory_space=pl.ANY))
        aliases = {len(operands): 0}
        operands.append(before)
    return pl.pallas_call(
        kin_kernel,
        grid=(count // tile,),
        in_specs=in_specs,
        out_specs=pl.BlockSpec((tile, width), lambda i: (i + first, 0)),
        out_shape=jax.ShapeDtypeStruct((people, width), F32),
        input_output_aliases=aliases,
        compiler_params=pltpu.CompilerParams(vmem_limit_bytes=VMEM_LIMIT),
        name="kinship",
    )(*operands)


def per_device(dosage, present, components):
    rows, cols = lax.axis_size("rows"), lax.axis_size("cols")
    ratio = cols // rows
    markers, people = dosage.shape
    comps = components.shape[0]
    width = people // ratio
    col = lax.axis_index("cols")
    raw = jnp.stack([dosage.astype(BF16), present.astype(BF16)])

    def across(x, axis, size):
        return [x] + [lax.ppermute(x, axis, [(i, i ^ d) for i in range(size)]) for d in range(1, size)]

    starts = [people * i // CHUNKS for i in range(CHUNKS + 1)]
    raw_rows = [
        lax.all_gather(raw[:, :, a:b], "cols", axis=1, tiled=True) for a, b in zip(starts, starts[1:])
    ]

    row = lax.axis_index("rows")
    core, plane = col % ratio, col // ratio
    halves = []
    for k in range(ratio):
        part = (core + k) % ratio
        mine = lax.dynamic_slice_in_dim(raw, part * width, width, 2).reshape(2 * markers, width)
        swaps = [(z * ratio + c, z * ratio + (c + k) % ratio) for z in range(rows) for c in range(ratio)]
        halves.append(lax.ppermute(mine, "cols", swaps) if k else mine)
    held = jnp.concatenate(halves, axis=0)
    height = held.shape[0] // rows
    quarters = []
    for d in range(rows):
        mine = lax.dynamic_slice_in_dim(held, (row ^ d) * height, height, 0)
        quarters.append(lax.ppermute(mine, "rows", [(i, i ^ d) for i in range(rows)]) if d else mine)
    quarters = jnp.stack(quarters)
    moved = []
    for e in range(rows):
        mine = lax.dynamic_index_in_dim(quarters, row ^ plane ^ e, 0, keepdims=False)
        hops = [(z * ratio + c, (z ^ e) * ratio + c) for z in range(rows) for c in range(ratio)]
        moved.append(lax.ppermute(mine, "cols", hops) if e else mine)
    pieces = across(jnp.stack(moved), "rows", rows)

    mine = lax.dynamic_slice_in_dim(components, core * width, width, 1)
    moves = [
        (r * cols + z * ratio + c, z * cols + r * ratio + c)
        for r in range(rows)
        for z in range(rows)
        for c in range(ratio)
    ]
    col_comps = lax.ppermute(mine, ("rows", "cols"), moves)

    gram = gram_call(dosage, present, components)
    coef = solve_call(across(gram, "rows", rows), comps, markers)
    coefs = across(coef, "cols", cols)
    coef, col_r, col_s = columns_call(rows, ratio, cols, col_comps, coefs, pieces)
    out = None
    for start, part in zip(starts, raw_rows):
        out = kin_call(start, part, components, coef, col_r, col_s, out)
    return out


def solution(mesh):
    placed = (P("cols", "rows"), P("cols", "rows"), P(None, "rows"))
    return jax.shard_map(
        per_device, mesh=mesh, in_specs=placed, out_specs=P("rows", "cols"), check_vma=False
    )
```

```python
import functools

import jax
import jax.numpy as jnp
from jax import lax
from jax.experimental import pallas as pl
from jax.experimental.pallas import tpu as pltpu
from jax.sharding import PartitionSpec as P

F32, BF16 = jnp.float32, jnp.bfloat16
VMEM_LIMIT = 56 * 1024 * 1024
SUB = 8
CHUNKS = 1


def split3(x):
    high = x.astype(BF16)
    rest = x - high.astype(F32)
    mid = rest.astype(BF16)
    low = (rest - mid.astype(F32)).astype(BF16)
    return high, mid, low


def group_starts(comps):
    starts, at = [], 0
    for j in range(comps):
        first = j // SUB * SUB
        starts.append((at, first))
        at += comps - first
    return starts, at


def gram_kernel(dosage_ref, present_ref, comps_ref, out_ref, lhs_ref):
    comps, people = comps_ref.shape
    markers = dosage_ref.shape[0]
    starts, total = group_starts(comps)
    chunk = 512 if people % 512 == 0 else people
    acc = None
    for at in range(0, people, chunk):
        span = slice(at, at + chunk)
        obs = present_ref[:, span].astype(F32)
        tgt = 0.5 * dosage_ref[:, span].astype(F32) * obs
        rhs = jnp.concatenate([obs, tgt], axis=0).astype(BF16)
        x = comps_ref[:, span]
        for j, (start, first) in enumerate(starts):
            lhs_ref[start : start + comps - first, :] = x[first:, :] * x[j : j + 1, :]
        lhs_ref[total : total + comps, :] = x
        tail = lhs_ref.shape[0] - total - comps
        lhs_ref[total + comps :, :] = jnp.ones((tail, chunk), F32)
        for part in split3(lhs_ref[...]):
            term = lax.dot_general(part, rhs, (((1,), (1,)), ((), ())), preferred_element_type=F32)
            acc = term if acc is None else acc + term
    half = total // 2
    out_ref[0:half, :] = jnp.concatenate([acc[0:half, 0:markers], acc[half:total, 0:markers]], axis=1)
    out_ref[half:, :] = acc[total : total + comps + SUB, :]


def gram_call(dosage, present, components):
    markers, people = dosage.shape
    comps = components.shape[0]
    total = group_starts(comps)[1]
    chunk = 512 if people % 512 == 0 else people
    return pl.pallas_call(
        gram_kernel,
        out_shape=jax.ShapeDtypeStruct((total // 2 + comps + SUB, 2 * markers), F32),
        scratch_shapes=[pltpu.VMEM((total + comps + 2 * SUB, chunk), F32)],
        compiler_params=pltpu.CompilerParams(vmem_limit_bytes=VMEM_LIMIT),
        name="gram",
    )(dosage, present, components)


def coef_rows(comps):
    return 6 * comps + 2 * SUB


def below(old, first, new):
    return new if first == 0 else jnp.concatenate([old[:first], new], axis=0)


def solve_kernel(comps, markers, *refs):
    out_ref = refs[-1]
    summed = refs[0][...]
    for ref in refs[1:-1]:
        summed = summed + ref[...]
    starts, total = group_starts(comps)
    half = total // 2
    left, right = summed[:, 0:markers], summed[:, markers : 2 * markers]

    def rows_of(start, count):
        if start + count <= half:
            return left[start : start + count]
        if start >= half:
            return right[start - half : start - half + count]
        return jnp.concatenate([left[start:half], right[0 : start + count - half]], axis=0)

    columns = [rows_of(start, comps - first) for start, first in starts]
    firsts = [first for _, first in starts]
    edge = left[half : half + comps]
    count = left[half + comps : half + comps + 1]
    moment = right[half : half + comps]
    moment_one = right[half + comps : half + comps + 1]
    factor, edge_f, moment_f = [], [], []
    for j in range(comps):
        first = firsts[j]
        column = columns[j]
        inv = 1.0 / column[j - first : j - first + 1]
        scaled = column * inv
        edge_j = edge[j : j + 1]
        moment_j = moment[j : j + 1]
        edge_s, moment_s = edge_j * inv, moment_j * inv
        row = lax.broadcasted_iota(jnp.int32, column.shape, 0) + first
        factor.append(jnp.where(row > j, scaled, 0.0))
        edge_f.append(edge_s)
        moment_f.append(moment_s)
        count = count - edge_s * edge_j
        moment_one = moment_one - edge_s * moment_j
        if j + 1 < comps:
            edge = below(edge, first, edge[first:] - column * edge_s)
            moment = below(moment, first, moment[first:] - column * moment_s)
        for k in range(j + 1, comps):
            offset = firsts[k] - first
            columns[k] = columns[k] - scaled[offset:] * column[k - first : k - first + 1]
    last = moment_one / count
    index = lax.broadcasted_iota(jnp.int32, (SUB, markers), 0)
    groups = [jnp.zeros((SUB, markers), F32) for _ in range(comps // SUB)]
    for j in range(comps - 1, -1, -1):
        first = firsts[j]
        value = moment_f[j] - edge_f[j] * last
        total_term = None
        for g in range(first // SUB, comps // SUB):
            term = factor[j][g * SUB - first : (g + 1) * SUB - first] * groups[g]
            total_term = term if total_term is None else total_term + term
        value = value - jnp.sum(total_term, axis=0, keepdims=True)
        g = j // SUB
        groups[g] = jnp.where(index == j - first, value, groups[g])
    coef = jnp.concatenate(groups, axis=0)
    c1, c2, c3 = [part.astype(F32) for part in split3(coef)]
    l1, l2, l3 = [part.astype(F32) for part in split3(last)]
    index = lax.broadcasted_iota(jnp.int32, (2 * SUB, markers), 0)
    ones = jnp.where(index == 0, l1, jnp.where(index == 1, l2, jnp.where(index == 2, l3, 0.0)))
    stacked = jnp.concatenate([c1, c1, c2, c2, c1, c3, ones], axis=0).astype(BF16)
    eye = (
        lax.broadcasted_iota(jnp.int32, (markers, markers), 0)
        == lax.broadcasted_iota(jnp.int32, (markers, markers), 1)
    ).astype(F32).astype(BF16)
    turned = lax.dot_general(eye, stacked, (((1,), (1,)), ((), ())), preferred_element_type=F32)
    out_ref[...] = turned.astype(BF16)


def solve_call(parts, comps, markers):
    return pl.pallas_call(
        functools.partial(solve_kernel, comps, markers),
        out_shape=jax.ShapeDtypeStruct((markers, coef_rows(comps)), BF16),
        compiler_params=pltpu.CompilerParams(vmem_limit_bytes=VMEM_LIMIT),
        name="solve",
    )(*parts)


def design_parts(x):
    d1, d2, d3 = split3(x)
    ones = jnp.ones((2 * SUB, x.shape[1]), BF16)
    return jnp.concatenate([d1, d2, d1, d2, d3, d1, ones], axis=0)


def panel(coef, x, dosage, present):
    fitted = lax.dot_general(
        coef, design_parts(x), (((1,), (0,)), ((), ())), preferred_element_type=F32
    )
    freq = jnp.clip(fitted, 0.01, 0.99)
    observed = present.astype(F32)
    resid = observed * (dosage.astype(F32) - 2.0 * freq)
    sdev = observed * jnp.sqrt(freq * (1.0 - freq))
    return resid.astype(BF16), (2.0 * sdev).astype(BF16)


def columns_kernel(rows, ratio, cols, col_comps_ref, *refs):
    coef_ref, piece_refs = refs[0], refs[1 : 1 + rows]
    coef_out, col_r, col_s, coef, raw_cols, sems = refs[1 + rows :]
    here = coef_ref.shape[1]
    width = col_r.shape[1]
    r = lax.axis_index("rows")
    q = lax.axis_index("cols")
    copies = []
    for d in range(cols):
        place = pl.multiple_of((q ^ d) * here, here)
        copies.append(
            pltpu.make_async_copy(coef_ref.at[d], coef.at[pl.ds(place, here), :], sems.at[len(copies)])
        )
    height = piece_refs[0].shape[1]
    for d in range(rows):
        begin = (r ^ d) * height
        k, part, inside = begin // (2 * here), lax.rem(begin // here, 2), lax.rem(begin, here)
        for e in range(rows):
            owner = ((q // ratio) ^ e) * ratio + lax.rem(q + ratio - k, ratio)
            place = pl.multiple_of(owner * here + inside, height)
            copies.append(
                pltpu.make_async_copy(
                    piece_refs[d].at[e], raw_cols.at[part, pl.ds(place, height), :], sems.at[len(copies)]
                )
            )
    for copy in copies:
        copy.start()
    for copy in copies:
        copy.wait()
    coef_out[...] = coef[...]
    step = 256 if width % 256 == 0 else width
    for at in range(0, width, step):
        span = slice(at, at + step)
        resid, sdev = panel(
            coef[...], col_comps_ref[:, span], raw_cols[0, :, span], raw_cols[1, :, span]
        )
        col_r[:, span] = resid
        col_s[:, span] = sdev


def columns_call(rows, ratio, cols, col_comps, coefs, pieces):
    comps, width = col_comps.shape
    markers = coefs.shape[1] * cols
    anywhere = pl.BlockSpec(memory_space=pl.ANY)
    return pl.pallas_call(
        functools.partial(columns_kernel, rows, ratio, cols),
        in_specs=[pl.BlockSpec(memory_space=pltpu.VMEM)] + [anywhere] * (1 + len(pieces)),
        out_shape=(
            jax.ShapeDtypeStruct((markers, coef_rows(comps)), BF16),
            jax.ShapeDtypeStruct((markers, width), BF16),
            jax.ShapeDtypeStruct((markers, width), BF16),
        ),
        scratch_shapes=[
            pltpu.VMEM((markers, coef_rows(comps)), BF16),
            pltpu.VMEM((2, markers, width), BF16),
            pltpu.SemaphoreType.DMA((cols + rows * rows,)),
        ],
        compiler_params=pltpu.CompilerParams(vmem_limit_bytes=VMEM_LIMIT),
        name="columns",
    )(col_comps, coefs, *pieces)


def kin_kernel(raw_ref, comps_ref, coef_ref, col_r, col_s, *refs):
    out_ref, row_r, row_s = refs[-3:]
    width = out_ref.shape[1]
    resid, sdev = panel(coef_ref[...], comps_ref[...], raw_ref[0], raw_ref[1])
    resid, sdev = resid.T, sdev.T
    step = 512 if width % 512 == 0 else width
    for at in range(0, width, step):
        span = slice(at, at + step)
        numer = jnp.dot(row_r[...], col_r[:, span], preferred_element_type=F32)
        denom = jnp.dot(row_s[...], col_s[:, span], preferred_element_type=F32)
        out_ref[:, span] = numer / denom
    row_r[...] = resid
    row_s[...] = sdev


def kin_call(start, raw, components, coef, col_r, col_s, before):
    _, markers, count = raw.shape
    comps, people = components.shape
    width = col_r.shape[1]
    tile = 256 if count % 256 == 0 else count
    first = start // tile
    last = count // tile - 1
    whole = lambda i: (0, 0)
    in_specs = [
        pl.BlockSpec((2, markers, tile), lambda i: (0, 0, jnp.minimum(i, last))),
        pl.BlockSpec((comps, tile), lambda i: (0, jnp.minimum(i, last) + first)),
        pl.BlockSpec(coef.shape, whole),
        pl.BlockSpec((markers, width), whole),
        pl.BlockSpec((markers, width), whole),
    ]
    operands = [raw, components, coef, col_r, col_s]
    aliases = {}
    if before is not None:
        in_specs.append(pl.BlockSpec(memory_space=pl.ANY))
        aliases = {len(operands): 0}
        operands.append(before)
    return pl.pallas_call(
        kin_kernel,
        grid=(count // tile + 1,),
        in_specs=in_specs,
        out_specs=pl.BlockSpec((tile, width), lambda i: (jnp.maximum(i - 1, 0) + first, 0)),
        out_shape=jax.ShapeDtypeStruct((people, width), F32),
        scratch_shapes=[pltpu.VMEM((tile, markers), BF16), pltpu.VMEM((tile, markers), BF16)],
        input_output_aliases=aliases,
        compiler_params=pltpu.CompilerParams(vmem_limit_bytes=VMEM_LIMIT),
        name="kinship",
    )(*operands)


def per_device(dosage, present, components):
    rows, cols = lax.axis_size("rows"), lax.axis_size("cols")
    ratio = cols // rows
    markers, people = dosage.shape
    comps = components.shape[0]
    width = people // ratio
    col = lax.axis_index("cols")
    raw = jnp.stack([dosage.astype(BF16), present.astype(BF16)])

    def across(x, axis, size):
        return [x] + [lax.ppermute(x, axis, [(i, i ^ d) for i in range(size)]) for d in range(1, size)]

    starts = [people * i // CHUNKS for i in range(CHUNKS + 1)]
    raw_rows = [
        lax.all_gather(raw[:, :, a:b], "cols", axis=1, tiled=True) for a, b in zip(starts, starts[1:])
    ]

    row = lax.axis_index("rows")
    core, plane = col % ratio, col // ratio
    halves = []
    for k in range(ratio):
        part = (core + k) % ratio
        mine = lax.dynamic_slice_in_dim(raw, part * width, width, 2).reshape(2 * markers, width)
        swaps = [(z * ratio + c, z * ratio + (c + k) % ratio) for z in range(rows) for c in range(ratio)]
        halves.append(lax.ppermute(mine, "cols", swaps) if k else mine)
    gram = gram_call(dosage, present, components)
    held, gram = lax.optimization_barrier((jnp.concatenate(halves, axis=0), gram))
    grams = across(gram, "rows", rows)
    height = held.shape[0] // rows
    quarters = []
    for d in range(rows):
        mine = lax.dynamic_slice_in_dim(held, (row ^ d) * height, height, 0)
        quarters.append(lax.ppermute(mine, "rows", [(i, i ^ d) for i in range(rows)]) if d else mine)
    quarters, *grams = lax.optimization_barrier((jnp.stack(quarters), *grams))
    coef = solve_call(grams, comps, markers)
    moved = []
    for e in range(rows):
        mine = lax.dynamic_index_in_dim(quarters, row ^ plane ^ e, 0, keepdims=False)
        hops = [(z * ratio + c, (z ^ e) * ratio + c) for z in range(rows) for c in range(ratio)]
        moved.append(lax.ppermute(mine, "cols", hops) if e else mine)
    moved, coef = lax.optimization_barrier((jnp.stack(moved), coef))
    pieces = across(moved, "rows", rows)
    coefs = coef[None]
    hop = 1
    while hop < cols:
        other = lax.ppermute(coefs, "cols", [(i, i ^ hop) for i in range(cols)])
        coefs = jnp.concatenate([coefs, other], axis=0)
        hop *= 2

    mine = lax.dynamic_slice_in_dim(components, core * width, width, 1)
    moves = [
        (r * cols + z * ratio + c, z * cols + r * ratio + c)
        for r in range(rows)
        for z in range(rows)
        for c in range(ratio)
    ]
    col_comps = lax.ppermute(mine, ("rows", "cols"), moves)

    coef, col_r, col_s = columns_call(rows, ratio, cols, col_comps, coefs, pieces)
    out = None
    for start, part in zip(starts, raw_rows):
        out = kin_call(start, part, components, coef, col_r, col_s, out)
    return out


def solution(mesh):
    placed = (P("cols", "rows"), P("cols", "rows"), P(None, "rows"))
    return jax.shard_map(
        per_device, mesh=mesh, in_specs=placed, out_specs=P("rows", "cols"), check_vma=False
    )
```

```python
import functools

import jax
import jax.numpy as jnp
from jax import lax
from jax.experimental import pallas as pl
from jax.experimental.pallas import tpu as pltpu
from jax.sharding import PartitionSpec as P

F32, BF16 = jnp.float32, jnp.bfloat16
VMEM_LIMIT = 56 * 1024 * 1024
SUB = 8


def split3(x):
    high = x.astype(BF16)
    rest = x - high.astype(F32)
    mid = rest.astype(BF16)
    low = (rest - mid.astype(F32)).astype(BF16)
    return high, mid, low


def group_starts(comps):
    starts, at = [], 0
    for j in range(comps):
        first = j // SUB * SUB
        starts.append((at, first))
        at += comps - first
    return starts, at


def gram_kernel(dosage_ref, present_ref, comps_ref, out_ref, lhs_ref):
    comps, people = comps_ref.shape
    markers = dosage_ref.shape[0]
    starts, total = group_starts(comps)
    chunk = 512 if people % 512 == 0 else people
    acc = None
    for at in range(0, people, chunk):
        span = slice(at, at + chunk)
        obs = present_ref[:, span].astype(F32)
        tgt = 0.5 * dosage_ref[:, span].astype(F32) * obs
        rhs = jnp.concatenate([obs, tgt], axis=0).astype(BF16)
        x = comps_ref[:, span]
        for j, (start, first) in enumerate(starts):
            lhs_ref[start : start + comps - first, :] = x[first:, :] * x[j : j + 1, :]
        lhs_ref[total : total + comps, :] = x
        tail = lhs_ref.shape[0] - total - comps
        lhs_ref[total + comps :, :] = jnp.ones((tail, chunk), F32)
        for part in split3(lhs_ref[...]):
            term = lax.dot_general(part, rhs, (((1,), (1,)), ((), ())), preferred_element_type=F32)
            acc = term if acc is None else acc + term
    half = total // 2
    out_ref[0:half, :] = jnp.concatenate([acc[0:half, 0:markers], acc[half:total, 0:markers]], axis=1)
    out_ref[half:, :] = acc[total : total + comps + SUB, :]


def gram_call(dosage, present, components):
    markers, people = dosage.shape
    comps = components.shape[0]
    total = group_starts(comps)[1]
    chunk = 512 if people % 512 == 0 else people
    return pl.pallas_call(
        gram_kernel,
        out_shape=jax.ShapeDtypeStruct((total // 2 + comps + SUB, 2 * markers), F32),
        scratch_shapes=[pltpu.VMEM((total + comps + 2 * SUB, chunk), F32)],
        compiler_params=pltpu.CompilerParams(vmem_limit_bytes=VMEM_LIMIT),
        name="gram",
    )(dosage, present, components)


def coef_rows(comps):
    return 6 * comps + 2 * SUB


def below(old, first, new):
    return new if first == 0 else jnp.concatenate([old[:first], new], axis=0)


def solve_kernel(comps, markers, *refs):
    out_ref = refs[-1]
    summed = refs[0][...]
    for ref in refs[1:-1]:
        summed = summed + ref[...]
    starts, total = group_starts(comps)
    half = total // 2
    left, right = summed[:, 0:markers], summed[:, markers : 2 * markers]

    def rows_of(start, count):
        if start + count <= half:
            return left[start : start + count]
        if start >= half:
            return right[start - half : start - half + count]
        return jnp.concatenate([left[start:half], right[0 : start + count - half]], axis=0)

    columns = [rows_of(start, comps - first) for start, first in starts]
    firsts = [first for _, first in starts]
    edge = left[half : half + comps]
    count = left[half + comps : half + comps + 1]
    moment = right[half : half + comps]
    moment_one = right[half + comps : half + comps + 1]
    factor, edge_f, moment_f = [], [], []
    for j in range(comps):
        first = firsts[j]
        column = columns[j]
        inv = 1.0 / column[j - first : j - first + 1]
        scaled = column * inv
        edge_j = edge[j : j + 1]
        moment_j = moment[j : j + 1]
        edge_s, moment_s = edge_j * inv, moment_j * inv
        row = lax.broadcasted_iota(jnp.int32, column.shape, 0) + first
        factor.append(jnp.where(row > j, scaled, 0.0))
        edge_f.append(edge_s)
        moment_f.append(moment_s)
        count = count - edge_s * edge_j
        moment_one = moment_one - edge_s * moment_j
        if j + 1 < comps:
            edge = below(edge, first, edge[first:] - column * edge_s)
            moment = below(moment, first, moment[first:] - column * moment_s)
        for k in range(j + 1, comps):
            offset = firsts[k] - first
            columns[k] = columns[k] - scaled[offset:] * column[k - first : k - first + 1]
    last = moment_one / count
    index = lax.broadcasted_iota(jnp.int32, (SUB, markers), 0)
    groups = [jnp.zeros((SUB, markers), F32) for _ in range(comps // SUB)]
    for j in range(comps - 1, -1, -1):
        first = firsts[j]
        value = moment_f[j] - edge_f[j] * last
        total_term = None
        for g in range(first // SUB, comps // SUB):
            term = factor[j][g * SUB - first : (g + 1) * SUB - first] * groups[g]
            total_term = term if total_term is None else total_term + term
        value = value - jnp.sum(total_term, axis=0, keepdims=True)
        g = j // SUB
        groups[g] = jnp.where(index == j - first, value, groups[g])
    coef = 2.0 * jnp.concatenate(groups, axis=0)
    last = 2.0 * last
    c1, c2, c3 = [part.astype(F32) for part in split3(coef)]
    l1, l2, l3 = [part.astype(F32) for part in split3(last)]
    index = lax.broadcasted_iota(jnp.int32, (2 * SUB, markers), 0)
    ones = jnp.where(index == 0, l1, jnp.where(index == 1, l2, jnp.where(index == 2, l3, 0.0)))
    stacked = jnp.concatenate([c1, c1, c2, c2, c1, c3, ones], axis=0).astype(BF16)
    eye = (
        lax.broadcasted_iota(jnp.int32, (markers, markers), 0)
        == lax.broadcasted_iota(jnp.int32, (markers, markers), 1)
    ).astype(F32).astype(BF16)
    turned = lax.dot_general(eye, stacked, (((1,), (1,)), ((), ())), preferred_element_type=F32)
    out_ref[...] = turned.astype(BF16)


def solve_call(parts, comps, markers):
    return pl.pallas_call(
        functools.partial(solve_kernel, comps, markers),
        out_shape=jax.ShapeDtypeStruct((markers, coef_rows(comps)), BF16),
        compiler_params=pltpu.CompilerParams(vmem_limit_bytes=VMEM_LIMIT),
        name="solve",
    )(*parts)


def design_parts(x):
    d1, d2, d3 = split3(x)
    ones = jnp.ones((2 * SUB, x.shape[1]), BF16)
    return jnp.concatenate([d1, d2, d1, d2, d3, d1, ones], axis=0)


def panel(coef, x, dosage, present):
    fitted = lax.dot_general(
        coef, design_parts(x), (((1,), (0,)), ((), ())), preferred_element_type=F32
    )
    twice = jnp.clip(fitted, 0.02, 1.98)
    observed = present.astype(F32)
    spread = twice * (2.0 - twice)
    resid = observed * (dosage.astype(F32) - twice)
    sdev = observed * (spread * lax.rsqrt(spread))
    return resid.astype(BF16), sdev.astype(BF16)


def columns_kernel(rows, ratio, cols, groups, col_comps_ref, *refs):
    coef_ref, piece_refs = refs[0], refs[1 : 1 + groups * rows]
    coef_out, col_r, col_s, coef, raw_cols, sems = refs[1 + groups * rows :]
    here = coef_ref.shape[1]
    width = col_r.shape[1]
    r = lax.axis_index("rows")
    q = lax.axis_index("cols")
    copies = []
    for d in range(cols):
        place = pl.multiple_of((q ^ d) * here, here)
        copies.append(
            pltpu.make_async_copy(coef_ref.at[d], coef.at[pl.ds(place, here), :], sems.at[len(copies)])
        )
    height = piece_refs[0].shape[1]
    for d in range(rows):
        begin = (r ^ d) * height
        k, part, inside = begin // (2 * here), lax.rem(begin // here, 2), lax.rem(begin, here)
        found = [ref.at[i] for ref in piece_refs[d::rows] for i in range(ref.shape[0])]
        for e, piece in enumerate(found):
            owner = ((q // ratio) ^ e) * ratio + lax.rem(q + ratio - k, ratio)
            place = pl.multiple_of(owner * here + inside, height)
            copies.append(
                pltpu.make_async_copy(
                    piece, raw_cols.at[part, pl.ds(place, height), :], sems.at[len(copies)]
                )
            )
    for copy in copies:
        copy.start()
    for copy in copies:
        copy.wait()
    coef_out[...] = coef[...]
    step = 256 if width % 256 == 0 else width
    for at in range(0, width, step):
        span = slice(at, at + step)
        resid, sdev = panel(
            coef[...], col_comps_ref[:, span], raw_cols[0, :, span], raw_cols[1, :, span]
        )
        col_r[:, span] = resid
        col_s[:, span] = sdev


def columns_call(rows, ratio, cols, col_comps, coefs, pieces):
    comps, width = col_comps.shape
    markers = coefs.shape[1] * cols
    anywhere = pl.BlockSpec(memory_space=pl.ANY)
    return pl.pallas_call(
        functools.partial(columns_kernel, rows, ratio, cols, len(pieces) // rows),
        in_specs=[pl.BlockSpec(memory_space=pltpu.VMEM)] + [anywhere] * (1 + len(pieces)),
        out_shape=(
            jax.ShapeDtypeStruct((markers, coef_rows(comps)), BF16),
            jax.ShapeDtypeStruct((markers, width), BF16),
            jax.ShapeDtypeStruct((markers, width), BF16),
        ),
        scratch_shapes=[
            pltpu.VMEM((markers, coef_rows(comps)), BF16),
            pltpu.VMEM((2, markers, width), BF16),
            pltpu.SemaphoreType.DMA((cols + rows * rows,)),
        ],
        compiler_params=pltpu.CompilerParams(vmem_limit_bytes=VMEM_LIMIT),
        name="columns",
    )(col_comps, coefs, *pieces)


def quotient(numer, denom):
    inverse = pl.reciprocal(denom, approx=True)
    return numer * (inverse * (2.0 - denom * inverse))


def kin_kernel(rows, ratio, turn, start_ref, comps_ref, coef_ref, col_r, col_s, *refs):
    own_ref = refs[0]
    from_left, from_right = refs[1:rows], refs[rows : 2 * rows - 1]
    out_ref, raw, sems = refs[-3:]
    tile, width = out_ref.shape
    here = own_ref.shape[0] // (2 * ratio)
    plane = lax.axis_index("cols") // ratio
    core = lax.rem(lax.axis_index("cols"), ratio)
    step = pl.program_id(0)

    def copies(block_ref, slot):
        source = lax.rem(plane - slot + rows, rows)
        for k in range(ratio):
            owner = source * ratio + lax.rem(core + 2 * ratio - turn - k, ratio)
            place = pl.multiple_of(owner * here, here)
            for part in range(2):
                begin = (2 * k + part) * here
                yield pltpu.make_async_copy(
                    block_ref.at[begin : begin + here, :],
                    raw.at[part, pl.ds(place, here), :],
                    sems.at[(slot * ratio + k) * 2 + part],
                )

    @pl.when(step == 0)
    def _():
        for copy in copies(own_ref, 0):
            copy.start()
        for slot in range(1, rows):

            @pl.when(plane >= slot)
            def _():
                for copy in copies(from_left[slot - 1], slot):
                    copy.start()

            @pl.when(plane < slot)
            def _():
                for copy in copies(from_right[rows - slot - 1], slot):
                    copy.start()

        for slot in range(rows):
            for copy in copies(own_ref, slot):
                copy.wait()

    here_span = pl.ds(pl.multiple_of(step * tile, tile), tile)
    resid, sdev = panel(coef_ref[...], comps_ref[...], raw[0, :, here_span], raw[1, :, here_span])
    contract = (((0,), (0,)), ((), ()))
    wide = 512 if width % 512 == 0 else width
    for at in range(0, width, wide):
        span = slice(at, at + wide)
        numer = lax.dot_general(resid, col_r[:, span], contract, preferred_element_type=F32)
        denom = lax.dot_general(sdev, col_s[:, span], contract, preferred_element_type=F32)
        out_ref[:, span] = quotient(numer, denom)


def kin_call(rows, ratio, turn, start, components, coef, col_r, col_s, blocks, before):
    height, count = blocks[0].shape
    comps, people = components.shape
    markers, width = col_r.shape
    tile = 256 if count % 256 == 0 else count
    whole = lambda i, at: (0, 0)
    in_specs = [
        pl.BlockSpec((comps, tile), lambda i, at: (0, i + at[0])),
        pl.BlockSpec(coef.shape, whole),
        pl.BlockSpec((markers, width), whole),
        pl.BlockSpec((markers, width), whole),
    ] + [pl.BlockSpec(memory_space=pl.ANY)] * len(blocks)
    operands = [components, coef, col_r, col_s, *blocks]
    aliases = {}
    if before is not None:
        in_specs.append(pl.BlockSpec(memory_space=pl.ANY))
        operands.append(before)
        aliases = {len(operands): 0}
    return pl.pallas_call(
        functools.partial(kin_kernel, rows, ratio, turn),
        grid_spec=pltpu.PrefetchScalarGridSpec(
            num_scalar_prefetch=1,
            grid=(count // tile,),
            in_specs=in_specs,
            out_specs=pl.BlockSpec((tile, width), lambda i, at: (i + at[0], 0)),
            scratch_shapes=[
                pltpu.VMEM((2, markers, count), BF16),
                pltpu.SemaphoreType.DMA((rows * ratio * 2,)),
            ],
        ),
        out_shape=jax.ShapeDtypeStruct((people, width), F32),
        input_output_aliases=aliases,
        compiler_params=pltpu.CompilerParams(vmem_limit_bytes=VMEM_LIMIT),
        name="kinship",
    )((start // tile)[None].astype(jnp.int32), *operands)


def per_device(dosage, present, components):
    rows, cols = lax.axis_size("rows"), lax.axis_size("cols")
    ratio = cols // rows
    markers, people = dosage.shape
    comps = components.shape[0]
    width = people // ratio
    row = lax.axis_index("rows")
    col = lax.axis_index("cols")
    core, plane = col % ratio, col // ratio

    def pairs(hop):
        moves = [(z, c, *hop(z, c)) for z in range(rows) for c in range(ratio)]
        return [(z * ratio + c, y * ratio + b) for z, c, y, b in moves if 0 <= y < rows]

    def across(x, axis, size):
        return [x] + [lax.ppermute(x, axis, [(i, i ^ d) for i in range(size)]) for d in range(1, size)]

    def swap(x, k):
        return lax.ppermute(x, "cols", pairs(lambda z, c: (z, (c + k) % ratio))) if k else x

    def along(x, way):
        return lax.ppermute(x, "cols", pairs(lambda z, c: (z + way, c)))

    halves = []
    for k in range(ratio):
        begin = (core + k) % ratio * width
        both = [lax.dynamic_slice_in_dim(x, begin, width, 1).astype(BF16) for x in (dosage, present)]
        halves.append(swap(jnp.concatenate(both, axis=0), k))
    held = jnp.concatenate(halves, axis=0)
    held, dosage, present = lax.optimization_barrier((held, dosage, present))
    from_left, from_right = [along(held, 1)], [along(held, -1)]

    height = held.shape[0] // rows
    quarters = []
    for d in range(rows):
        mine = lax.dynamic_slice_in_dim(held, (row ^ d) * height, height, 0)
        quarters.append(lax.ppermute(mine, "rows", [(i, i ^ d) for i in range(rows)]) if d else mine)
    gram = gram_call(dosage, present, components)
    col_comps = lax.dynamic_slice_in_dim(components, core * width, width, 1)
    grams = across(gram, "rows", rows)
    quarters, grams, col_comps, from_left[0], from_right[0] = lax.optimization_barrier(
        (jnp.stack(quarters), grams, col_comps, from_left[0], from_right[0])
    )
    moved = []
    for e in range(rows):
        mine = lax.dynamic_index_in_dim(quarters, row ^ plane ^ e, 0, keepdims=False)
        moved.append(lax.ppermute(mine, "cols", pairs(lambda z, c: (z ^ e, c))) if e else mine)
    coefs = solve_call(grams, comps, markers)[None]
    sent = [
        lax.ppermute(
            col_comps,
            ("rows", "cols"),
            [(z * cols + z * ratio + c, (z ^ d) * cols + z * ratio + c) for z in range(rows) for c in range(ratio)],
        )
        for d in range(1, rows)
    ]
    moved, coefs, sent, held, from_left, from_right = lax.optimization_barrier(
        (moved, coefs, sent, held, from_left, from_right)
    )
    pieces = []
    for step in range(rows - 2):
        begin, end = rows * step // (rows - 2), rows * (step + 1) // (rows - 2)
        pieces.append(across(jnp.stack(moved[begin:end]), "rows", rows))
        from_left.append(along(from_left[-1], 1))
        from_right.append(along(from_right[-1], -1))
        hop = 1
        while step == 0 and hop < cols:
            other = lax.ppermute(coefs, "cols", [(i, i ^ hop) for i in range(cols)])
            coefs = jnp.concatenate([coefs, other], axis=0)
            hop *= 2
        if step < rows - 3:
            pieces, coefs, held, from_left, from_right = lax.optimization_barrier(
                (pieces, coefs, held, from_left, from_right)
            )
    col_comps = sum(sent, jnp.where(row == plane, col_comps, 0.0))
    coef, col_r, col_s = columns_call(rows, ratio, cols, col_comps, coefs, sum(pieces, []))
    out = None
    for turn in range(ratio):
        start = (core + ratio - turn) % ratio * width
        came = [swap(block, turn) for block in [held, *from_left, *from_right]]
        out = kin_call(rows, ratio, turn, start, components, coef, col_r, col_s, came, out)
    return out


def solution(mesh):
    placed = (P("cols", "rows"), P("cols", "rows"), P(None, "rows"))
    return jax.shard_map(
        per_device, mesh=mesh, in_specs=placed, out_specs=P("rows", "cols"), check_vma=False
    )
```

```python
import functools

import jax
import jax.numpy as jnp
from jax import lax
from jax.experimental import pallas as pl
from jax.experimental.pallas import tpu as pltpu
from jax.sharding import PartitionSpec as P

F32, BF16 = jnp.float32, jnp.bfloat16
VMEM_LIMIT = 56 * 1024 * 1024
SUB = 8


def split3(x):
    high = x.astype(BF16)
    rest = x - high.astype(F32)
    mid = rest.astype(BF16)
    low = (rest - mid.astype(F32)).astype(BF16)
    return high, mid, low


def group_starts(comps):
    starts, at = [], 0
    for j in range(comps):
        first = j // SUB * SUB
        starts.append((at, first))
        at += comps - first
    return starts, at


def gram_kernel(dosage_ref, present_ref, comps_ref, out_ref, lhs_ref):
    comps, people = comps_ref.shape
    markers = dosage_ref.shape[0]
    starts, total = group_starts(comps)
    chunk = 512 if people % 512 == 0 else people
    acc = None
    for at in range(0, people, chunk):
        span = slice(at, at + chunk)
        obs = present_ref[:, span].astype(F32)
        tgt = 0.5 * dosage_ref[:, span].astype(F32) * obs
        rhs = jnp.concatenate([obs, tgt], axis=0).astype(BF16)
        x = comps_ref[:, span]
        for j, (start, first) in enumerate(starts):
            lhs_ref[start : start + comps - first, :] = x[first:, :] * x[j : j + 1, :]
        lhs_ref[total : total + comps, :] = x
        tail = lhs_ref.shape[0] - total - comps
        lhs_ref[total + comps :, :] = jnp.ones((tail, chunk), F32)
        for part in split3(lhs_ref[...]):
            term = lax.dot_general(part, rhs, (((1,), (1,)), ((), ())), preferred_element_type=F32)
            acc = term if acc is None else acc + term
    half = total // 2
    out_ref[0:half, :] = jnp.concatenate([acc[0:half, 0:markers], acc[half:total, 0:markers]], axis=1)
    out_ref[half:, :] = acc[total : total + comps + SUB, :]


def gram_call(dosage, present, components):
    markers, people = dosage.shape
    comps = components.shape[0]
    total = group_starts(comps)[1]
    chunk = 512 if people % 512 == 0 else people
    return pl.pallas_call(
        gram_kernel,
        out_shape=jax.ShapeDtypeStruct((total // 2 + comps + SUB, 2 * markers), F32),
        scratch_shapes=[pltpu.VMEM((total + comps + 2 * SUB, chunk), F32)],
        compiler_params=pltpu.CompilerParams(vmem_limit_bytes=VMEM_LIMIT),
        name="gram",
    )(dosage, present, components)


def coef_rows(comps):
    return 6 * comps + 2 * SUB


def below(old, first, new):
    return new if first == 0 else jnp.concatenate([old[:first], new], axis=0)


def solve_kernel(comps, markers, *refs):
    out_ref = refs[-1]
    summed = refs[0][...]
    for ref in refs[1:-1]:
        summed = summed + ref[...]
    starts, total = group_starts(comps)
    half = total // 2
    left, right = summed[:, 0:markers], summed[:, markers : 2 * markers]

    def rows_of(start, count):
        if start + count <= half:
            return left[start : start + count]
        if start >= half:
            return right[start - half : start - half + count]
        return jnp.concatenate([left[start:half], right[0 : start + count - half]], axis=0)

    columns = [rows_of(start, comps - first) for start, first in starts]
    firsts = [first for _, first in starts]
    edge = left[half : half + comps]
    count = left[half + comps : half + comps + 1]
    moment = right[half : half + comps]
    moment_one = right[half + comps : half + comps + 1]
    factor, edge_f, moment_f = [], [], []
    for j in range(comps):
        first = firsts[j]
        column = columns[j]
        inv = 1.0 / column[j - first : j - first + 1]
        scaled = column * inv
        edge_j = edge[j : j + 1]
        moment_j = moment[j : j + 1]
        edge_s, moment_s = edge_j * inv, moment_j * inv
        row = lax.broadcasted_iota(jnp.int32, column.shape, 0) + first
        factor.append(jnp.where(row > j, scaled, 0.0))
        edge_f.append(edge_s)
        moment_f.append(moment_s)
        count = count - edge_s * edge_j
        moment_one = moment_one - edge_s * moment_j
        if j + 1 < comps:
            edge = below(edge, first, edge[first:] - column * edge_s)
            moment = below(moment, first, moment[first:] - column * moment_s)
        for k in range(j + 1, comps):
            offset = firsts[k] - first
            columns[k] = columns[k] - scaled[offset:] * column[k - first : k - first + 1]
    last = moment_one / count
    index = lax.broadcasted_iota(jnp.int32, (SUB, markers), 0)
    groups = [jnp.zeros((SUB, markers), F32) for _ in range(comps // SUB)]
    for j in range(comps - 1, -1, -1):
        first = firsts[j]
        value = moment_f[j] - edge_f[j] * last
        total_term = None
        for g in range(first // SUB, comps // SUB):
            term = factor[j][g * SUB - first : (g + 1) * SUB - first] * groups[g]
            total_term = term if total_term is None else total_term + term
        value = value - jnp.sum(total_term, axis=0, keepdims=True)
        g = j // SUB
        groups[g] = jnp.where(index == j - first, value, groups[g])
    coef = 2.0 * jnp.concatenate(groups, axis=0)
    last = 2.0 * last
    c1, c2, c3 = [part.astype(F32) for part in split3(coef)]
    l1, l2, l3 = [part.astype(F32) for part in split3(last)]
    index = lax.broadcasted_iota(jnp.int32, (2 * SUB, markers), 0)
    ones = jnp.where(index == 0, l1, jnp.where(index == 1, l2, jnp.where(index == 2, l3, 0.0)))
    stacked = jnp.concatenate([c1, c1, c2, c2, c1, c3, ones], axis=0).astype(BF16)
    eye = (
        lax.broadcasted_iota(jnp.int32, (markers, markers), 0)
        == lax.broadcasted_iota(jnp.int32, (markers, markers), 1)
    ).astype(F32).astype(BF16)
    turned = lax.dot_general(eye, stacked, (((1,), (1,)), ((), ())), preferred_element_type=F32)
    out_ref[...] = turned.astype(BF16)


def solve_call(parts, comps, markers):
    return pl.pallas_call(
        functools.partial(solve_kernel, comps, markers),
        out_shape=jax.ShapeDtypeStruct((markers, coef_rows(comps)), BF16),
        compiler_params=pltpu.CompilerParams(vmem_limit_bytes=VMEM_LIMIT),
        name="solve",
    )(*parts)


def design_parts(x):
    d1, d2, d3 = split3(x)
    ones = jnp.ones((2 * SUB, x.shape[1]), BF16)
    return jnp.concatenate([d1, d2, d1, d2, d3, d1, ones], axis=0)


def panel(coef, x, dosage, present):
    fitted = lax.dot_general(
        coef, design_parts(x), (((1,), (0,)), ((), ())), preferred_element_type=F32
    )
    twice = jnp.clip(fitted, 0.02, 1.98)
    observed = present.astype(F32)
    spread = twice * (2.0 - twice)
    resid = observed * (dosage.astype(F32) - twice)
    sdev = observed * (spread * lax.rsqrt(spread))
    return resid.astype(BF16), sdev.astype(BF16)


def columns_kernel(rows, ratio, cols, col_comps_ref, *refs):
    coef_refs, piece_refs = refs[:rows], refs[rows : 2 * rows]
    coef_out, col_r, col_s, coef, raw_cols, sems = refs[2 * rows :]
    here = coef_refs[0].shape[0] // ratio
    width = col_r.shape[1]
    r = lax.axis_index("rows")
    q = lax.axis_index("cols")
    copies = []
    for e in range(rows):
        for k in range(ratio):
            owner = ((q // ratio) ^ e) * ratio + lax.rem(q + ratio - k, ratio)
            place = pl.multiple_of(owner * here, here)
            copies.append(
                pltpu.make_async_copy(
                    coef_refs[e].at[k * here : (k + 1) * here, :],
                    coef.at[pl.ds(place, here), :],
                    sems.at[len(copies)],
                )
            )
    height = piece_refs[0].shape[1]
    for d in range(rows):
        begin = (r ^ d) * height
        k, part, inside = begin // (2 * here), lax.rem(begin // here, 2), lax.rem(begin, here)
        for e in range(rows):
            owner = ((q // ratio) ^ e) * ratio + lax.rem(q + ratio - k, ratio)
            place = pl.multiple_of(owner * here + inside, height)
            copies.append(
                pltpu.make_async_copy(
                    piece_refs[d].at[e], raw_cols.at[part, pl.ds(place, height), :], sems.at[len(copies)]
                )
            )
    for copy in copies:
        copy.start()
    for copy in copies:
        copy.wait()
    coef_out[...] = coef[...]
    step = 256 if width % 256 == 0 else width
    for at in range(0, width, step):
        span = slice(at, at + step)
        resid, sdev = panel(
            coef[...], col_comps_ref[:, span], raw_cols[0, :, span], raw_cols[1, :, span]
        )
        col_r[:, span] = resid
        col_s[:, span] = sdev


def columns_call(rows, ratio, cols, col_comps, coefs, pieces):
    comps, width = col_comps.shape
    markers = coefs[0].shape[0] * rows
    anywhere = pl.BlockSpec(memory_space=pl.ANY)
    return pl.pallas_call(
        functools.partial(columns_kernel, rows, ratio, cols),
        in_specs=[pl.BlockSpec(memory_space=pltpu.VMEM)] + [anywhere] * (len(coefs) + len(pieces)),
        out_shape=(
            jax.ShapeDtypeStruct((markers, coef_rows(comps)), BF16),
            jax.ShapeDtypeStruct((markers, width), BF16),
            jax.ShapeDtypeStruct((markers, width), BF16),
        ),
        scratch_shapes=[
            pltpu.VMEM((markers, coef_rows(comps)), BF16),
            pltpu.VMEM((2, markers, width), BF16),
            pltpu.SemaphoreType.DMA((cols + rows * rows,)),
        ],
        compiler_params=pltpu.CompilerParams(vmem_limit_bytes=VMEM_LIMIT),
        name="columns",
    )(col_comps, *coefs, *pieces)


def quotient(numer, denom):
    inverse = pl.reciprocal(denom, approx=True)
    return numer * (inverse * (2.0 - denom * inverse))


def kin_kernel(rows, ratio, turn, start_ref, comps_ref, coef_ref, col_r, col_s, *refs):
    block_refs = refs[:rows]
    out_ref, raw, row_r, row_s, sems = refs[-5:]
    count = out_ref.shape[0]
    here = block_refs[0].shape[0] // (2 * ratio)

    @pl.when(pl.program_id(0) == 0)
    def _():
        plane = lax.axis_index("cols") // ratio
        core = lax.rem(lax.axis_index("cols"), ratio)
        copies = []
        for slot in range(rows):
            source = lax.rem(plane - slot + rows, rows)
            for k in range(ratio):
                owner = source * ratio + lax.rem(core + 2 * ratio - turn - k, ratio)
                place = pl.multiple_of(owner * here, here)
                for part in range(2):
                    begin = (2 * k + part) * here
                    copies.append(
                        pltpu.make_async_copy(
                            block_refs[slot].at[begin : begin + here, :],
                            raw.at[part, pl.ds(place, here), :],
                            sems.at[len(copies)],
                        )
                    )
        for copy in copies:
            copy.start()
        for copy in copies:
            copy.wait()
        step = 256 if count % 256 == 0 else count
        for at in range(0, count, step):
            span = slice(at, at + step)
            resid, sdev = panel(coef_ref[...], comps_ref[:, span], raw[0, :, span], raw[1, :, span])
            row_r[span, :] = resid.T
            row_s[span, :] = sdev.T

    numer = jnp.dot(row_r[...], col_r[...], preferred_element_type=F32)
    denom = jnp.dot(row_s[...], col_s[...], preferred_element_type=F32)
    out_ref[...] = quotient(numer, denom)


def kin_call(rows, ratio, turn, part, components, coef, col_r, col_s, blocks, before):
    count = blocks[0].shape[1]
    comps, people = components.shape
    markers, width = col_r.shape
    wide = 256 if width % 256 == 0 else width
    in_specs = [
        pl.BlockSpec((comps, count), lambda i, at: (0, at[0])),
        pl.BlockSpec(coef.shape, lambda i, at: (0, 0)),
        pl.BlockSpec((markers, wide), lambda i, at: (0, i)),
        pl.BlockSpec((markers, wide), lambda i, at: (0, i)),
    ] + [pl.BlockSpec(memory_space=pl.ANY)] * len(blocks)
    operands = [components, coef, col_r, col_s, *blocks]
    aliases = {}
    if before is not None:
        in_specs.append(pl.BlockSpec(memory_space=pl.ANY))
        operands.append(before)
        aliases = {len(operands): 0}
    return pl.pallas_call(
        functools.partial(kin_kernel, rows, ratio, turn),
        grid_spec=pltpu.PrefetchScalarGridSpec(
            num_scalar_prefetch=1,
            grid=(width // wide,),
            in_specs=in_specs,
            out_specs=pl.BlockSpec((count, wide), lambda i, at: (at[0], i)),
            scratch_shapes=[
                pltpu.VMEM((2, markers, count), BF16),
                pltpu.VMEM((count, markers), BF16),
                pltpu.VMEM((count, markers), BF16),
                pltpu.SemaphoreType.DMA((rows * ratio * 2,)),
            ],
        ),
        out_shape=jax.ShapeDtypeStruct((people, width), F32),
        input_output_aliases=aliases,
        compiler_params=pltpu.CompilerParams(vmem_limit_bytes=VMEM_LIMIT),
        name="kinship",
    )(part[None].astype(jnp.int32), *operands)


def per_device(dosage, present, components):
    rows, cols = lax.axis_size("rows"), lax.axis_size("cols")
    ratio = cols // rows
    markers, people = dosage.shape
    comps = components.shape[0]
    width = people // ratio
    row = lax.axis_index("rows")
    col = lax.axis_index("cols")
    core, plane = col % ratio, col // ratio

    def pairs(hop):
        moves = [(z, c, *hop(z, c)) for z in range(rows) for c in range(ratio)]
        return [(z * ratio + c, y * ratio + b) for z, c, y, b in moves if 0 <= y < rows]

    def across(x, axis, size):
        return [x] + [lax.ppermute(x, axis, [(i, i ^ d) for i in range(size)]) for d in range(1, size)]

    def swap(x, k):
        return lax.ppermute(x, "cols", pairs(lambda z, c: (z, (c + k) % ratio))) if k else x

    def along(x, way):
        return lax.ppermute(x, "cols", pairs(lambda z, c: (z + way, c)))

    halves = []
    for k in range(ratio):
        begin = (core + k) % ratio * width
        both = [lax.dynamic_slice_in_dim(x, begin, width, 1).astype(BF16) for x in (dosage, present)]
        halves.append(swap(jnp.concatenate(both, axis=0), k))
    held = jnp.concatenate(halves, axis=0)
    held, dosage, present = lax.optimization_barrier((held, dosage, present))
    from_left, from_right = [along(held, 1)], [along(held, -1)]

    height = held.shape[0] // rows
    quarters = []
    for d in range(rows):
        mine = lax.dynamic_slice_in_dim(held, (row ^ d) * height, height, 0)
        quarters.append(lax.ppermute(mine, "rows", [(i, i ^ d) for i in range(rows)]) if d else mine)
    gram = gram_call(dosage, present, components)
    col_comps = lax.dynamic_slice_in_dim(components, core * width, width, 1)
    hops = [1 << i for i in range(rows.bit_length() - 1)]
    first, later = hops[0], hops[1:]

    def doubled(x, hop):
        moves = [
            (r * cols + z * ratio + c, (r ^ hop) * cols + z * ratio + c)
            for z in range(rows)
            for r in range(rows)
            if (r ^ z) < hop
            for c in range(ratio)
        ]
        return jnp.where((row ^ plane) < hop, x, lax.ppermute(x, ("rows", "cols"), moves))

    quarters, gram, col_comps, from_left, from_right = lax.optimization_barrier(
        (jnp.stack(quarters), gram, col_comps, from_left, from_right)
    )
    moved = []
    for e in range(rows):
        mine = lax.dynamic_index_in_dim(quarters, row ^ plane ^ e, 0, keepdims=False)
        moved.append(lax.ppermute(mine, "cols", pairs(lambda z, c: (z ^ e, c))) if e else mine)
    for hop in hops[:-1]:
        gram = gram + lax.ppermute(gram, "rows", [(i, i ^ hop) for i in range(rows)])
    grams = [gram, lax.ppermute(gram, "rows", [(i, i ^ hops[-1]) for i in range(rows)])]
    coef = solve_call(grams, comps, markers)
    coef = jnp.concatenate([swap(coef, k) for k in range(ratio)], axis=0)
    col_comps = doubled(col_comps, first)
    moved, coef, col_comps, held, from_left, from_right = lax.optimization_barrier(
        (jnp.stack(moved), coef, col_comps, held, from_left, from_right)
    )
    coefs = [lax.ppermute(coef, "cols", pairs(lambda z, c: (z ^ e, c))) if e else coef for e in range(rows)]
    coefs, from_left, from_right = lax.optimization_barrier((coefs, from_left, from_right))
    for hop in later:
        col_comps = doubled(col_comps, hop)
    pieces = [moved]
    for step in range(rows - 2):
        from_left.append(along(from_left[-1], 1))
        from_right.append(along(from_right[-1], -1))
        begin, end = (rows * step + rows - 3) // (rows - 2), (rows * (step + 1) + rows - 3) // (rows - 2)
        for d in range(max(begin, 1), min(end, rows - 1) + 1 if step < rows - 3 else rows):
            if d == len(pieces):
                pieces.append(lax.ppermute(moved, "rows", [(i, i ^ d) for i in range(rows)]))
        if step < rows - 3:
            pieces, col_comps, held, from_left, from_right = lax.optimization_barrier(
                (pieces, col_comps, held, from_left, from_right)
            )
    slots = [held]
    for slot in range(1, rows):
        slots.append(jnp.where(plane >= slot, from_left[slot - 1], from_right[rows - slot - 1]))
    coef, col_r, col_s = columns_call(rows, ratio, cols, col_comps, coefs, pieces)
    out = None
    for turn in range(ratio):
        part = (core + ratio - turn) % ratio
        came = [swap(block, turn) for block in slots]
        out = kin_call(rows, ratio, turn, part, components, coef, col_r, col_s, came, out)
    return out


def solution(mesh):
    placed = (P("cols", "rows"), P("cols", "rows"), P(None, "rows"))
    return jax.shard_map(
        per_device, mesh=mesh, in_specs=placed, out_specs=P("rows", "cols"), check_vma=False
    )
```

```python
import functools

import jax
import jax.numpy as jnp
from jax import lax
from jax.experimental import pallas as pl
from jax.experimental.pallas import tpu as pltpu
from jax.sharding import PartitionSpec as P

F32, BF16 = jnp.float32, jnp.bfloat16
VMEM_LIMIT = 56 * 1024 * 1024
SUB = 8


def split3(x):
    high = x.astype(BF16)
    rest = x - high.astype(F32)
    mid = rest.astype(BF16)
    low = (rest - mid.astype(F32)).astype(BF16)
    return high, mid, low


def group_starts(comps):
    starts, at = [], 0
    for j in range(comps):
        first = j // SUB * SUB
        starts.append((at, first))
        at += comps - first
    return starts, at


def gram_kernel(dosage_ref, present_ref, comps_ref, out_ref, lhs_ref):
    comps, people = comps_ref.shape
    markers = dosage_ref.shape[0]
    starts, total = group_starts(comps)
    chunk = 512 if people % 512 == 0 else people
    acc = None
    for at in range(0, people, chunk):
        span = slice(at, at + chunk)
        obs = present_ref[:, span].astype(F32)
        tgt = 0.5 * dosage_ref[:, span].astype(F32) * obs
        rhs = jnp.concatenate([obs, tgt], axis=0).astype(BF16)
        x = comps_ref[:, span]
        for j, (start, first) in enumerate(starts):
            lhs_ref[start : start + comps - first, :] = x[first:, :] * x[j : j + 1, :]
        lhs_ref[total : total + comps, :] = x
        tail = lhs_ref.shape[0] - total - comps
        lhs_ref[total + comps :, :] = jnp.ones((tail, chunk), F32)
        for part in split3(lhs_ref[...]):
            term = lax.dot_general(part, rhs, (((1,), (1,)), ((), ())), preferred_element_type=F32)
            acc = term if acc is None else acc + term
    half = total // 2
    out_ref[0:half, :] = jnp.concatenate([acc[0:half, 0:markers], acc[half:total, 0:markers]], axis=1)
    out_ref[half:, :] = acc[total : total + comps + SUB, :]


def gram_call(dosage, present, components):
    markers, people = dosage.shape
    comps = components.shape[0]
    total = group_starts(comps)[1]
    chunk = 512 if people % 512 == 0 else people
    return pl.pallas_call(
        gram_kernel,
        out_shape=jax.ShapeDtypeStruct((total // 2 + comps + SUB, 2 * markers), F32),
        scratch_shapes=[pltpu.VMEM((total + comps + 2 * SUB, chunk), F32)],
        compiler_params=pltpu.CompilerParams(vmem_limit_bytes=VMEM_LIMIT),
        name="gram",
    )(dosage, present, components)


def coef_rows(comps):
    return 6 * comps + 2 * SUB


def below(old, first, new):
    return new if first == 0 else jnp.concatenate([old[:first], new], axis=0)


def solve_kernel(comps, markers, *refs):
    out_ref = refs[-1]
    summed = refs[0][...]
    for ref in refs[1:-1]:
        summed = summed + ref[...]
    starts, total = group_starts(comps)
    half = total // 2
    left, right = summed[:, 0:markers], summed[:, markers : 2 * markers]

    def rows_of(start, count):
        if start + count <= half:
            return left[start : start + count]
        if start >= half:
            return right[start - half : start - half + count]
        return jnp.concatenate([left[start:half], right[0 : start + count - half]], axis=0)

    columns = [rows_of(start, comps - first) for start, first in starts]
    firsts = [first for _, first in starts]
    edge = left[half : half + comps]
    count = left[half + comps : half + comps + 1]
    moment = right[half : half + comps]
    moment_one = right[half + comps : half + comps + 1]
    factor, edge_f, moment_f = [], [], []
    for j in range(comps):
        first = firsts[j]
        column = columns[j]
        inv = 1.0 / column[j - first : j - first + 1]
        scaled = column * inv
        edge_j = edge[j : j + 1]
        moment_j = moment[j : j + 1]
        edge_s, moment_s = edge_j * inv, moment_j * inv
        row = lax.broadcasted_iota(jnp.int32, column.shape, 0) + first
        factor.append(jnp.where(row > j, scaled, 0.0))
        edge_f.append(edge_s)
        moment_f.append(moment_s)
        count = count - edge_s * edge_j
        moment_one = moment_one - edge_s * moment_j
        if j + 1 < comps:
            edge = below(edge, first, edge[first:] - column * edge_s)
            moment = below(moment, first, moment[first:] - column * moment_s)
        for k in range(j + 1, comps):
            offset = firsts[k] - first
            columns[k] = columns[k] - scaled[offset:] * column[k - first : k - first + 1]
    last = moment_one / count
    index = lax.broadcasted_iota(jnp.int32, (SUB, markers), 0)
    groups = [jnp.zeros((SUB, markers), F32) for _ in range(comps // SUB)]
    for j in range(comps - 1, -1, -1):
        first = firsts[j]
        value = moment_f[j] - edge_f[j] * last
        total_term = None
        for g in range(first // SUB, comps // SUB):
            term = factor[j][g * SUB - first : (g + 1) * SUB - first] * groups[g]
            total_term = term if total_term is None else total_term + term
        value = value - jnp.sum(total_term, axis=0, keepdims=True)
        g = j // SUB
        groups[g] = jnp.where(index == j - first, value, groups[g])
    coef = 2.0 * jnp.concatenate(groups, axis=0)
    last = 2.0 * last
    c1, c2, c3 = [part.astype(F32) for part in split3(coef)]
    l1, l2, l3 = [part.astype(F32) for part in split3(last)]
    index = lax.broadcasted_iota(jnp.int32, (2 * SUB, markers), 0)
    ones = jnp.where(index == 0, l1, jnp.where(index == 1, l2, jnp.where(index == 2, l3, 0.0)))
    stacked = jnp.concatenate([c1, c1, c2, c2, c1, c3, ones], axis=0).astype(BF16)
    eye = (
        lax.broadcasted_iota(jnp.int32, (markers, markers), 0)
        == lax.broadcasted_iota(jnp.int32, (markers, markers), 1)
    ).astype(F32).astype(BF16)
    turned = lax.dot_general(eye, stacked, (((1,), (1,)), ((), ())), preferred_element_type=F32)
    out_ref[...] = turned.astype(BF16)


def solve_call(parts, comps, markers):
    return pl.pallas_call(
        functools.partial(solve_kernel, comps, markers),
        out_shape=jax.ShapeDtypeStruct((markers, coef_rows(comps)), BF16),
        compiler_params=pltpu.CompilerParams(vmem_limit_bytes=VMEM_LIMIT),
        name="solve",
    )(*parts)


def design_parts(x):
    d1, d2, d3 = split3(x)
    ones = jnp.ones((2 * SUB, x.shape[1]), BF16)
    return jnp.concatenate([d1, d2, d1, d2, d3, d1, ones], axis=0)


def factors(twice):
    twice = jnp.clip(twice, 0.02, 1.98)
    spread = twice * (2.0 - twice)
    return twice, spread * lax.rsqrt(spread)


def weigh(fitted, dosage, observed):
    twice, spread = factors(fitted)
    return (observed * (dosage - twice)).astype(BF16), (observed * spread).astype(BF16)


def parted(block, groups):
    block = block.astype(F32)
    height = block.shape[0] // (2 * groups)
    dosage = [block[2 * g * height : (2 * g + 1) * height] for g in range(groups)]
    present = [block[(2 * g + 1) * height : (2 * g + 2) * height] for g in range(groups)]
    if groups == 1:
        return dosage[0], present[0]
    return jnp.concatenate(dosage, axis=0), jnp.concatenate(present, axis=0)


def early_source(plane, rows):
    return jnp.where(plane == 0, 1, plane - 1)


def late_source(plane, rows):
    return jnp.where(plane == 0, rows - 1, jnp.where(plane == rows - 1, 0, plane + 1))


def slot_of(source, plane, rows):
    slot = lax.rem(plane - source + rows, rows) - 1
    slot = jnp.where(source == early_source(plane, rows), rows - 2, slot)
    slot = jnp.where(source == late_source(plane, rows), rows - 1, slot)
    return jnp.where(source == plane, 0, slot)


def early_kernel(rows, near, row_x_ref, col_x_ref, *refs):
    coef_refs, refs = refs[: rows.bit_length()], refs[rows.bit_length() :]
    held_ref, refs = refs[0], refs[1:]
    from_left, from_right = refs[: rows - 2], refs[rows - 2 : 2 * rows - 4]
    piece_refs, refs = refs[2 * rows - 4 : 2 * rows - 4 + near], refs[2 * rows - 4 + near :]
    row_out, col_out, row_fit, col_fit, coef, fit = refs
    chip = coef_refs[0].shape[0]
    height = chip // rows
    space = coef.shape[0] // rows
    row = lax.axis_index("rows")
    plane = lax.axis_index("cols") // (lax.axis_size("cols") // rows)
    slots = [slot_of(plane ^ e, plane, rows) for e in range(rows)]

    @pl.when(pl.program_id(0) == 0)
    def _():
        if space != chip:
            coef[...] = jnp.zeros(coef.shape, BF16)
        found = [ref[at : at + chip, :] for ref in coef_refs for at in range(0, ref.shape[0], chip)]
        for e in range(rows):
            coef[pl.ds(pl.multiple_of(slots[e] * space, space), chip), :] = found[e]

    def fitted(x):
        return lax.dot_general(
            coef[...], design_parts(x), (((1,), (0,)), ((), ())), preferred_element_type=F32
        )

    if space != chip:
        row_out[...] = jnp.zeros(row_out.shape, BF16)
        col_out[...] = jnp.zeros(col_out.shape, BF16)
    fit_rows = fitted(row_x_ref[...])
    for slot in range(rows - 1):
        if slot == 0:
            block = held_ref[...]
        elif slot == rows - 2:
            block = jnp.where(plane == 0, from_right[0][...], from_left[0][...])
        else:
            away = slot + 1
            block = jnp.where(plane >= away, from_left[away - 1][...], from_right[rows - away - 1][...])
        resid, sdev = weigh(fit_rows[slot * space : slot * space + chip], *parted(block, rows))
        row_out[0, :, slot * space : slot * space + chip] = resid.T
        row_out[1, :, slot * space : slot * space + chip] = sdev.T
    row_fit[...] = fit_rows[(rows - 1) * space : (rows - 1) * space + chip]
    fit[...] = fitted(col_x_ref[...])
    for d in range(rows):
        for e in range(rows):
            place = pl.multiple_of(slots[e] * space + (row ^ d) * height, height)
            here = fit[pl.ds(place, height), :]
            if d < near:
                resid, sdev = weigh(here, *parted(piece_refs[d][e], 1))
                group = slots[e] * (space // height) + (row ^ d)
                col_out[0, group] = resid
                col_out[1, group] = sdev
            else:
                col_fit[e] = here


def early_call(rows, part, components, col_comps, coefs, held, from_left, from_right, pieces):
    comps, width = col_comps.shape
    chip = coefs[0].shape[0]
    space = -(-chip // 128) * 128
    height = chip // rows
    wide = 256 if width % 256 == 0 else width
    whole = lambda i, at: (0, 0)
    block = pl.BlockSpec((2 * chip, wide), lambda i, at: (0, i))
    piece = pl.BlockSpec((rows, 2 * height, wide), lambda i, at: (0, 0, i))
    return pl.pallas_call(
        functools.partial(early_kernel_at, rows, len(pieces)),
        grid_spec=pltpu.PrefetchScalarGridSpec(
            num_scalar_prefetch=1,
            grid=(width // wide,),
            in_specs=[
                pl.BlockSpec((comps, wide), lambda i, at: (0, at[0] * (width // wide) + i)),
                pl.BlockSpec((comps, wide), lambda i, at: (0, i)),
            ]
            + [pl.BlockSpec(x.shape, whole) for x in coefs]
            + [block] * (1 + len(from_left) + len(from_right))
            + [piece] * len(pieces),
            out_specs=(
                pl.BlockSpec((2, wide, rows * space), lambda i, at: (0, i, 0)),
                pl.BlockSpec((2, rows * space // height, height, wide), lambda i, at: (0, 0, 0, i)),
                pl.BlockSpec((chip, wide), lambda i, at: (0, i)),
                pl.BlockSpec((rows, height, wide), lambda i, at: (0, 0, i)),
            ),
            scratch_shapes=[
                pltpu.VMEM((rows * space, coefs[0].shape[1]), BF16),
                pltpu.VMEM((rows * space, wide), F32),
            ],
        ),
        out_shape=(
            jax.ShapeDtypeStruct((2, width, rows * space), BF16),
            jax.ShapeDtypeStruct((2, rows * space // height, height, width), BF16),
            jax.ShapeDtypeStruct((chip, width), F32),
            jax.ShapeDtypeStruct((rows, height, width), F32),
        ),
        compiler_params=pltpu.CompilerParams(vmem_limit_bytes=VMEM_LIMIT),
        name="early",
    )(part[None].astype(jnp.int32), components, col_comps, *coefs, held, *from_left, *from_right, *pieces)


def early_kernel_at(rows, near, part_ref, *refs):
    early_kernel(rows, near, *refs)


def late_kernel(rows, group_ref, row_fit, col_fit, left_ref, right_ref, next_ref, piece_ref, *refs):
    row_out, col_out = refs[2:]
    plane = lax.axis_index("cols") // (lax.axis_size("cols") // rows)
    resid, sdev = weigh(col_fit[0], *parted(piece_ref[0], 1))
    col_out[0, 0] = resid
    col_out[1, 0] = sdev

    @pl.when(pl.program_id(0) == 0)
    def _():
        block = jnp.where(plane == rows - 1, left_ref[...], next_ref[...])
        block = jnp.where(plane == 0, right_ref[...], block)
        resid, sdev = weigh(row_fit[...], *parted(block, rows))
        chip = row_fit.shape[0]
        if row_out.shape[2] != chip:
            row_out[...] = jnp.zeros(row_out.shape, BF16)
        row_out[0, :, 0:chip] = resid.T
        row_out[1, :, 0:chip] = sdev.T


def late_call(rows, groups, row_fit, col_fit, left, right, following, piece, row_panel, col_panel):
    chip, width = row_fit.shape
    height = chip // rows
    space = row_panel.shape[2] // rows
    whole = pl.BlockSpec((2 * chip, width), lambda e, at: (0, 0))
    anywhere = pl.BlockSpec(memory_space=pl.ANY)
    return pl.pallas_call(
        functools.partial(late_kernel, rows),
        grid_spec=pltpu.PrefetchScalarGridSpec(
            num_scalar_prefetch=1,
            grid=(rows,),
            in_specs=[
                pl.BlockSpec((chip, width), lambda e, at: (0, 0)),
                pl.BlockSpec((1, height, width), lambda e, at: (e, 0, 0)),
                whole,
                whole,
                whole,
                pl.BlockSpec((1, 2 * height, width), lambda e, at: (e, 0, 0)),
                anywhere,
                anywhere,
            ],
            out_specs=(
                pl.BlockSpec((2, width, space), lambda e, at: (0, 0, rows - 1)),
                pl.BlockSpec((2, 1, height, width), lambda e, at: (0, at[e], 0, 0)),
            ),
        ),
        out_shape=(
            jax.ShapeDtypeStruct(row_panel.shape, BF16),
            jax.ShapeDtypeStruct(col_panel.shape, BF16),
        ),
        input_output_aliases={7: 0, 8: 1},
        compiler_params=pltpu.CompilerParams(vmem_limit_bytes=VMEM_LIMIT),
        name="late",
    )(groups, row_fit, col_fit, left, right, following, piece, row_panel, col_panel)


def quotient(numer, denom):
    inverse = pl.reciprocal(denom, approx=True)
    return numer * (inverse * (2.0 - denom * inverse))


def kin_kernel(part_ref, row_ref, col_ref, *refs):
    out_ref = refs[-1]
    numer = jnp.dot(row_ref[0], col_ref[0], preferred_element_type=F32)
    denom = jnp.dot(row_ref[1], col_ref[1], preferred_element_type=F32)
    out_ref[...] = quotient(numer, denom)


def kin_call(part, people, row_panel, col_panel, before):
    _, count, depth = row_panel.shape
    width = col_panel.shape[2]
    wide = 256 if width % 256 == 0 else width
    in_specs = [
        pl.BlockSpec((2, count, depth), lambda i, at: (0, 0, 0)),
        pl.BlockSpec((2, depth, wide), lambda i, at: (0, 0, i)),
    ]
    operands = [row_panel, col_panel]
    aliases = {}
    if before is not None:
        in_specs.append(pl.BlockSpec(memory_space=pl.ANY))
        operands.append(before)
        aliases = {len(operands): 0}
    return pl.pallas_call(
        kin_kernel,
        grid_spec=pltpu.PrefetchScalarGridSpec(
            num_scalar_prefetch=1,
            grid=(width // wide,),
            in_specs=in_specs,
            out_specs=pl.BlockSpec((count, wide), lambda i, at: (at[0], i)),
        ),
        out_shape=jax.ShapeDtypeStruct((people, width), F32),
        input_output_aliases=aliases,
        compiler_params=pltpu.CompilerParams(vmem_limit_bytes=VMEM_LIMIT),
        name="kinship",
    )(part[None].astype(jnp.int32), *operands)


def per_device(dosage, present, components):
    rows, cols = lax.axis_size("rows"), lax.axis_size("cols")
    ratio = cols // rows
    markers, people = dosage.shape
    comps = components.shape[0]
    width = people // ratio
    row = lax.axis_index("rows")
    col = lax.axis_index("cols")
    core, plane = col % ratio, col // ratio

    def pairs(hop):
        moves = [(z, c, *hop(z, c)) for z in range(rows) for c in range(ratio)]
        return [(z * ratio + c, y * ratio + b) for z, c, y, b in moves if 0 <= y < rows]

    def swap(x, k):
        return lax.ppermute(x, "cols", pairs(lambda z, c: (z, (c + k) % ratio))) if k else x

    def along(x, way):
        return lax.ppermute(x, "cols", pairs(lambda z, c: (z + way, c)))

    def beside(x, d):
        return lax.ppermute(x, "rows", [(i, i ^ d) for i in range(rows)]) if d else x

    def across(x, e):
        return lax.ppermute(x, "cols", pairs(lambda z, c: (z ^ e, c))) if e else x

    def by_core(parts):
        placed = []
        for p in range(ratio):
            chosen = parts[0]
            for k in range(1, ratio):
                chosen = jnp.where((core - p) % ratio == k, parts[k], chosen)
            placed.append(chosen)
        return jnp.concatenate(placed, axis=0)

    subs = rows // ratio
    fine = markers // subs
    halves = []
    for k in range(ratio):
        begin = (core + k) % ratio * width
        both = [
            lax.dynamic_slice_in_dim(x, begin, width, 1).astype(BF16).reshape(subs, 1, fine, width)
            for x in (dosage, present)
        ]
        halves.append(swap(jnp.concatenate(both, axis=1).reshape(2 * markers, width), k))
    held = by_core(halves)
    held, dosage, present = lax.optimization_barrier((held, dosage, present))
    from_left, from_right = [along(held, 1)], [along(held, -1)]

    height = held.shape[0] // rows
    quarters = [beside(lax.dynamic_slice_in_dim(held, (row ^ d) * height, height, 0), d) for d in range(rows)]
    hops = [1 << i for i in range(rows.bit_length() - 1)]
    gram = gram_call(dosage, present, components)
    for hop in hops[:-1]:
        gram = gram + beside(gram, hop)
    grams = [gram, beside(gram, hops[-1])]
    col_comps = lax.dynamic_slice_in_dim(components, core * width, width, 1)
    quarters, grams, col_comps, from_left, from_right = lax.optimization_barrier(
        (jnp.stack(quarters), grams, col_comps, from_left, from_right)
    )
    moved = [
        across(lax.dynamic_index_in_dim(quarters, row ^ plane ^ e, 0, keepdims=False), e) for e in range(rows)
    ]
    def doubled(x, hop):
        moves = [
            (r * cols + z * ratio + c, (r ^ hop) * cols + z * ratio + c)
            for z in range(rows)
            for r in range(rows)
            if (r ^ z) < hop
            for c in range(ratio)
        ]
        return jnp.where((row ^ plane) < hop, x, lax.ppermute(x, ("rows", "cols"), moves))

    for hop in hops:
        col_comps = doubled(col_comps, hop)
    coef = solve_call(grams, comps, markers)
    moved, coef, col_comps, held, from_left, from_right = lax.optimization_barrier(
        (jnp.stack(moved), coef, col_comps, held, from_left, from_right)
    )
    coefs = [by_core([swap(coef, k) for k in range(ratio)])]
    for hop in hops:
        coefs.append(across(coefs[0] if len(coefs) == 1 else jnp.concatenate(coefs, axis=0), hop))
    near = [moved]
    for step in range(rows - 3):
        from_left.append(along(from_left[-1], 1))
        from_right.append(along(from_right[-1], -1))
        upto = rows - 1 if step == rows - 4 else min(rows - 1, 2 * step + 3)
        near += [beside(moved, d) for d in range(len(near), upto)]
        near, coefs, col_comps, held, from_left, from_right = lax.optimization_barrier(
            (near, coefs, col_comps, held, from_left, from_right)
        )
    last_left, last_right = along(from_left[-1], 1), along(from_right[-1], -1)
    far = beside(near[0], rows - 1)
    row_panel, col_panel, row_fit, col_fit = early_call(
        rows, core, components, col_comps, coefs, held, from_left, from_right, near
    )
    space = row_panel.shape[2] // rows
    groups = jnp.stack(
        [
            slot_of(plane ^ e, plane, rows) * (2 * space // height) + (row ^ (rows - 1))
            for e in range(rows)
        ]
    ).astype(jnp.int32)
    row_panel, col_panel = late_call(
        rows, groups, row_fit, col_fit, last_left, last_right, from_right[0], far, row_panel, col_panel
    )
    col_panel = col_panel.reshape(2, rows * space, width)
    out = None
    for turn in range(ratio):
        out = kin_call((core + ratio - turn) % ratio, people, swap(row_panel, turn), col_panel, out)
    return out


def solution(mesh):
    placed = (P("cols", "rows"), P("cols", "rows"), P(None, "rows"))
    return jax.shard_map(
        per_device, mesh=mesh, in_specs=placed, out_specs=P("rows", "cols"), check_vma=False
    )
```

```python
import functools

import jax
import jax.numpy as jnp
from jax import lax
from jax.experimental import pallas as pl
from jax.experimental.pallas import tpu as pltpu
from jax.sharding import PartitionSpec as P

F32, BF16 = jnp.float32, jnp.bfloat16
VMEM_LIMIT = 56 * 1024 * 1024
SUB = 8


def split3(x):
    high = x.astype(BF16)
    rest = x - high.astype(F32)
    mid = rest.astype(BF16)
    low = (rest - mid.astype(F32)).astype(BF16)
    return high, mid, low


def group_starts(comps):
    starts, at = [], 0
    for j in range(comps):
        first = j // SUB * SUB
        starts.append((at, first))
        at += comps - first
    return starts, at


def gram_kernel(dosage_ref, present_ref, comps_ref, out_ref, lhs_ref):
    comps, people = comps_ref.shape
    markers = dosage_ref.shape[0]
    starts, total = group_starts(comps)
    chunk = 512 if people % 512 == 0 else people
    acc = None
    for at in range(0, people, chunk):
        span = slice(at, at + chunk)
        obs = present_ref[:, span].astype(F32)
        tgt = 0.5 * dosage_ref[:, span].astype(F32) * obs
        rhs = jnp.concatenate([obs, tgt], axis=0).astype(BF16)
        x = comps_ref[:, span]
        for j, (start, first) in enumerate(starts):
            lhs_ref[start : start + comps - first, :] = x[first:, :] * x[j : j + 1, :]
        lhs_ref[total : total + comps, :] = x
        tail = lhs_ref.shape[0] - total - comps
        lhs_ref[total + comps :, :] = jnp.ones((tail, chunk), F32)
        for part in split3(lhs_ref[...]):
            term = lax.dot_general(part, rhs, (((1,), (1,)), ((), ())), preferred_element_type=F32)
            acc = term if acc is None else acc + term
    half = total // 2
    out_ref[0:half, :] = jnp.concatenate([acc[0:half, 0:markers], acc[half:total, 0:markers]], axis=1)
    out_ref[half:, :] = acc[total : total + comps + SUB, :]


def gram_call(dosage, present, components):
    markers, people = dosage.shape
    comps = components.shape[0]
    total = group_starts(comps)[1]
    chunk = 512 if people % 512 == 0 else people
    return pl.pallas_call(
        gram_kernel,
        out_shape=jax.ShapeDtypeStruct((total // 2 + comps + SUB, 2 * markers), F32),
        scratch_shapes=[pltpu.VMEM((total + comps + 2 * SUB, chunk), F32)],
        compiler_params=pltpu.CompilerParams(vmem_limit_bytes=VMEM_LIMIT),
        name="gram",
    )(dosage, present, components)


def coef_rows(comps):
    return 6 * comps + 2 * SUB


def below(old, first, new):
    return new if first == 0 else jnp.concatenate([old[:first], new], axis=0)


def solve_kernel(comps, markers, *refs):
    out_ref = refs[-1]
    summed = refs[0][...]
    for ref in refs[1:-1]:
        summed = summed + ref[...]
    starts, total = group_starts(comps)
    half = total // 2
    left, right = summed[:, 0:markers], summed[:, markers : 2 * markers]

    def rows_of(start, count):
        if start + count <= half:
            return left[start : start + count]
        if start >= half:
            return right[start - half : start - half + count]
        return jnp.concatenate([left[start:half], right[0 : start + count - half]], axis=0)

    columns = [rows_of(start, comps - first) for start, first in starts]
    firsts = [first for _, first in starts]
    edge = left[half : half + comps]
    count = left[half + comps : half + comps + 1]
    moment = right[half : half + comps]
    moment_one = right[half + comps : half + comps + 1]
    factor, edge_f, moment_f = [], [], []
    for j in range(comps):
        first = firsts[j]
        column = columns[j]
        inv = 1.0 / column[j - first : j - first + 1]
        scaled = column * inv
        edge_j = edge[j : j + 1]
        moment_j = moment[j : j + 1]
        edge_s, moment_s = edge_j * inv, moment_j * inv
        row = lax.broadcasted_iota(jnp.int32, column.shape, 0) + first
        factor.append(jnp.where(row > j, scaled, 0.0))
        edge_f.append(edge_s)
        moment_f.append(moment_s)
        count = count - edge_s * edge_j
        moment_one = moment_one - edge_s * moment_j
        if j + 1 < comps:
            edge = below(edge, first, edge[first:] - column * edge_s)
            moment = below(moment, first, moment[first:] - column * moment_s)
        for k in range(j + 1, comps):
            offset = firsts[k] - first
            columns[k] = columns[k] - scaled[offset:] * column[k - first : k - first + 1]
    last = moment_one / count
    index = lax.broadcasted_iota(jnp.int32, (SUB, markers), 0)
    groups = [jnp.zeros((SUB, markers), F32) for _ in range(comps // SUB)]
    for j in range(comps - 1, -1, -1):
        first = firsts[j]
        value = moment_f[j] - edge_f[j] * last
        total_term = None
        for g in range(first // SUB, comps // SUB):
            term = factor[j][g * SUB - first : (g + 1) * SUB - first] * groups[g]
            total_term = term if total_term is None else total_term + term
        value = value - jnp.sum(total_term, axis=0, keepdims=True)
        g = j // SUB
        groups[g] = jnp.where(index == j - first, value, groups[g])
    coef = 2.0 * jnp.concatenate(groups, axis=0)
    last = 2.0 * last
    c1, c2, c3 = [part.astype(F32) for part in split3(coef)]
    l1, l2, l3 = [part.astype(F32) for part in split3(last)]
    index = lax.broadcasted_iota(jnp.int32, (2 * SUB, markers), 0)
    ones = jnp.where(index == 0, l1, jnp.where(index == 1, l2, jnp.where(index == 2, l3, 0.0)))
    stacked = jnp.concatenate([c1, c1, c2, c2, c1, c3, ones], axis=0).astype(BF16)
    eye = (
        lax.broadcasted_iota(jnp.int32, (markers, markers), 0)
        == lax.broadcasted_iota(jnp.int32, (markers, markers), 1)
    ).astype(F32).astype(BF16)
    turned = lax.dot_general(eye, stacked, (((1,), (1,)), ((), ())), preferred_element_type=F32)
    out_ref[...] = turned.astype(BF16)


def solve_call(parts, comps, markers):
    return pl.pallas_call(
        functools.partial(solve_kernel, comps, markers),
        out_shape=jax.ShapeDtypeStruct((markers, coef_rows(comps)), BF16),
        compiler_params=pltpu.CompilerParams(vmem_limit_bytes=VMEM_LIMIT),
        name="solve",
    )(*parts)


def design_parts(x):
    d1, d2, d3 = split3(x)
    ones = jnp.ones((2 * SUB, x.shape[1]), BF16)
    return jnp.concatenate([d1, d2, d1, d2, d3, d1, ones], axis=0)


def factors(twice):
    twice = jnp.clip(twice, 0.02, 1.98)
    spread = twice * (2.0 - twice)
    return twice, spread * lax.rsqrt(spread)


def weigh(fitted, dosage, observed):
    twice, spread = factors(fitted)
    return (observed * (dosage - twice)).astype(BF16), (observed * spread).astype(BF16)


def parted(block, groups):
    block = block.astype(F32)
    height = block.shape[0] // (2 * groups)
    dosage = [block[2 * g * height : (2 * g + 1) * height] for g in range(groups)]
    present = [block[(2 * g + 1) * height : (2 * g + 2) * height] for g in range(groups)]
    if groups == 1:
        return dosage[0], present[0]
    return jnp.concatenate(dosage, axis=0), jnp.concatenate(present, axis=0)


def early_source(plane, rows):
    return jnp.where(plane == 0, 1, plane - 1)


def late_source(plane, rows):
    return jnp.where(plane == 0, rows - 1, jnp.where(plane == rows - 1, 0, plane + 1))


def slot_of(source, plane, rows):
    slot = lax.rem(plane - source + rows, rows) - 1
    slot = jnp.where(source == early_source(plane, rows), rows - 2, slot)
    slot = jnp.where(source == late_source(plane, rows), rows - 1, slot)
    return jnp.where(source == plane, 0, slot)


def early_kernel(rows, near, row_x_ref, col_x_ref, *refs):
    coef_refs, refs = refs[: rows.bit_length()], refs[rows.bit_length() :]
    held_ref, refs = refs[0], refs[1:]
    from_left, from_right = refs[: rows - 2], refs[rows - 2 : 2 * rows - 4]
    piece_refs, refs = refs[2 * rows - 4 : 2 * rows - 4 + near], refs[2 * rows - 4 + near :]
    row_out, col_out, row_fit, col_fit, coef, fit = refs
    chip = coef_refs[0].shape[0]
    height = chip // rows
    space = coef.shape[0] // rows
    row = lax.axis_index("rows")
    plane = lax.axis_index("cols") // (lax.axis_size("cols") // rows)
    slots = [slot_of(plane ^ e, plane, rows) for e in range(rows)]

    @pl.when(pl.program_id(0) == 0)
    def _():
        if space != chip:
            coef[...] = jnp.zeros(coef.shape, BF16)
        found = [ref[at : at + chip, :] for ref in coef_refs for at in range(0, ref.shape[0], chip)]
        for e in range(rows):
            coef[pl.ds(pl.multiple_of(slots[e] * space, space), chip), :] = found[e]

    def fitted(x):
        return lax.dot_general(
            coef[...], design_parts(x), (((1,), (0,)), ((), ())), preferred_element_type=F32
        )

    if space != chip:
        row_out[...] = jnp.zeros(row_out.shape, BF16)
        col_out[...] = jnp.zeros(col_out.shape, BF16)
    fit_rows = fitted(row_x_ref[...])
    for slot in range(rows - 1):
        if slot == 0:
            block = held_ref[...]
        elif slot == rows - 2:
            block = jnp.where(plane == 0, from_right[0][...], from_left[0][...])
        else:
            away = slot + 1
            block = jnp.where(plane >= away, from_left[away - 1][...], from_right[rows - away - 1][...])
        resid, sdev = weigh(fit_rows[slot * space : slot * space + chip], *parted(block, rows))
        row_out[0, :, slot * space : slot * space + chip] = resid.T
        row_out[1, :, slot * space : slot * space + chip] = sdev.T
    row_fit[...] = fit_rows[(rows - 1) * space : (rows - 1) * space + chip]
    fit[...] = fitted(col_x_ref[...])
    for d in range(rows):
        for e in range(rows):
            place = pl.multiple_of(slots[e] * space + (row ^ d) * height, height)
            here = fit[pl.ds(place, height), :]
            if d < near:
                resid, sdev = weigh(here, *parted(piece_refs[d][e], 1))
                group = slots[e] * (space // height) + (row ^ d)
                col_out[0, group] = resid
                col_out[1, group] = sdev
            else:
                col_fit[e] = here


def early_call(rows, part, components, col_comps, coefs, held, from_left, from_right, pieces):
    comps, width = col_comps.shape
    chip = coefs[0].shape[0]
    space = -(-chip // 128) * 128
    height = chip // rows
    wide = 256 if width % 256 == 0 else width
    whole = lambda i, at: (0, 0)
    block = pl.BlockSpec((2 * chip, wide), lambda i, at: (0, i))
    piece = pl.BlockSpec((rows, 2 * height, wide), lambda i, at: (0, 0, i))
    return pl.pallas_call(
        functools.partial(early_kernel_at, rows, len(pieces)),
        grid_spec=pltpu.PrefetchScalarGridSpec(
            num_scalar_prefetch=1,
            grid=(width // wide,),
            in_specs=[
                pl.BlockSpec((comps, wide), lambda i, at: (0, at[0] * (width // wide) + i)),
                pl.BlockSpec((comps, wide), lambda i, at: (0, i)),
            ]
            + [pl.BlockSpec(x.shape, whole) for x in coefs]
            + [block] * (1 + len(from_left) + len(from_right))
            + [piece] * len(pieces),
            out_specs=(
                pl.BlockSpec((2, wide, rows * space), lambda i, at: (0, i, 0)),
                pl.BlockSpec((2, rows * space // height, height, wide), lambda i, at: (0, 0, 0, i)),
                pl.BlockSpec((chip, wide), lambda i, at: (0, i)),
                pl.BlockSpec((rows, height, wide), lambda i, at: (0, 0, i)),
            ),
            scratch_shapes=[
                pltpu.VMEM((rows * space, coefs[0].shape[1]), BF16),
                pltpu.VMEM((rows * space, wide), F32),
            ],
        ),
        out_shape=(
            jax.ShapeDtypeStruct((2, width, rows * space), BF16),
            jax.ShapeDtypeStruct((2, rows * space // height, height, width), BF16),
            jax.ShapeDtypeStruct((chip, width), F32),
            jax.ShapeDtypeStruct((rows, height, width), F32),
        ),
        compiler_params=pltpu.CompilerParams(vmem_limit_bytes=VMEM_LIMIT),
        name="early",
    )(part[None].astype(jnp.int32), components, col_comps, *coefs, held, *from_left, *from_right, *pieces)


def early_kernel_at(rows, near, part_ref, *refs):
    early_kernel(rows, near, *refs)


def late_kernel(rows, group_ref, row_fit, col_fit, left_ref, right_ref, next_ref, piece_ref, *refs):
    row_out, col_out, block, sem = refs[2:]
    plane = lax.axis_index("cols") // (lax.axis_size("cols") // rows)
    step = pl.program_id(0)

    @pl.when((step == 0) & (plane == 0))
    def _():
        pltpu.make_async_copy(right_ref, block, sem).start()

    @pl.when((step == 0) & (plane == rows - 1))
    def _():
        pltpu.make_async_copy(left_ref, block, sem).start()

    @pl.when((step == 0) & (plane > 0) & (plane < rows - 1))
    def _():
        pltpu.make_async_copy(next_ref, block, sem).start()

    resid, sdev = weigh(col_fit[0], *parted(piece_ref[0], 1))
    col_out[0, 0] = resid
    col_out[1, 0] = sdev

    @pl.when(step == rows - 1)
    def _():
        pltpu.make_async_copy(next_ref, block, sem).wait()
        resid, sdev = weigh(row_fit[...], *parted(block[...], rows))
        chip = row_fit.shape[0]
        if row_out.shape[2] != chip:
            row_out[...] = jnp.zeros(row_out.shape, BF16)
        row_out[0, :, 0:chip] = resid.T
        row_out[1, :, 0:chip] = sdev.T


def late_call(rows, groups, row_fit, col_fit, left, right, following, piece, row_panel, col_panel):
    chip, width = row_fit.shape
    height = chip // rows
    space = row_panel.shape[2] // rows
    anywhere = pl.BlockSpec(memory_space=pl.ANY)
    return pl.pallas_call(
        functools.partial(late_kernel, rows),
        grid_spec=pltpu.PrefetchScalarGridSpec(
            num_scalar_prefetch=1,
            grid=(rows,),
            in_specs=[
                pl.BlockSpec((chip, width), lambda e, at: (0, 0)),
                pl.BlockSpec((1, height, width), lambda e, at: (e, 0, 0)),
                anywhere,
                anywhere,
                anywhere,
                pl.BlockSpec((1, 2 * height, width), lambda e, at: (e, 0, 0)),
                anywhere,
                anywhere,
            ],
            out_specs=(
                pl.BlockSpec((2, width, space), lambda e, at: (0, 0, rows - 1)),
                pl.BlockSpec((2, 1, height, width), lambda e, at: (0, at[e], 0, 0)),
            ),
            scratch_shapes=[pltpu.VMEM((2 * chip, width), BF16), pltpu.SemaphoreType.DMA],
        ),
        out_shape=(
            jax.ShapeDtypeStruct(row_panel.shape, BF16),
            jax.ShapeDtypeStruct(col_panel.shape, BF16),
        ),
        input_output_aliases={7: 0, 8: 1},
        compiler_params=pltpu.CompilerParams(vmem_limit_bytes=VMEM_LIMIT),
        name="late",
    )(groups, row_fit, col_fit, left, right, following, piece, row_panel, col_panel)


def quotient(numer, denom):
    inverse = pl.reciprocal(denom, approx=True)
    return numer * (inverse * (2.0 - denom * inverse))


def kin_kernel(part_ref, row_ref, col_ref, *refs):
    out_ref = refs[-1]
    count = out_ref.shape[0]
    step = 512 if count % 512 == 0 else count
    for at in range(0, count, step):
        span = slice(at, at + step)
        numer = jnp.dot(row_ref[0, span, :], col_ref[0], preferred_element_type=F32)
        denom = jnp.dot(row_ref[1, span, :], col_ref[1], preferred_element_type=F32)
        out_ref[span, :] = quotient(numer, denom)


def kin_call(part, people, row_panel, col_panel, before):
    _, count, depth = row_panel.shape
    width = col_panel.shape[2]
    wide = 256 if width % 256 == 0 else width
    in_specs = [
        pl.BlockSpec((2, count, depth), lambda i, at: (0, 0, 0)),
        pl.BlockSpec((2, depth, wide), lambda i, at: (0, 0, i)),
    ]
    operands = [row_panel, col_panel]
    aliases = {}
    if before is not None:
        in_specs.append(pl.BlockSpec(memory_space=pl.ANY))
        operands.append(before)
        aliases = {len(operands): 0}
    return pl.pallas_call(
        kin_kernel,
        grid_spec=pltpu.PrefetchScalarGridSpec(
            num_scalar_prefetch=1,
            grid=(width // wide,),
            in_specs=in_specs,
            out_specs=pl.BlockSpec((count, wide), lambda i, at: (at[0], i)),
        ),
        out_shape=jax.ShapeDtypeStruct((people, width), F32),
        input_output_aliases=aliases,
        compiler_params=pltpu.CompilerParams(vmem_limit_bytes=VMEM_LIMIT),
        name="kinship",
    )(part[None].astype(jnp.int32), *operands)


def per_device(dosage, present, components):
    rows, cols = lax.axis_size("rows"), lax.axis_size("cols")
    ratio = cols // rows
    markers, people = dosage.shape
    comps = components.shape[0]
    width = people // ratio
    row = lax.axis_index("rows")
    col = lax.axis_index("cols")
    core, plane = col % ratio, col // ratio

    def pairs(hop):
        moves = [(z, c, *hop(z, c)) for z in range(rows) for c in range(ratio)]
        return [(z * ratio + c, y * ratio + b) for z, c, y, b in moves if 0 <= y < rows]

    def swap(x, k):
        return lax.ppermute(x, "cols", pairs(lambda z, c: (z, (c + k) % ratio))) if k else x

    def along(x, way):
        return lax.ppermute(x, "cols", pairs(lambda z, c: (z + way, c)))

    def beside(x, d):
        return lax.ppermute(x, "rows", [(i, i ^ d) for i in range(rows)]) if d else x

    def across(x, e):
        return lax.ppermute(x, "cols", pairs(lambda z, c: (z ^ e, c))) if e else x

    def by_core(parts):
        placed = []
        for p in range(ratio):
            chosen = parts[0]
            for k in range(1, ratio):
                chosen = jnp.where((core - p) % ratio == k, parts[k], chosen)
            placed.append(chosen)
        return jnp.concatenate(placed, axis=0)

    subs = rows // ratio
    fine = markers // subs
    halves = []
    for k in range(ratio):
        begin = (core + k) % ratio * width
        both = [
            lax.dynamic_slice_in_dim(x, begin, width, 1).astype(BF16).reshape(subs, 1, fine, width)
            for x in (dosage, present)
        ]
        halves.append(swap(jnp.concatenate(both, axis=1).reshape(2 * markers, width), k))
    held = by_core(halves)
    held, dosage, present = lax.optimization_barrier((held, dosage, present))
    from_left, from_right = [along(held, 1)], [along(held, -1)]

    height = held.shape[0] // rows
    quarters = [beside(lax.dynamic_slice_in_dim(held, (row ^ d) * height, height, 0), d) for d in range(rows)]
    hops = [1 << i for i in range(rows.bit_length() - 1)]

    def doubled(x, hop):
        moves = [
            (r * cols + z * ratio + c, (r ^ hop) * cols + z * ratio + c)
            for z in range(rows)
            for r in range(rows)
            if (r ^ z) < hop
            for c in range(ratio)
        ]
        return jnp.where((row ^ plane) < hop, x, lax.ppermute(x, ("rows", "cols"), moves))

    quarters[1], dosage, present = lax.optimization_barrier((quarters[1], dosage, present))
    gram = gram_call(dosage, present, components)
    gram = gram + beside(gram, hops[0])
    col_comps = lax.dynamic_slice_in_dim(components, core * width, width, 1)
    quarters, gram, col_comps, from_left, from_right = lax.optimization_barrier(
        (jnp.stack(quarters), gram, col_comps, from_left, from_right)
    )
    moved = [
        across(lax.dynamic_index_in_dim(quarters, row ^ plane ^ e, 0, keepdims=False), e) for e in range(rows)
    ]
    for hop in hops[1:-1]:
        gram = gram + beside(gram, hop)
    grams = [gram, beside(gram, hops[-1])]
    for hop in hops:
        col_comps = doubled(col_comps, hop)
    coef = solve_call(grams, comps, markers)
    coefs = [by_core([swap(coef, k) for k in range(ratio)])]
    for hop in hops[:-1]:
        coefs.append(across(coefs[0] if len(coefs) == 1 else jnp.concatenate(coefs, axis=0), hop))
    moved, coefs, col_comps, held, from_left, from_right = lax.optimization_barrier(
        (jnp.stack(moved), coefs, col_comps, held, from_left, from_right)
    )
    coefs.append(across(jnp.concatenate(coefs, axis=0), hops[-1]))
    near = [moved]
    for step in range(rows - 3):
        from_left.append(along(from_left[-1], 1))
        from_right.append(along(from_right[-1], -1))
        upto = rows - 1 if step == rows - 4 else min(rows - 1, 2 * step + 3)
        near += [beside(moved, d) for d in range(len(near), upto)]
        near, coefs, col_comps, held, from_left, from_right = lax.optimization_barrier(
            (near, coefs, col_comps, held, from_left, from_right)
        )
    last_left, last_right = along(from_left[-1], 1), along(from_right[-1], -1)
    far = beside(near[0], rows - 1)
    row_panel, col_panel, row_fit, col_fit = early_call(
        rows, core, components, col_comps, coefs, held, from_left, from_right, near
    )
    space = row_panel.shape[2] // rows
    groups = jnp.stack(
        [
            slot_of(plane ^ e, plane, rows) * (2 * space // height) + (row ^ (rows - 1))
            for e in range(rows)
        ]
    ).astype(jnp.int32)
    row_panel, col_panel = late_call(
        rows, groups, row_fit, col_fit, last_left, last_right, from_right[0], far, row_panel, col_panel
    )
    col_panel = col_panel.reshape(2, rows * space, width)
    out = None
    for turn in range(ratio):
        out = kin_call((core + ratio - turn) % ratio, people, swap(row_panel, turn), col_panel, out)
    return out


def solution(mesh):
    placed = (P("cols", "rows"), P("cols", "rows"), P(None, "rows"))
    return jax.shard_map(
        per_device, mesh=mesh, in_specs=placed, out_specs=P("rows", "cols"), check_vma=False
    )
```

```python
import functools

import jax
import jax.numpy as jnp
from jax import lax
from jax.experimental import pallas as pl
from jax.experimental.pallas import tpu as pltpu
from jax.sharding import PartitionSpec as P

F32, BF16 = jnp.float32, jnp.bfloat16
VMEM_LIMIT = 56 * 1024 * 1024
SUB = 8


def split3(x):
    high = x.astype(BF16)
    rest = x - high.astype(F32)
    mid = rest.astype(BF16)
    low = (rest - mid.astype(F32)).astype(BF16)
    return high, mid, low


def group_starts(comps):
    starts, at = [], 0
    for j in range(comps):
        first = j // SUB * SUB
        starts.append((at, first))
        at += comps - first
    return starts, at


def gram_kernel(dosage_ref, present_ref, comps_ref, out_ref, lhs_ref):
    comps, people = comps_ref.shape
    markers = dosage_ref.shape[0]
    starts, total = group_starts(comps)
    chunk = 512 if people % 512 == 0 else people
    acc = None
    for at in range(0, people, chunk):
        span = slice(at, at + chunk)
        obs = present_ref[:, span].astype(F32)
        tgt = 0.5 * dosage_ref[:, span].astype(F32) * obs
        rhs = jnp.concatenate([obs, tgt], axis=0).astype(BF16)
        x = comps_ref[:, span]
        for j, (start, first) in enumerate(starts):
            lhs_ref[start : start + comps - first, :] = x[first:, :] * x[j : j + 1, :]
        lhs_ref[total : total + comps, :] = x
        tail = lhs_ref.shape[0] - total - comps
        lhs_ref[total + comps :, :] = jnp.ones((tail, chunk), F32)
        for part in split3(lhs_ref[...]):
            term = lax.dot_general(part, rhs, (((1,), (1,)), ((), ())), preferred_element_type=F32)
            acc = term if acc is None else acc + term
    half = total // 2
    out_ref[0:half, :] = jnp.concatenate([acc[0:half, 0:markers], acc[half:total, 0:markers]], axis=1)
    out_ref[half:, :] = acc[total : total + comps + SUB, :]


def gram_call(dosage, present, components):
    markers, people = dosage.shape
    comps = components.shape[0]
    total = group_starts(comps)[1]
    chunk = 512 if people % 512 == 0 else people
    return pl.pallas_call(
        gram_kernel,
        out_shape=jax.ShapeDtypeStruct((total // 2 + comps + SUB, 2 * markers), F32),
        scratch_shapes=[pltpu.VMEM((total + comps + 2 * SUB, chunk), F32)],
        compiler_params=pltpu.CompilerParams(vmem_limit_bytes=VMEM_LIMIT),
        name="gram",
    )(dosage, present, components)


def coef_rows(comps):
    return 4 * comps


def below(old, first, new):
    return new if first == 0 else jnp.concatenate([old[:first], new], axis=0)


def solve_kernel(comps, markers, *refs):
    out_ref = refs[-1]
    summed = refs[0][...]
    for ref in refs[1:-1]:
        summed = summed + ref[...]
    starts, total = group_starts(comps)
    half = total // 2
    left, right = summed[:, 0:markers], summed[:, markers : 2 * markers]

    def rows_of(start, count):
        if start + count <= half:
            return left[start : start + count]
        if start >= half:
            return right[start - half : start - half + count]
        return jnp.concatenate([left[start:half], right[0 : start + count - half]], axis=0)

    columns = [rows_of(start, comps - first) for start, first in starts]
    firsts = [first for _, first in starts]
    edge = left[half : half + comps]
    count = left[half + comps : half + comps + 1]
    moment = right[half : half + comps]
    moment_one = right[half + comps : half + comps + 1]
    factor, edge_f, moment_f = [], [], []
    for j in range(comps):
        first = firsts[j]
        column = columns[j]
        inv = 1.0 / column[j - first : j - first + 1]
        scaled = column * inv
        edge_j = edge[j : j + 1]
        moment_j = moment[j : j + 1]
        edge_s, moment_s = edge_j * inv, moment_j * inv
        row = lax.broadcasted_iota(jnp.int32, column.shape, 0) + first
        factor.append(jnp.where(row > j, scaled, 0.0))
        edge_f.append(edge_s)
        moment_f.append(moment_s)
        count = count - edge_s * edge_j
        moment_one = moment_one - edge_s * moment_j
        if j + 1 < comps:
            edge = below(edge, first, edge[first:] - column * edge_s)
            moment = below(moment, first, moment[first:] - column * moment_s)
        for k in range(j + 1, comps):
            offset = firsts[k] - first
            columns[k] = columns[k] - scaled[offset:] * column[k - first : k - first + 1]
    last = moment_one / count
    index = lax.broadcasted_iota(jnp.int32, (SUB, markers), 0)
    groups = [jnp.zeros((SUB, markers), F32) for _ in range(comps // SUB)]
    for j in range(comps - 1, -1, -1):
        first = firsts[j]
        value = moment_f[j] - edge_f[j] * last
        total_term = None
        for g in range(first // SUB, comps // SUB):
            term = factor[j][g * SUB - first : (g + 1) * SUB - first] * groups[g]
            total_term = term if total_term is None else total_term + term
        value = value - jnp.sum(total_term, axis=0, keepdims=True)
        g = j // SUB
        groups[g] = jnp.where(index == j - first, value, groups[g])
    coef = 2.0 * jnp.concatenate(groups, axis=0)
    last = 2.0 * last
    c1, c2, c3 = [part.astype(F32) for part in split3(coef)]
    l1, l2, l3 = [part.astype(F32) for part in split3(last)]
    index = lax.broadcasted_iota(jnp.int32, (comps, markers), 0)
    ones = jnp.where(index == 0, l1, jnp.where(index == 1, l2, jnp.where(index == 2, l3, 0.0)))
    stacked = jnp.concatenate([c1, c2, c3, ones], axis=0).astype(BF16)
    eye = (
        lax.broadcasted_iota(jnp.int32, (markers, markers), 0)
        == lax.broadcasted_iota(jnp.int32, (markers, markers), 1)
    ).astype(F32).astype(BF16)
    turned = lax.dot_general(eye, stacked, (((1,), (1,)), ((), ())), preferred_element_type=F32)
    out_ref[...] = turned.astype(BF16)


def solve_call(parts, comps, markers):
    return pl.pallas_call(
        functools.partial(solve_kernel, comps, markers),
        out_shape=jax.ShapeDtypeStruct((markers, coef_rows(comps)), BF16),
        compiler_params=pltpu.CompilerParams(vmem_limit_bytes=VMEM_LIMIT),
        name="solve",
    )(*parts)


def doubled_coef(coef):
    lanes = coef.shape[1]
    wide = coef.astype(F32)
    again = jnp.concatenate([wide[:, lanes // 2 :], wide[:, : lanes // 2]], axis=1)
    index = lax.broadcasted_iota(jnp.int32, wide.shape, 1)
    again = jnp.where(index < lanes // 2, wide, jnp.where(index < lanes // 4 * 3, again, 0.0))
    return jnp.concatenate([coef, again.astype(BF16)], axis=1)


def design_parts(x):
    d1, d2, d3 = split3(x)
    ones = jnp.ones(x.shape, BF16)
    return jnp.concatenate([d1, d1, d1, ones, d2, d2, d3, jnp.zeros(x.shape, BF16)], axis=0)


def factors(twice):
    twice = jnp.clip(twice, 0.02, 1.98)
    spread = twice * (2.0 - twice)
    return twice, spread * lax.rsqrt(spread)


def weigh(fitted, dosage, observed):
    twice, spread = factors(fitted)
    return (observed * (dosage - twice)).astype(BF16), (observed * spread).astype(BF16)


def parted(block, groups):
    block = block.astype(F32)
    height = block.shape[0] // (2 * groups)
    dosage = [block[2 * g * height : (2 * g + 1) * height] for g in range(groups)]
    present = [block[(2 * g + 1) * height : (2 * g + 2) * height] for g in range(groups)]
    if groups == 1:
        return dosage[0], present[0]
    return jnp.concatenate(dosage, axis=0), jnp.concatenate(present, axis=0)


def slot_of(source, plane, rows):
    ahead = lax.rem(source - plane + rows, rows)
    return jnp.where(lax.rem(plane, 2) == 0, ahead, lax.rem(rows - ahead, rows))


def by_even(slot, plane, rows):
    return jnp.where(lax.rem(plane, 2) == 0, plane < rows - slot, plane >= slot)


def early_kernel(rows, near, row_x_ref, col_x_ref, *refs):
    coef_refs, refs = refs[:rows], refs[rows:]
    held_ref, refs = refs[0], refs[1:]
    even, odd = refs[: rows - 2], refs[rows - 2 : 2 * rows - 4]
    piece_refs, refs = refs[2 * rows - 4 : 2 * rows - 4 + near], refs[2 * rows - 4 + near :]
    row_out, col_out, row_fit, col_fit, coef, fit = refs
    chip = coef_refs[0].shape[0]
    height = chip // rows
    space = coef.shape[0] // rows
    row = lax.axis_index("rows")
    plane = lax.axis_index("cols") // (lax.axis_size("cols") // rows)
    slots = [slot_of(plane ^ e, plane, rows) for e in range(rows)]

    @pl.when(pl.program_id(0) == 0)
    def _():
        if space != chip:
            coef[...] = jnp.zeros(coef.shape, BF16)
        for e in range(rows):
            place = pl.multiple_of(slots[e] * space, space)
            coef[pl.ds(place, chip), :] = doubled_coef(coef_refs[e][...])

    def fitted(x):
        return lax.dot_general(
            coef[...], design_parts(x), (((1,), (0,)), ((), ())), preferred_element_type=F32
        )

    if space != chip:
        row_out[...] = jnp.zeros(row_out.shape, BF16)
        col_out[...] = jnp.zeros(col_out.shape, BF16)
    fit_rows = fitted(row_x_ref[...])
    for slot in range(rows - 1):
        if slot == 0:
            block = held_ref[...]
        elif slot == 1:
            block = even[0][...]
        else:
            block = jnp.where(by_even(slot, plane, rows), even[slot - 1][...], odd[rows - slot - 1][...])
        resid, sdev = weigh(fit_rows[slot * space : slot * space + chip], *parted(block, rows))
        row_out[0, :, slot * space : slot * space + chip] = resid.T
        row_out[1, :, slot * space : slot * space + chip] = sdev.T
    row_fit[...] = fit_rows[(rows - 1) * space : (rows - 1) * space + chip]
    fit[...] = fitted(col_x_ref[...])
    for d in range(rows):
        for e in range(rows):
            place = pl.multiple_of(slots[e] * space + (row ^ d) * height, height)
            here = fit[pl.ds(place, height), :]
            if d < near:
                resid, sdev = weigh(here, *parted(piece_refs[d][e], 1))
                group = slots[e] * (space // height) + (row ^ d)
                col_out[0, group] = resid
                col_out[1, group] = sdev
            else:
                col_fit[e] = here


def early_call(rows, part, components, col_comps, coefs, held, even, odd, pieces):
    comps, width = col_comps.shape
    chip = coefs[0].shape[0]
    space = -(-chip // 128) * 128
    height = chip // rows
    wide = 256 if width % 256 == 0 else width
    whole = lambda i, at: (0, 0)
    block = pl.BlockSpec((2 * chip, wide), lambda i, at: (0, i))
    piece = pl.BlockSpec((rows, 2 * height, wide), lambda i, at: (0, 0, i))
    return pl.pallas_call(
        functools.partial(early_kernel_at, rows, len(pieces)),
        grid_spec=pltpu.PrefetchScalarGridSpec(
            num_scalar_prefetch=1,
            grid=(width // wide,),
            in_specs=[
                pl.BlockSpec((comps, wide), lambda i, at: (0, at[0] * (width // wide) + i)),
                pl.BlockSpec((comps, wide), lambda i, at: (0, i)),
            ]
            + [pl.BlockSpec(x.shape, whole) for x in coefs]
            + [block] * (1 + len(even) + len(odd))
            + [piece] * len(pieces),
            out_specs=(
                pl.BlockSpec((2, wide, rows * space), lambda i, at: (0, i, 0)),
                pl.BlockSpec((2, rows * space // height, height, wide), lambda i, at: (0, 0, 0, i)),
                pl.BlockSpec((chip, wide), lambda i, at: (0, i)),
                pl.BlockSpec((rows, height, wide), lambda i, at: (0, 0, i)),
            ),
            scratch_shapes=[
                pltpu.VMEM((rows * space, 2 * coefs[0].shape[1]), BF16),
                pltpu.VMEM((rows * space, wide), F32),
            ],
        ),
        out_shape=(
            jax.ShapeDtypeStruct((2, width, rows * space), BF16),
            jax.ShapeDtypeStruct((2, rows * space // height, height, width), BF16),
            jax.ShapeDtypeStruct((chip, width), F32),
            jax.ShapeDtypeStruct((rows, height, width), F32),
        ),
        compiler_params=pltpu.CompilerParams(vmem_limit_bytes=VMEM_LIMIT),
        name="early",
    )(part[None].astype(jnp.int32), components, col_comps, *coefs, held, *even, *odd, *pieces)


def early_kernel_at(rows, near, part_ref, *refs):
    early_kernel(rows, near, *refs)


def late_kernel(rows, group_ref, row_fit, col_fit, even_ref, odd_ref, piece_ref, *refs):
    row_out, col_out, block, sem = refs[2:]
    plane = lax.axis_index("cols") // (lax.axis_size("cols") // rows)
    step = pl.program_id(0)
    last = by_even(rows - 1, plane, rows)

    @pl.when((step == 0) & last)
    def _():
        pltpu.make_async_copy(even_ref, block, sem).start()

    @pl.when((step == 0) & jnp.logical_not(last))
    def _():
        pltpu.make_async_copy(odd_ref, block, sem).start()

    resid, sdev = weigh(col_fit[0], *parted(piece_ref[0], 1))
    col_out[0, 0] = resid
    col_out[1, 0] = sdev

    @pl.when(step == rows - 1)
    def _():
        pltpu.make_async_copy(odd_ref, block, sem).wait()
        resid, sdev = weigh(row_fit[...], *parted(block[...], rows))
        chip = row_fit.shape[0]
        if row_out.shape[2] != chip:
            row_out[...] = jnp.zeros(row_out.shape, BF16)
        row_out[0, :, 0:chip] = resid.T
        row_out[1, :, 0:chip] = sdev.T


def late_call(rows, groups, row_fit, col_fit, even, odd, piece, row_panel, col_panel):
    chip, width = row_fit.shape
    height = chip // rows
    space = row_panel.shape[2] // rows
    anywhere = pl.BlockSpec(memory_space=pl.ANY)
    return pl.pallas_call(
        functools.partial(late_kernel, rows),
        grid_spec=pltpu.PrefetchScalarGridSpec(
            num_scalar_prefetch=1,
            grid=(rows,),
            in_specs=[
                pl.BlockSpec((chip, width), lambda e, at: (0, 0)),
                pl.BlockSpec((1, height, width), lambda e, at: (e, 0, 0)),
                anywhere,
                anywhere,
                pl.BlockSpec((1, 2 * height, width), lambda e, at: (e, 0, 0)),
                anywhere,
                anywhere,
            ],
            out_specs=(
                pl.BlockSpec((2, width, space), lambda e, at: (0, 0, rows - 1)),
                pl.BlockSpec((2, 1, height, width), lambda e, at: (0, at[e], 0, 0)),
            ),
            scratch_shapes=[pltpu.VMEM((2 * chip, width), BF16), pltpu.SemaphoreType.DMA],
        ),
        out_shape=(
            jax.ShapeDtypeStruct(row_panel.shape, BF16),
            jax.ShapeDtypeStruct(col_panel.shape, BF16),
        ),
        input_output_aliases={6: 0, 7: 1},
        compiler_params=pltpu.CompilerParams(vmem_limit_bytes=VMEM_LIMIT),
        name="late",
    )(groups, row_fit, col_fit, even, odd, piece, row_panel, col_panel)


def quotient(numer, denom):
    inverse = pl.reciprocal(denom, approx=True)
    return numer * (inverse * (2.0 - denom * inverse))


def kin_kernel(part_ref, panel_ref, col_ref, *refs):
    out_ref, row_ref, sem = refs[-3:]

    @pl.when(pl.program_id(0) == 0)
    def _():
        copy = pltpu.make_async_copy(panel_ref, row_ref, sem)
        copy.start()
        copy.wait()

    numer = jnp.dot(row_ref[0], col_ref[0], preferred_element_type=F32)
    denom = jnp.dot(row_ref[1], col_ref[1], preferred_element_type=F32)
    out_ref[...] = quotient(numer, denom)


def kin_call(part, people, row_panel, col_panel, before):
    _, count, depth = row_panel.shape
    width = col_panel.shape[2]
    wide = 256 if width % 256 == 0 else width
    in_specs = [
        pl.BlockSpec(memory_space=pl.ANY),
        pl.BlockSpec((2, depth, wide), lambda i, at: (0, 0, i)),
    ]
    operands = [row_panel, col_panel]
    aliases = {}
    if before is not None:
        in_specs.append(pl.BlockSpec(memory_space=pl.ANY))
        operands.append(before)
        aliases = {len(operands): 0}
    return pl.pallas_call(
        kin_kernel,
        grid_spec=pltpu.PrefetchScalarGridSpec(
            num_scalar_prefetch=1,
            grid=(width // wide,),
            in_specs=in_specs,
            out_specs=pl.BlockSpec((count, wide), lambda i, at: (at[0], i)),
            scratch_shapes=[pltpu.VMEM(row_panel.shape, BF16), pltpu.SemaphoreType.DMA],
        ),
        out_shape=jax.ShapeDtypeStruct((people, width), F32),
        input_output_aliases=aliases,
        compiler_params=pltpu.CompilerParams(vmem_limit_bytes=VMEM_LIMIT),
        name="kinship",
    )(part[None].astype(jnp.int32), *operands)


def per_device(dosage, present, components):
    rows, cols = lax.axis_size("rows"), lax.axis_size("cols")
    ratio = cols // rows
    markers, people = dosage.shape
    comps = components.shape[0]
    width = people // ratio
    row = lax.axis_index("rows")
    col = lax.axis_index("cols")
    core, plane = col % ratio, col // ratio

    def pairs(hop):
        moves = [(z, c, *hop(z, c)) for z in range(rows) for c in range(ratio)]
        return [(z * ratio + c, y * ratio + b) for z, c, y, b in moves if 0 <= y < rows]

    def swap(x, k):
        return lax.ppermute(x, "cols", pairs(lambda z, c: (z, (c + k) % ratio))) if k else x

    def exchange(x, first):
        other = [z + 1 if (z - first) % 2 == 0 else z - 1 for z in range(rows)]
        other = [y if 0 <= y < rows else z for z, y in enumerate(other)]
        return lax.ppermute(x, "cols", pairs(lambda z, c: (other[z], c)))

    def beside(x, d):
        return lax.ppermute(x, "rows", [(i, i ^ d) for i in range(rows)]) if d else x

    def across(x, e):
        return lax.ppermute(x, "cols", pairs(lambda z, c: (z ^ e, c))) if e else x

    def by_core(parts):
        placed = []
        for p in range(ratio):
            chosen = parts[0]
            for k in range(1, ratio):
                chosen = jnp.where((core - p) % ratio == k, parts[k], chosen)
            placed.append(chosen)
        return jnp.concatenate(placed, axis=0)

    subs = rows // ratio
    fine = markers // subs
    halves = []
    for k in range(ratio):
        begin = (core + k) % ratio * width
        both = [
            lax.dynamic_slice_in_dim(x, begin, width, 1).astype(BF16).reshape(subs, 1, fine, width)
            for x in (dosage, present)
        ]
        halves.append(swap(jnp.concatenate(both, axis=1).reshape(2 * markers, width), k))
    held = by_core(halves)
    held, dosage, present = lax.optimization_barrier((held, dosage, present))
    even, odd = [exchange(held, 0)], [exchange(held, 1)]

    height = held.shape[0] // rows
    quarters = [beside(lax.dynamic_slice_in_dim(held, (row ^ d) * height, height, 0), d) for d in range(rows)]
    hops = [1 << i for i in range(rows.bit_length() - 1)]

    def doubled(x, hop):
        moves = [
            (r * cols + z * ratio + c, (r ^ hop) * cols + z * ratio + c)
            for z in range(rows)
            for r in range(rows)
            if (r ^ z) < hop
            for c in range(ratio)
        ]
        return jnp.where((row ^ plane) < hop, x, lax.ppermute(x, ("rows", "cols"), moves))

    gram = gram_call(dosage, present, components)
    col_comps = lax.dynamic_slice_in_dim(components, core * width, width, 1)
    quarters, gram, col_comps, held, even, odd = lax.optimization_barrier(
        (jnp.stack(quarters), gram, col_comps, held, even, odd)
    )
    moved = [
        across(lax.dynamic_index_in_dim(quarters, row ^ plane ^ e, 0, keepdims=False), e) for e in range(rows)
    ]
    for hop in hops[:-1]:
        gram = gram + beside(gram, hop)
    coef = solve_call([gram, beside(gram, hops[-1])], comps, markers)
    coef = by_core([swap(coef, k) for k in range(ratio)])
    col_comps = doubled(col_comps, hops[0])
    moved, coef, col_comps, held, even, odd = lax.optimization_barrier(
        (jnp.stack(moved), coef, col_comps, held, even, odd)
    )
    coefs = [across(coef, e) for e in range(rows)]
    coefs, even, odd = lax.optimization_barrier((coefs, even, odd))
    for hop in hops[1:]:
        col_comps = doubled(col_comps, hop)
    near = [moved]
    for step in range(rows - 3):
        even, odd = even + [exchange(odd[-1], 0)], odd + [exchange(even[-1], 1)]
        upto = rows - 1 if step == rows - 4 else min(rows - 1, 2 * step + 3)
        near += [beside(moved, d) for d in range(len(near), upto)]
        near, coefs, col_comps, held, even, odd = lax.optimization_barrier(
            (near, coefs, col_comps, held, even, odd)
        )
    last = exchange(odd[-1], 0)
    far = beside(near[0], rows - 1)
    row_panel, col_panel, row_fit, col_fit = early_call(
        rows, core, components, col_comps, coefs, held, even, odd, near
    )
    space = row_panel.shape[2] // rows
    groups = jnp.stack(
        [
            slot_of(plane ^ e, plane, rows) * (2 * space // height) + (row ^ (rows - 1))
            for e in range(rows)
        ]
    ).astype(jnp.int32)
    row_panel, col_panel = late_call(
        rows, groups, row_fit, col_fit, last, odd[0], far, row_panel, col_panel
    )
    col_panel = col_panel.reshape(2, rows * space, width)
    out = None
    for turn in range(ratio):
        out = kin_call((core + ratio - turn) % ratio, people, swap(row_panel, turn), col_panel, out)
    return out


def solution(mesh):
    placed = (P("cols", "rows"), P("cols", "rows"), P(None, "rows"))
    return jax.shard_map(
        per_device, mesh=mesh, in_specs=placed, out_specs=P("rows", "cols"), check_vma=False
    )
```

```python
import functools

import jax
import jax.numpy as jnp
from jax import lax
from jax.experimental import pallas as pl
from jax.experimental.pallas import tpu as pltpu
from jax.sharding import PartitionSpec as P

F32, BF16 = jnp.float32, jnp.bfloat16
VMEM_LIMIT = 56 * 1024 * 1024
SUB = 8


def split3(x):
    high = x.astype(BF16)
    rest = x - high.astype(F32)
    mid = rest.astype(BF16)
    low = (rest - mid.astype(F32)).astype(BF16)
    return high, mid, low


def group_starts(comps):
    starts, at = [], 0
    for j in range(comps):
        first = j // SUB * SUB
        starts.append((at, first))
        at += comps - first
    return starts, at


def gram_kernel(dosage_ref, present_ref, comps_ref, out_ref, lhs_ref):
    comps, people = comps_ref.shape
    markers = dosage_ref.shape[0]
    starts, total = group_starts(comps)
    chunk = 512 if people % 512 == 0 else people
    acc = None
    for at in range(0, people, chunk):
        span = slice(at, at + chunk)
        obs = present_ref[:, span].astype(F32)
        tgt = 0.5 * dosage_ref[:, span].astype(F32) * obs
        rhs = jnp.concatenate([obs, tgt], axis=0).astype(BF16)
        x = comps_ref[:, span]
        for j, (start, first) in enumerate(starts):
            lhs_ref[start : start + comps - first, :] = x[first:, :] * x[j : j + 1, :]
        lhs_ref[total : total + comps, :] = x
        tail = lhs_ref.shape[0] - total - comps
        lhs_ref[total + comps :, :] = jnp.ones((tail, chunk), F32)
        for part in split3(lhs_ref[...]):
            term = lax.dot_general(part, rhs, (((1,), (1,)), ((), ())), preferred_element_type=F32)
            acc = term if acc is None else acc + term
    half = total // 2
    out_ref[0:half, :] = jnp.concatenate([acc[0:half, 0:markers], acc[half:total, 0:markers]], axis=1)
    out_ref[half:, :] = acc[total : total + comps + SUB, :]


def gram_call(dosage, present, components):
    markers, people = dosage.shape
    comps = components.shape[0]
    total = group_starts(comps)[1]
    chunk = 512 if people % 512 == 0 else people
    return pl.pallas_call(
        gram_kernel,
        out_shape=jax.ShapeDtypeStruct((total // 2 + comps + SUB, 2 * markers), F32),
        scratch_shapes=[pltpu.VMEM((total + comps + 2 * SUB, chunk), F32)],
        compiler_params=pltpu.CompilerParams(vmem_limit_bytes=VMEM_LIMIT),
        name="gram",
    )(dosage, present, components)


def coef_rows(comps):
    return 4 * comps


def below(old, first, new):
    return new if first == 0 else jnp.concatenate([old[:first], new], axis=0)


def solve_kernel(comps, markers, *refs):
    out_ref = refs[-1]
    summed = refs[0][...]
    for ref in refs[1:-1]:
        summed = summed + ref[...]
    starts, total = group_starts(comps)
    half = total // 2
    left, right = summed[:, 0:markers], summed[:, markers : 2 * markers]

    def rows_of(start, count):
        if start + count <= half:
            return left[start : start + count]
        if start >= half:
            return right[start - half : start - half + count]
        return jnp.concatenate([left[start:half], right[0 : start + count - half]], axis=0)

    columns = [rows_of(start, comps - first) for start, first in starts]
    firsts = [first for _, first in starts]
    edge = left[half : half + comps]
    count = left[half + comps : half + comps + 1]
    moment = right[half : half + comps]
    moment_one = right[half + comps : half + comps + 1]
    factor, edge_f, moment_f = [], [], []
    for j in range(comps):
        first = firsts[j]
        column = columns[j]
        inv = 1.0 / column[j - first : j - first + 1]
        scaled = column * inv
        edge_j = edge[j : j + 1]
        moment_j = moment[j : j + 1]
        edge_s, moment_s = edge_j * inv, moment_j * inv
        row = lax.broadcasted_iota(jnp.int32, column.shape, 0) + first
        factor.append(jnp.where(row > j, scaled, 0.0))
        edge_f.append(edge_s)
        moment_f.append(moment_s)
        count = count - edge_s * edge_j
        moment_one = moment_one - edge_s * moment_j
        if j + 1 < comps:
            edge = below(edge, first, edge[first:] - column * edge_s)
            moment = below(moment, first, moment[first:] - column * moment_s)
        for k in range(j + 1, comps):
            offset = firsts[k] - first
            columns[k] = columns[k] - scaled[offset:] * column[k - first : k - first + 1]
    last = moment_one / count
    index = lax.broadcasted_iota(jnp.int32, (SUB, markers), 0)
    groups = [jnp.zeros((SUB, markers), F32) for _ in range(comps // SUB)]
    for j in range(comps - 1, -1, -1):
        first = firsts[j]
        value = moment_f[j] - edge_f[j] * last
        total_term = None
        for g in range(first // SUB, comps // SUB):
            term = factor[j][g * SUB - first : (g + 1) * SUB - first] * groups[g]
            total_term = term if total_term is None else total_term + term
        value = value - jnp.sum(total_term, axis=0, keepdims=True)
        g = j // SUB
        groups[g] = jnp.where(index == j - first, value, groups[g])
    coef = 2.0 * jnp.concatenate(groups, axis=0)
    last = 2.0 * last
    c1, c2, c3 = [part.astype(F32) for part in split3(coef)]
    l1, l2, l3 = [part.astype(F32) for part in split3(last)]
    index = lax.broadcasted_iota(jnp.int32, (comps, markers), 0)
    ones = jnp.where(index == 0, l1, jnp.where(index == 1, l2, jnp.where(index == 2, l3, 0.0)))
    stacked = jnp.concatenate([c1, c2, c3, ones], axis=0).astype(BF16)
    eye = (
        lax.broadcasted_iota(jnp.int32, (markers, markers), 0)
        == lax.broadcasted_iota(jnp.int32, (markers, markers), 1)
    ).astype(F32).astype(BF16)
    turned = lax.dot_general(eye, stacked, (((1,), (1,)), ((), ())), preferred_element_type=F32)
    out_ref[...] = turned.astype(BF16)


def solve_call(parts, comps, markers):
    return pl.pallas_call(
        functools.partial(solve_kernel, comps, markers),
        out_shape=jax.ShapeDtypeStruct((markers, coef_rows(comps)), BF16),
        compiler_params=pltpu.CompilerParams(vmem_limit_bytes=VMEM_LIMIT),
        name="solve",
    )(*parts)


def doubled_coef(coef):
    lanes = coef.shape[1]
    wide = coef.astype(F32)
    again = jnp.concatenate([wide[:, lanes // 2 :], wide[:, : lanes // 2]], axis=1)
    index = lax.broadcasted_iota(jnp.int32, wide.shape, 1)
    again = jnp.where(index < lanes // 2, wide, jnp.where(index < lanes // 4 * 3, again, 0.0))
    return jnp.concatenate([coef, again.astype(BF16)], axis=1)


def design_parts(x):
    d1, d2, d3 = split3(x)
    ones = jnp.ones(x.shape, BF16)
    return jnp.concatenate([d1, d1, d1, ones, d2, d2, d3, jnp.zeros(x.shape, BF16)], axis=0)


def factors(twice):
    twice = jnp.clip(twice, 0.02, 1.98)
    spread = twice * (2.0 - twice)
    return twice, spread * lax.rsqrt(spread)


def weigh(fitted, dosage, observed):
    twice, spread = factors(fitted)
    return observed * (dosage - twice), observed * spread


def parted(block, groups):
    block = block.astype(F32)
    height = block.shape[0] // (2 * groups)
    dosage = [block[2 * g * height : (2 * g + 1) * height] for g in range(groups)]
    present = [block[(2 * g + 1) * height : (2 * g + 2) * height] for g in range(groups)]
    if groups == 1:
        return dosage[0], present[0]
    return jnp.concatenate(dosage, axis=0), jnp.concatenate(present, axis=0)


def slot_of(source, plane, rows):
    ahead = lax.rem(source - plane + rows, rows)
    return jnp.where(lax.rem(plane, 2) == 0, ahead, lax.rem(rows - ahead, rows))


def by_even(slot, plane, rows):
    return jnp.where(lax.rem(plane, 2) == 0, plane < rows - slot, plane >= slot)


def early_kernel(rows, near, row_x_ref, col_x_ref, *refs):
    coef_refs, refs = refs[:rows], refs[rows:]
    held_ref, refs = refs[0], refs[1:]
    even, odd = refs[: rows - 2], refs[rows - 2 : 2 * rows - 4]
    piece_refs, refs = refs[2 * rows - 4 : 2 * rows - 4 + near], refs[2 * rows - 4 + near :]
    row_out, col_out, row_fit, col_fit, coef, fit = refs
    chip = coef_refs[0].shape[0]
    height = chip // rows
    space = coef.shape[0] // rows
    row = lax.axis_index("rows")
    plane = lax.axis_index("cols") // (lax.axis_size("cols") // rows)
    slots = [slot_of(plane ^ e, plane, rows) for e in range(rows)]

    @pl.when(pl.program_id(0) == 0)
    def _():
        if space != chip:
            coef[...] = jnp.zeros(coef.shape, BF16)
        for e in range(rows):
            place = pl.multiple_of(slots[e] * space, space)
            coef[pl.ds(place, chip), :] = doubled_coef(coef_refs[e][...])

    def fitted(x):
        return lax.dot_general(
            coef[...], design_parts(x), (((1,), (0,)), ((), ())), preferred_element_type=F32
        )

    if space != chip:
        row_out[...] = jnp.zeros(row_out.shape, BF16)
        col_out[...] = jnp.zeros(col_out.shape, BF16)
    fit_rows = fitted(row_x_ref[...])
    for slot in range(rows - 1):
        if slot == 0:
            block = held_ref[...]
        elif slot == 1:
            block = even[0][...]
        else:
            block = jnp.where(by_even(slot, plane, rows), even[slot - 1][...], odd[rows - slot - 1][...])
        resid, sdev = weigh(fit_rows[slot * space : slot * space + chip], *parted(block, rows))
        row_out[0, :, slot * space : slot * space + chip] = resid.astype(BF16).T
        row_out[1, :, slot * space : slot * space + chip] = sdev.astype(BF16).T
    row_fit[...] = fit_rows[(rows - 1) * space : (rows - 1) * space + chip]
    fit[...] = fitted(col_x_ref[...])
    for d in range(rows):
        for e in range(rows):
            place = pl.multiple_of(slots[e] * space + (row ^ d) * height, height)
            here = fit[pl.ds(place, height), :]
            if d < near:
                resid, sdev = weigh(here, *parted(piece_refs[d][e], 1))
                group = slots[e] * (space // height) + (row ^ d)
                col_out[0, group] = resid.astype(BF16)
                col_out[1, group] = sdev.astype(BF16)
            else:
                col_fit[e] = here


def early_call(rows, part, components, col_comps, coefs, held, even, odd, pieces):
    comps, width = col_comps.shape
    chip = coefs[0].shape[0]
    space = -(-chip // 128) * 128
    height = chip // rows
    wide = 256 if width % 256 == 0 else width
    whole = lambda i, at: (0, 0)
    block = pl.BlockSpec((2 * chip, wide), lambda i, at: (0, i))
    piece = pl.BlockSpec((rows, 2 * height, wide), lambda i, at: (0, 0, i))
    return pl.pallas_call(
        functools.partial(early_kernel_at, rows, len(pieces)),
        grid_spec=pltpu.PrefetchScalarGridSpec(
            num_scalar_prefetch=1,
            grid=(width // wide,),
            in_specs=[
                pl.BlockSpec((comps, wide), lambda i, at: (0, at[0] * (width // wide) + i)),
                pl.BlockSpec((comps, wide), lambda i, at: (0, i)),
            ]
            + [pl.BlockSpec(x.shape, whole) for x in coefs]
            + [block] * (1 + len(even) + len(odd))
            + [piece] * len(pieces),
            out_specs=(
                pl.BlockSpec((2, wide, rows * space), lambda i, at: (0, i, 0)),
                pl.BlockSpec((2, rows * space // height, height, wide), lambda i, at: (0, 0, 0, i)),
                pl.BlockSpec((chip, wide), lambda i, at: (0, i)),
                pl.BlockSpec((rows, height, wide), lambda i, at: (0, 0, i)),
            ),
            scratch_shapes=[
                pltpu.VMEM((rows * space, 2 * coefs[0].shape[1]), BF16),
                pltpu.VMEM((rows * space, wide), F32),
            ],
        ),
        out_shape=(
            jax.ShapeDtypeStruct((2, width, rows * space), BF16),
            jax.ShapeDtypeStruct((2, rows * space // height, height, width), BF16),
            jax.ShapeDtypeStruct((chip, width), F32),
            jax.ShapeDtypeStruct((rows, height, width), F32),
        ),
        compiler_params=pltpu.CompilerParams(vmem_limit_bytes=VMEM_LIMIT),
        name="early",
    )(part[None].astype(jnp.int32), components, col_comps, *coefs, held, *even, *odd, *pieces)


def early_kernel_at(rows, near, part_ref, *refs):
    early_kernel(rows, near, *refs)


def late_kernel(rows, group_ref, row_fit, col_fit, even_ref, odd_ref, piece_ref, *refs):
    row_out, col_out, block, sem = refs[2:]
    plane = lax.axis_index("cols") // (lax.axis_size("cols") // rows)
    step = pl.program_id(0)
    last = by_even(rows - 1, plane, rows)

    @pl.when((step == 0) & last)
    def _():
        pltpu.make_async_copy(even_ref, block, sem).start()

    @pl.when((step == 0) & jnp.logical_not(last))
    def _():
        pltpu.make_async_copy(odd_ref, block, sem).start()

    resid, sdev = weigh(col_fit[0], *parted(piece_ref[0], 1))
    col_out[0, 0] = resid.astype(BF16)
    col_out[1, 0] = sdev.astype(BF16)

    @pl.when(step == rows - 1)
    def _():
        pltpu.make_async_copy(odd_ref, block, sem).wait()
        resid, sdev = weigh(row_fit[...], *parted(block[...], rows))
        chip = row_fit.shape[0]
        if row_out.shape[2] != chip:
            row_out[...] = jnp.zeros(row_out.shape, BF16)
        row_out[0, :, 0:chip] = resid.T.astype(BF16)
        row_out[1, :, 0:chip] = sdev.T.astype(BF16)


def late_call(rows, groups, row_fit, col_fit, even, odd, piece, row_panel, col_panel):
    chip, width = row_fit.shape
    height = chip // rows
    space = row_panel.shape[2] // rows
    anywhere = pl.BlockSpec(memory_space=pl.ANY)
    return pl.pallas_call(
        functools.partial(late_kernel, rows),
        grid_spec=pltpu.PrefetchScalarGridSpec(
            num_scalar_prefetch=1,
            grid=(rows,),
            in_specs=[
                pl.BlockSpec((chip, width), lambda e, at: (0, 0)),
                pl.BlockSpec((1, height, width), lambda e, at: (e, 0, 0)),
                anywhere,
                anywhere,
                pl.BlockSpec((1, 2 * height, width), lambda e, at: (e, 0, 0)),
                anywhere,
                anywhere,
            ],
            out_specs=(
                pl.BlockSpec((2, width, space), lambda e, at: (0, 0, rows - 1)),
                pl.BlockSpec((2, 1, height, width), lambda e, at: (0, at[e], 0, 0)),
            ),
            scratch_shapes=[pltpu.VMEM((2 * chip, width), BF16), pltpu.SemaphoreType.DMA],
        ),
        out_shape=(
            jax.ShapeDtypeStruct(row_panel.shape, BF16),
            jax.ShapeDtypeStruct(col_panel.shape, BF16),
        ),
        input_output_aliases={6: 0, 7: 1},
        compiler_params=pltpu.CompilerParams(vmem_limit_bytes=VMEM_LIMIT),
        name="late",
    )(groups, row_fit, col_fit, even, odd, piece, row_panel, col_panel)


def quotient(numer, denom):
    inverse = pl.reciprocal(denom, approx=True)
    return numer * (inverse * (2.0 - denom * inverse))


def kin_kernel(part_ref, row_ref, col_ref, *refs):
    out_ref = refs[-1]
    numer = jnp.dot(row_ref[0], col_ref[0], preferred_element_type=F32)
    denom = jnp.dot(row_ref[1], col_ref[1], preferred_element_type=F32)
    out_ref[...] = quotient(numer, denom)


def kin_call(part, people, row_panel, col_panel, before):
    _, count, depth = row_panel.shape
    width = col_panel.shape[2]
    wide = 512 if width % 512 == 0 else width
    in_specs = [
        pl.BlockSpec((2, count, depth), lambda i, at: (0, 0, 0)),
        pl.BlockSpec((2, depth, wide), lambda i, at: (0, 0, i)),
    ]
    operands = [row_panel, col_panel]
    aliases = {}
    if before is not None:
        in_specs.append(pl.BlockSpec(memory_space=pl.ANY))
        operands.append(before)
        aliases = {len(operands): 0}
    return pl.pallas_call(
        kin_kernel,
        grid_spec=pltpu.PrefetchScalarGridSpec(
            num_scalar_prefetch=1,
            grid=(width // wide,),
            in_specs=in_specs,
            out_specs=pl.BlockSpec((count, wide), lambda i, at: (at[0], i)),
        ),
        out_shape=jax.ShapeDtypeStruct((people, width), F32),
        input_output_aliases=aliases,
        compiler_params=pltpu.CompilerParams(vmem_limit_bytes=VMEM_LIMIT),
        name="kinship",
    )(part[None].astype(jnp.int32), *operands)


def per_device(dosage, present, components):
    rows, cols = lax.axis_size("rows"), lax.axis_size("cols")
    ratio = cols // rows
    markers, people = dosage.shape
    comps = components.shape[0]
    width = people // ratio
    row = lax.axis_index("rows")
    col = lax.axis_index("cols")
    core, plane = col % ratio, col // ratio

    def pairs(hop):
        moves = [(z, c, *hop(z, c)) for z in range(rows) for c in range(ratio)]
        return [(z * ratio + c, y * ratio + b) for z, c, y, b in moves if 0 <= y < rows]

    def swap(x, k):
        return lax.ppermute(x, "cols", pairs(lambda z, c: (z, (c + k) % ratio))) if k else x

    def exchange(x, first):
        other = [z + 1 if (z - first) % 2 == 0 else z - 1 for z in range(rows)]
        other = [y if 0 <= y < rows else z for z, y in enumerate(other)]
        return lax.ppermute(x, "cols", pairs(lambda z, c: (other[z], c)))

    def beside(x, d):
        return lax.ppermute(x, "rows", [(i, i ^ d) for i in range(rows)]) if d else x

    def across(x, e):
        return lax.ppermute(x, "cols", pairs(lambda z, c: (z ^ e, c))) if e else x

    def by_core(parts):
        placed = []
        for p in range(ratio):
            chosen = parts[0]
            for k in range(1, ratio):
                chosen = jnp.where((core - p) % ratio == k, parts[k], chosen)
            placed.append(chosen)
        return jnp.concatenate(placed, axis=0)

    subs = rows // ratio
    fine = markers // subs
    halves = []
    for k in range(ratio):
        begin = (core + k) % ratio * width
        both = [
            lax.dynamic_slice_in_dim(x, begin, width, 1).astype(BF16).reshape(subs, 1, fine, width)
            for x in (dosage, present)
        ]
        halves.append(swap(jnp.concatenate(both, axis=1).reshape(2 * markers, width), k))
    held = by_core(halves)
    held, dosage, present = lax.optimization_barrier((held, dosage, present))
    odd = [exchange(held, 1)]
    even = [exchange(held, 0)]

    height = held.shape[0] // rows
    quarters = [beside(lax.dynamic_slice_in_dim(held, (row ^ d) * height, height, 0), d) for d in range(rows)]
    hops = [1 << i for i in range(rows.bit_length() - 1)]

    def doubled(x, hop):
        moves = [
            (r * cols + z * ratio + c, (r ^ hop) * cols + z * ratio + c)
            for z in range(rows)
            for r in range(rows)
            if (r ^ z) < hop
            for c in range(ratio)
        ]
        return jnp.where((row ^ plane) < hop, x, lax.ppermute(x, ("rows", "cols"), moves))

    gram = gram_call(dosage, present, components)
    quarters, gram = lax.optimization_barrier((quarters, gram))
    gram = gram + beside(gram, hops[0])
    col_comps = lax.dynamic_slice_in_dim(components, core * width, width, 1)
    quarters, gram, col_comps, held, odd, even = lax.optimization_barrier(
        (jnp.stack(quarters), gram, col_comps, held, odd, even)
    )
    moved = [
        across(lax.dynamic_index_in_dim(quarters, row ^ plane ^ e, 0, keepdims=False), e) for e in range(rows)
    ]
    for hop in hops[1:-1]:
        gram = gram + beside(gram, hop)
    coef = solve_call([gram, beside(gram, hops[-1])], comps, markers)
    coef = by_core([swap(coef, k) for k in range(ratio)])
    col_comps = doubled(col_comps, hops[0])
    moved, coef, col_comps, held, odd, even = lax.optimization_barrier(
        (jnp.stack(moved), coef, col_comps, held, odd, even)
    )
    coefs = [across(coef, e) for e in range(rows)]
    coefs, even, odd = lax.optimization_barrier((coefs, even, odd))
    for hop in hops[1:]:
        col_comps = doubled(col_comps, hop)
    near = [moved]
    for step in range(rows - 3):
        odd, even = odd + [exchange(even[-1], 1)], even + [exchange(odd[-1], 0)]
        upto = rows - 1 if step == rows - 4 else min(rows - 1, 2 * step + 3)
        near += [beside(moved, d) for d in range(len(near), upto)]
        near, coefs, col_comps, held, odd, even = lax.optimization_barrier(
            (near, coefs, col_comps, held, odd, even)
        )
    last = exchange(odd[-1], 0)
    far = beside(near[0], rows - 1)
    row_panel, col_panel, row_fit, col_fit = early_call(
        rows, core, components, col_comps, coefs, held, even, odd, near
    )
    space = row_panel.shape[2] // rows
    groups = jnp.stack(
        [
            slot_of(plane ^ e, plane, rows) * (2 * space // height) + (row ^ (rows - 1))
            for e in range(rows)
        ]
    ).astype(jnp.int32)
    row_panel, col_panel = late_call(
        rows, groups, row_fit, col_fit, last, odd[0], far, row_panel, col_panel
    )
    col_panel = col_panel.reshape(2, rows * space, width)
    out = None
    for turn in range(ratio):
        out = kin_call((core + ratio - turn) % ratio, people, swap(row_panel, turn), col_panel, out)
    return out


def solution(mesh):
    placed = (P("cols", "rows"), P("cols", "rows"), P(None, "rows"))
    return jax.shard_map(
        per_device, mesh=mesh, in_specs=placed, out_specs=P("rows", "cols"), check_vma=False
    )
```

```python
import functools

import jax
import jax.numpy as jnp
from jax import lax
from jax.experimental import pallas as pl
from jax.experimental.pallas import tpu as pltpu
from jax.sharding import PartitionSpec as P

F32, BF16 = jnp.float32, jnp.bfloat16
VMEM_LIMIT = 56 * 1024 * 1024
VMEM_ALL = 63 * 1024 * 1024
SUB = 8


def split3(x):
    high = x.astype(BF16)
    rest = x - high.astype(F32)
    mid = rest.astype(BF16)
    low = (rest - mid.astype(F32)).astype(BF16)
    return high, mid, low


def group_starts(comps):
    starts, at = [], 0
    for j in range(comps):
        first = j // SUB * SUB
        starts.append((at, first))
        at += comps - first
    return starts, at


def gram_kernel(dosage_ref, present_ref, comps_ref, out_ref, lhs_ref):
    comps, people = comps_ref.shape
    markers = dosage_ref.shape[0]
    starts, total = group_starts(comps)
    chunk = 512 if people % 512 == 0 else people
    acc = None
    for at in range(0, people, chunk):
        span = slice(at, at + chunk)
        obs = present_ref[:, span].astype(F32)
        tgt = 0.5 * dosage_ref[:, span].astype(F32) * obs
        rhs = jnp.concatenate([obs, tgt], axis=0).astype(BF16)
        x = comps_ref[:, span]
        for j, (start, first) in enumerate(starts):
            lhs_ref[start : start + comps - first, :] = x[first:, :] * x[j : j + 1, :]
        lhs_ref[total : total + comps, :] = x
        tail = lhs_ref.shape[0] - total - comps
        lhs_ref[total + comps :, :] = jnp.ones((tail, chunk), F32)
        for part in split3(lhs_ref[...]):
            term = lax.dot_general(part, rhs, (((1,), (1,)), ((), ())), preferred_element_type=F32)
            acc = term if acc is None else acc + term
    half = total // 2
    out_ref[0:half, :] = jnp.concatenate([acc[0:half, 0:markers], acc[half:total, 0:markers]], axis=1)
    out_ref[half:, :] = acc[total : total + comps + SUB, :]


def gram_call(dosage, present, components):
    markers, people = dosage.shape
    comps = components.shape[0]
    total = group_starts(comps)[1]
    chunk = 512 if people % 512 == 0 else people
    return pl.pallas_call(
        gram_kernel,
        out_shape=jax.ShapeDtypeStruct((total // 2 + comps + SUB, 2 * markers), F32),
        scratch_shapes=[pltpu.VMEM((total + comps + 2 * SUB, chunk), F32)],
        compiler_params=pltpu.CompilerParams(vmem_limit_bytes=VMEM_LIMIT),
        name="gram",
    )(dosage, present, components)


def coef_rows(comps):
    return 4 * comps


def below(old, first, new):
    return new if first == 0 else jnp.concatenate([old[:first], new], axis=0)


def solve_kernel(comps, markers, *refs):
    out_ref = refs[-1]
    summed = refs[0][...]
    for ref in refs[1:-1]:
        summed = summed + ref[...]
    starts, total = group_starts(comps)
    half = total // 2
    left, right = summed[:, 0:markers], summed[:, markers : 2 * markers]

    def rows_of(start, count):
        if start + count <= half:
            return left[start : start + count]
        if start >= half:
            return right[start - half : start - half + count]
        return jnp.concatenate([left[start:half], right[0 : start + count - half]], axis=0)

    columns = [rows_of(start, comps - first) for start, first in starts]
    firsts = [first for _, first in starts]
    edge = left[half : half + comps]
    count = left[half + comps : half + comps + 1]
    moment = right[half : half + comps]
    moment_one = right[half + comps : half + comps + 1]
    factor, edge_f, moment_f = [], [], []
    for j in range(comps):
        first = firsts[j]
        column = columns[j]
        inv = 1.0 / column[j - first : j - first + 1]
        scaled = column * inv
        edge_j = edge[j : j + 1]
        moment_j = moment[j : j + 1]
        edge_s, moment_s = edge_j * inv, moment_j * inv
        row = lax.broadcasted_iota(jnp.int32, column.shape, 0) + first
        factor.append(jnp.where(row > j, scaled, 0.0))
        edge_f.append(edge_s)
        moment_f.append(moment_s)
        count = count - edge_s * edge_j
        moment_one = moment_one - edge_s * moment_j
        if j + 1 < comps:
            edge = below(edge, first, edge[first:] - column * edge_s)
            moment = below(moment, first, moment[first:] - column * moment_s)
        for k in range(j + 1, comps):
            offset = firsts[k] - first
            columns[k] = columns[k] - scaled[offset:] * column[k - first : k - first + 1]
    last = moment_one / count
    index = lax.broadcasted_iota(jnp.int32, (SUB, markers), 0)
    groups = [jnp.zeros((SUB, markers), F32) for _ in range(comps // SUB)]
    for j in range(comps - 1, -1, -1):
        first = firsts[j]
        value = moment_f[j] - edge_f[j] * last
        total_term = None
        for g in range(first // SUB, comps // SUB):
            term = factor[j][g * SUB - first : (g + 1) * SUB - first] * groups[g]
            total_term = term if total_term is None else total_term + term
        value = value - jnp.sum(total_term, axis=0, keepdims=True)
        g = j // SUB
        groups[g] = jnp.where(index == j - first, value, groups[g])
    coef = 2.0 * jnp.concatenate(groups, axis=0)
    last = 2.0 * last
    c1, c2, c3 = [part.astype(F32) for part in split3(coef)]
    l1, l2, l3 = [part.astype(F32) for part in split3(last)]
    index = lax.broadcasted_iota(jnp.int32, (comps, markers), 0)
    ones = jnp.where(index == 0, l1, jnp.where(index == 1, l2, jnp.where(index == 2, l3, 0.0)))
    stacked = jnp.concatenate([c1, c2, c3, ones], axis=0).astype(BF16)
    eye = (
        lax.broadcasted_iota(jnp.int32, (markers, markers), 0)
        == lax.broadcasted_iota(jnp.int32, (markers, markers), 1)
    ).astype(F32).astype(BF16)
    turned = lax.dot_general(eye, stacked, (((1,), (1,)), ((), ())), preferred_element_type=F32)
    out_ref[...] = turned.astype(BF16)


def solve_call(parts, comps, markers):
    return pl.pallas_call(
        functools.partial(solve_kernel, comps, markers),
        out_shape=jax.ShapeDtypeStruct((markers, coef_rows(comps)), BF16),
        compiler_params=pltpu.CompilerParams(vmem_limit_bytes=VMEM_LIMIT),
        name="solve",
    )(*parts)


def doubled_coef(coef):
    lanes = coef.shape[1]
    wide = coef.astype(F32)
    again = jnp.concatenate([wide[:, lanes // 2 :], wide[:, : lanes // 2]], axis=1)
    index = lax.broadcasted_iota(jnp.int32, wide.shape, 1)
    again = jnp.where(index < lanes // 2, wide, jnp.where(index < lanes // 4 * 3, again, 0.0))
    return jnp.concatenate([coef, again.astype(BF16)], axis=1)


def design_parts(x):
    d1, d2, d3 = split3(x)
    ones = jnp.ones(x.shape, BF16)
    return jnp.concatenate([d1, d1, d1, ones, d2, d2, d3, jnp.zeros(x.shape, BF16)], axis=0)


def factors(twice):
    twice = jnp.clip(twice, 0.02, 1.98)
    spread = twice * (2.0 - twice)
    return twice, spread * lax.rsqrt(spread)


def weigh(fitted, dosage, observed):
    twice, spread = factors(fitted)
    return observed * (dosage - twice), observed * spread


def parted(block, groups):
    block = block.astype(F32)
    height = block.shape[0] // (2 * groups)
    dosage = [block[2 * g * height : (2 * g + 1) * height] for g in range(groups)]
    present = [block[(2 * g + 1) * height : (2 * g + 2) * height] for g in range(groups)]
    if groups == 1:
        return dosage[0], present[0]
    return jnp.concatenate(dosage, axis=0), jnp.concatenate(present, axis=0)


def slot_of(source, plane, rows):
    ahead = lax.rem(source - plane + rows, rows)
    return jnp.where(lax.rem(plane, 2) == 0, ahead, lax.rem(rows - ahead, rows))


def by_even(slot, plane, rows):
    return jnp.where(lax.rem(plane, 2) == 0, plane < rows - slot, plane >= slot)


def early_kernel(rows, near, row_x_ref, col_x_ref, *refs):
    coef_refs, refs = refs[:rows], refs[rows:]
    held_ref, refs = refs[0], refs[1:]
    even, odd = refs[: rows - 2], refs[rows - 2 : 2 * rows - 4]
    piece_refs, refs = refs[2 * rows - 4 : 2 * rows - 4 + near], refs[2 * rows - 4 + near :]
    row_out, col_out, row_fit, col_fit, coef, fit = refs
    chip = coef_refs[0].shape[0]
    height = chip // rows
    space = coef.shape[0] // rows
    row = lax.axis_index("rows")
    plane = lax.axis_index("cols") // (lax.axis_size("cols") // rows)
    slots = [slot_of(plane ^ e, plane, rows) for e in range(rows)]

    @pl.when(pl.program_id(0) == 0)
    def _():
        if space != chip:
            coef[...] = jnp.zeros(coef.shape, BF16)
        for e in range(rows):
            place = pl.multiple_of(slots[e] * space, space)
            coef[pl.ds(place, chip), :] = doubled_coef(coef_refs[e][...])

    def fitted(x):
        return lax.dot_general(
            coef[...], design_parts(x), (((1,), (0,)), ((), ())), preferred_element_type=F32
        )

    if space != chip:
        row_out[...] = jnp.zeros(row_out.shape, BF16)
        col_out[...] = jnp.zeros(col_out.shape, BF16)
    fit_rows = fitted(row_x_ref[...])
    for slot in range(rows - 1):
        if slot == 0:
            block = held_ref[...]
        elif slot == 1:
            block = even[0][...]
        else:
            block = jnp.where(by_even(slot, plane, rows), even[slot - 1][...], odd[rows - slot - 1][...])
        resid, sdev = weigh(fit_rows[slot * space : slot * space + chip], *parted(block, rows))
        row_out[0, :, slot * space : slot * space + chip] = resid.astype(BF16).T
        row_out[1, :, slot * space : slot * space + chip] = sdev.astype(BF16).T
    row_fit[...] = fit_rows[(rows - 1) * space : (rows - 1) * space + chip]
    fit[...] = fitted(col_x_ref[...])
    for d in range(rows):
        for e in range(rows):
            place = pl.multiple_of(slots[e] * space + (row ^ d) * height, height)
            here = fit[pl.ds(place, height), :]
            if d < near:
                resid, sdev = weigh(here, *parted(piece_refs[d][e], 1))
                group = slots[e] * (space // height) + (row ^ d)
                col_out[0, group] = resid.astype(BF16)
                col_out[1, group] = sdev.astype(BF16)
            else:
                col_fit[e] = here


def early_call(rows, part, components, col_comps, coefs, held, even, odd, pieces):
    comps, width = col_comps.shape
    chip = coefs[0].shape[0]
    space = -(-chip // 128) * 128
    height = chip // rows
    wide = 256 if width % 256 == 0 else width
    whole = lambda i, at: (0, 0)
    block = pl.BlockSpec((2 * chip, wide), lambda i, at: (0, i))
    piece = pl.BlockSpec((rows, 2 * height, wide), lambda i, at: (0, 0, i))
    return pl.pallas_call(
        functools.partial(early_kernel_at, rows, len(pieces)),
        grid_spec=pltpu.PrefetchScalarGridSpec(
            num_scalar_prefetch=1,
            grid=(width // wide,),
            in_specs=[
                pl.BlockSpec((comps, wide), lambda i, at: (0, at[0] * (width // wide) + i)),
                pl.BlockSpec((comps, wide), lambda i, at: (0, i)),
            ]
            + [pl.BlockSpec(x.shape, whole) for x in coefs]
            + [block] * (1 + len(even) + len(odd))
            + [piece] * len(pieces),
            out_specs=(
                pl.BlockSpec((2, wide, rows * space), lambda i, at: (0, i, 0)),
                pl.BlockSpec((2, rows * space // height, height, wide), lambda i, at: (0, 0, 0, i)),
                pl.BlockSpec((chip, wide), lambda i, at: (0, i)),
                pl.BlockSpec((rows, height, wide), lambda i, at: (0, 0, i)),
            ),
            scratch_shapes=[
                pltpu.VMEM((rows * space, 2 * coefs[0].shape[1]), BF16),
                pltpu.VMEM((rows * space, wide), F32),
            ],
        ),
        out_shape=(
            jax.ShapeDtypeStruct((2, width, rows * space), BF16),
            jax.ShapeDtypeStruct((2, rows * space // height, height, width), BF16),
            jax.ShapeDtypeStruct((chip, width), F32),
            jax.ShapeDtypeStruct((rows, height, width), F32),
        ),
        compiler_params=pltpu.CompilerParams(vmem_limit_bytes=VMEM_ALL),
        name="early",
    )(part[None].astype(jnp.int32), components, col_comps, *coefs, held, *even, *odd, *pieces)


def early_kernel_at(rows, near, part_ref, *refs):
    early_kernel(rows, near, *refs)


def late_kernel(rows, group_ref, row_fit, col_fit, even_ref, odd_ref, piece_ref, *refs):
    row_out, col_out, block, sem = refs[2:]
    plane = lax.axis_index("cols") // (lax.axis_size("cols") // rows)
    step = pl.program_id(0)
    last = by_even(rows - 1, plane, rows)

    @pl.when((step == 0) & last)
    def _():
        pltpu.make_async_copy(even_ref, block, sem).start()

    @pl.when((step == 0) & jnp.logical_not(last))
    def _():
        pltpu.make_async_copy(odd_ref, block, sem).start()

    resid, sdev = weigh(col_fit[0], *parted(piece_ref[0], 1))
    col_out[0, 0] = resid.astype(BF16)
    col_out[1, 0] = sdev.astype(BF16)

    @pl.when(step == rows - 1)
    def _():
        pltpu.make_async_copy(odd_ref, block, sem).wait()
        resid, sdev = weigh(row_fit[...], *parted(block[...], rows))
        chip = row_fit.shape[0]
        if row_out.shape[2] != chip:
            row_out[...] = jnp.zeros(row_out.shape, BF16)
        row_out[0, :, 0:chip] = resid.T.astype(BF16)
        row_out[1, :, 0:chip] = sdev.T.astype(BF16)


def late_call(rows, groups, row_fit, col_fit, even, odd, piece, row_panel, col_panel):
    chip, width = row_fit.shape
    height = chip // rows
    space = row_panel.shape[2] // rows
    anywhere = pl.BlockSpec(memory_space=pl.ANY)
    return pl.pallas_call(
        functools.partial(late_kernel, rows),
        grid_spec=pltpu.PrefetchScalarGridSpec(
            num_scalar_prefetch=1,
            grid=(rows,),
            in_specs=[
                pl.BlockSpec((chip, width), lambda e, at: (0, 0)),
                pl.BlockSpec((1, height, width), lambda e, at: (e, 0, 0)),
                anywhere,
                anywhere,
                pl.BlockSpec((1, 2 * height, width), lambda e, at: (e, 0, 0)),
                anywhere,
                anywhere,
            ],
            out_specs=(
                pl.BlockSpec((2, width, space), lambda e, at: (0, 0, rows - 1)),
                pl.BlockSpec((2, 1, height, width), lambda e, at: (0, at[e], 0, 0)),
            ),
            scratch_shapes=[pltpu.VMEM((2 * chip, width), BF16), pltpu.SemaphoreType.DMA],
        ),
        out_shape=(
            jax.ShapeDtypeStruct(row_panel.shape, BF16),
            jax.ShapeDtypeStruct(col_panel.shape, BF16),
        ),
        input_output_aliases={6: 0, 7: 1},
        compiler_params=pltpu.CompilerParams(vmem_limit_bytes=VMEM_ALL),
        name="late",
    )(groups, row_fit, col_fit, even, odd, piece, row_panel, col_panel)


def quotient(numer, denom):
    inverse = pl.reciprocal(denom, approx=True)
    return numer * (inverse * (2.0 - denom * inverse))


def kin_kernel(part_ref, row_ref, col_ref, *refs):
    out_ref = refs[-1]
    numer = jnp.dot(row_ref[0], col_ref[0], preferred_element_type=F32)
    denom = jnp.dot(row_ref[1], col_ref[1], preferred_element_type=F32)
    out_ref[...] = quotient(numer, denom)


def kin_call(part, people, row_panel, col_panel, before):
    _, count, depth = row_panel.shape
    width = col_panel.shape[2]
    wide = 512 if width % 512 == 0 else width
    in_specs = [
        pl.BlockSpec((2, count, depth), lambda i, at: (0, 0, 0)),
        pl.BlockSpec((2, depth, wide), lambda i, at: (0, 0, i)),
    ]
    operands = [row_panel, col_panel]
    aliases = {}
    if before is not None:
        in_specs.append(pl.BlockSpec(memory_space=pl.ANY))
        operands.append(before)
        aliases = {len(operands): 0}
    return pl.pallas_call(
        kin_kernel,
        grid_spec=pltpu.PrefetchScalarGridSpec(
            num_scalar_prefetch=1,
            grid=(width // wide,),
            in_specs=in_specs,
            out_specs=pl.BlockSpec((count, wide), lambda i, at: (at[0], i)),
        ),
        out_shape=jax.ShapeDtypeStruct((people, width), F32),
        input_output_aliases=aliases,
        compiler_params=pltpu.CompilerParams(vmem_limit_bytes=VMEM_ALL),
        name="kinship",
    )(part[None].astype(jnp.int32), *operands)


def per_device(dosage, present, components):
    rows, cols = lax.axis_size("rows"), lax.axis_size("cols")
    ratio = cols // rows
    markers, people = dosage.shape
    comps = components.shape[0]
    width = people // ratio
    row = lax.axis_index("rows")
    col = lax.axis_index("cols")
    core, plane = col % ratio, col // ratio

    def pairs(hop):
        moves = [(z, c, *hop(z, c)) for z in range(rows) for c in range(ratio)]
        return [(z * ratio + c, y * ratio + b) for z, c, y, b in moves if 0 <= y < rows]

    def swap(x, k):
        return lax.ppermute(x, "cols", pairs(lambda z, c: (z, (c + k) % ratio))) if k else x

    def exchange(x, first):
        other = [z + 1 if (z - first) % 2 == 0 else z - 1 for z in range(rows)]
        other = [y if 0 <= y < rows else z for z, y in enumerate(other)]
        return lax.ppermute(x, "cols", pairs(lambda z, c: (other[z], c)))

    def beside(x, d):
        return lax.ppermute(x, "rows", [(i, i ^ d) for i in range(rows)]) if d else x

    def across(x, e):
        return lax.ppermute(x, "cols", pairs(lambda z, c: (z ^ e, c))) if e else x

    def by_core(parts):
        placed = []
        for p in range(ratio):
            chosen = parts[0]
            for k in range(1, ratio):
                chosen = jnp.where((core - p) % ratio == k, parts[k], chosen)
            placed.append(chosen)
        return jnp.concatenate(placed, axis=0)

    subs = rows // ratio
    fine = markers // subs
    halves = []
    for k in range(ratio):
        begin = (core + k) % ratio * width
        both = [
            lax.dynamic_slice_in_dim(x, begin, width, 1).astype(BF16).reshape(subs, 1, fine, width)
            for x in (dosage, present)
        ]
        halves.append(swap(jnp.concatenate(both, axis=1).reshape(2 * markers, width), k))
    held = by_core(halves)
    held, dosage, present = lax.optimization_barrier((held, dosage, present))
    odd = [exchange(held, 1)]
    even = [exchange(held, 0)]

    height = held.shape[0] // rows
    quarters = [beside(lax.dynamic_slice_in_dim(held, (row ^ d) * height, height, 0), d) for d in range(rows)]
    hops = [1 << i for i in range(rows.bit_length() - 1)]

    def doubled(x, hop):
        moves = [
            (r * cols + z * ratio + c, (r ^ hop) * cols + z * ratio + c)
            for z in range(rows)
            for r in range(rows)
            if (r ^ z) < hop
            for c in range(ratio)
        ]
        return jnp.where((row ^ plane) < hop, x, lax.ppermute(x, ("rows", "cols"), moves))

    gram = gram_call(dosage, present, components)
    quarters, gram = lax.optimization_barrier((quarters, gram))
    gram = gram + beside(gram, hops[0])
    col_comps = lax.dynamic_slice_in_dim(components, core * width, width, 1)
    quarters, gram, col_comps, held, odd, even = lax.optimization_barrier(
        (jnp.stack(quarters), gram, col_comps, held, odd, even)
    )
    moved = [
        across(lax.dynamic_index_in_dim(quarters, row ^ plane ^ e, 0, keepdims=False), e) for e in range(rows)
    ]
    for hop in hops[1:-1]:
        gram = gram + beside(gram, hop)
    coef = solve_call([gram, beside(gram, hops[-1])], comps, markers)
    coef = by_core([swap(coef, k) for k in range(ratio)])
    col_comps = doubled(col_comps, hops[0])
    coefs = [across(coef, e) for e in range(rows)]
    moved, coefs, col_comps, held, odd, even = lax.optimization_barrier(
        (jnp.stack(moved), coefs, col_comps, held, odd, even)
    )
    for hop in hops[1:]:
        col_comps = doubled(col_comps, hop)
    near = [moved]
    for step in range(rows - 3):
        odd, even = odd + [exchange(even[-1], 1)], even + [exchange(odd[-1], 0)]
        upto = rows - 1 if step == rows - 4 else min(rows - 1, 2 * step + 3)
        near += [beside(moved, d) for d in range(len(near), upto)]
        near, coefs, col_comps, held, odd, even = lax.optimization_barrier(
            (near, coefs, col_comps, held, odd, even)
        )
    last = exchange(odd[-1], 0)
    far = beside(near[0], rows - 1)
    row_panel, col_panel, row_fit, col_fit = early_call(
        rows, core, components, col_comps, coefs, held, even, odd, near
    )
    space = row_panel.shape[2] // rows
    groups = jnp.stack(
        [
            slot_of(plane ^ e, plane, rows) * (2 * space // height) + (row ^ (rows - 1))
            for e in range(rows)
        ]
    ).astype(jnp.int32)
    row_panel, col_panel = late_call(
        rows, groups, row_fit, col_fit, last, odd[0], far, row_panel, col_panel
    )
    col_panel = col_panel.reshape(2, rows * space, width)
    out = None
    for turn in range(ratio):
        out = kin_call((core + ratio - turn) % ratio, people, swap(row_panel, turn), col_panel, out)
    return out


def solution(mesh):
    placed = (P("cols", "rows"), P("cols", "rows"), P(None, "rows"))
    return jax.shard_map(
        per_device, mesh=mesh, in_specs=placed, out_specs=P("rows", "cols"), check_vma=False
    )
```

```python
import functools

import jax
import jax.numpy as jnp
from jax import lax
from jax.experimental import pallas as pl
from jax.experimental.pallas import tpu as pltpu
from jax.sharding import PartitionSpec as P

F32, BF16 = jnp.float32, jnp.bfloat16
VMEM_LIMIT = 56 * 1024 * 1024
VMEM_ALL = 63 * 1024 * 1024
SUB = 8


def split3(x):
    high = x.astype(BF16)
    rest = x - high.astype(F32)
    mid = rest.astype(BF16)
    low = (rest - mid.astype(F32)).astype(BF16)
    return high, mid, low


def group_starts(comps):
    starts, at = [], 0
    for j in range(comps):
        first = j // SUB * SUB
        starts.append((at, first))
        at += comps - first
    return starts, at


def gram_kernel(dosage_ref, present_ref, comps_ref, out_ref, lhs_ref):
    comps, people = comps_ref.shape
    markers = dosage_ref.shape[0]
    starts, total = group_starts(comps)
    chunk = 512 if people % 512 == 0 else people
    acc = None
    for at in range(0, people, chunk):
        span = slice(at, at + chunk)
        obs = present_ref[:, span].astype(F32)
        tgt = 0.5 * dosage_ref[:, span].astype(F32) * obs
        rhs = jnp.concatenate([obs, tgt], axis=0).astype(BF16)
        x = comps_ref[:, span]
        for j, (start, first) in enumerate(starts):
            lhs_ref[start : start + comps - first, :] = x[first:, :] * x[j : j + 1, :]
        lhs_ref[total : total + comps, :] = x
        tail = lhs_ref.shape[0] - total - comps
        lhs_ref[total + comps :, :] = jnp.ones((tail, chunk), F32)
        for part in split3(lhs_ref[...]):
            term = lax.dot_general(part, rhs, (((1,), (1,)), ((), ())), preferred_element_type=F32)
            acc = term if acc is None else acc + term
    half = total // 2
    out_ref[0:half, :] = jnp.concatenate([acc[0:half, 0:markers], acc[half:total, 0:markers]], axis=1)
    out_ref[half:, :] = acc[total : total + comps + SUB, :]


def gram_call(dosage, present, components):
    markers, people = dosage.shape
    comps = components.shape[0]
    total = group_starts(comps)[1]
    chunk = 512 if people % 512 == 0 else people
    return pl.pallas_call(
        gram_kernel,
        out_shape=jax.ShapeDtypeStruct((total // 2 + comps + SUB, 2 * markers), F32),
        scratch_shapes=[pltpu.VMEM((total + comps + 2 * SUB, chunk), F32)],
        compiler_params=pltpu.CompilerParams(vmem_limit_bytes=VMEM_LIMIT),
        name="gram",
    )(dosage, present, components)


def coef_rows(comps):
    return 4 * comps


def below(old, first, new):
    return new if first == 0 else jnp.concatenate([old[:first], new], axis=0)


def solve_kernel(comps, markers, *refs):
    out_ref = refs[-1]
    summed = refs[0][...]
    for ref in refs[1:-1]:
        summed = summed + ref[...]
    starts, total = group_starts(comps)
    half = total // 2
    left, right = summed[:, 0:markers], summed[:, markers : 2 * markers]

    def rows_of(start, count):
        if start + count <= half:
            return left[start : start + count]
        if start >= half:
            return right[start - half : start - half + count]
        return jnp.concatenate([left[start:half], right[0 : start + count - half]], axis=0)

    columns = [rows_of(start, comps - first) for start, first in starts]
    firsts = [first for _, first in starts]
    edge = left[half : half + comps]
    count = left[half + comps : half + comps + 1]
    moment = right[half : half + comps]
    moment_one = right[half + comps : half + comps + 1]
    factor, edge_f, moment_f = [], [], []
    for j in range(comps):
        first = firsts[j]
        column = columns[j]
        inv = 1.0 / column[j - first : j - first + 1]
        scaled = column * inv
        edge_j = edge[j : j + 1]
        moment_j = moment[j : j + 1]
        edge_s, moment_s = edge_j * inv, moment_j * inv
        row = lax.broadcasted_iota(jnp.int32, column.shape, 0) + first
        factor.append(jnp.where(row > j, scaled, 0.0))
        edge_f.append(edge_s)
        moment_f.append(moment_s)
        count = count - edge_s * edge_j
        moment_one = moment_one - edge_s * moment_j
        if j + 1 < comps:
            edge = below(edge, first, edge[first:] - column * edge_s)
            moment = below(moment, first, moment[first:] - column * moment_s)
        for k in range(j + 1, comps):
            offset = firsts[k] - first
            columns[k] = columns[k] - scaled[offset:] * column[k - first : k - first + 1]
    last = moment_one / count
    index = lax.broadcasted_iota(jnp.int32, (SUB, markers), 0)
    groups = [jnp.zeros((SUB, markers), F32) for _ in range(comps // SUB)]
    for j in range(comps - 1, -1, -1):
        first = firsts[j]
        value = moment_f[j] - edge_f[j] * last
        total_term = None
        for g in range(first // SUB, comps // SUB):
            term = factor[j][g * SUB - first : (g + 1) * SUB - first] * groups[g]
            total_term = term if total_term is None else total_term + term
        value = value - jnp.sum(total_term, axis=0, keepdims=True)
        g = j // SUB
        groups[g] = jnp.where(index == j - first, value, groups[g])
    coef = 2.0 * jnp.concatenate(groups, axis=0)
    last = 2.0 * last
    c1, c2, c3 = [part.astype(F32) for part in split3(coef)]
    l1, l2, l3 = [part.astype(F32) for part in split3(last)]
    index = lax.broadcasted_iota(jnp.int32, (comps, markers), 0)
    ones = jnp.where(index == 0, l1, jnp.where(index == 1, l2, jnp.where(index == 2, l3, 0.0)))
    stacked = jnp.concatenate([c1, c2, c3, ones], axis=0).astype(BF16)
    eye = (
        lax.broadcasted_iota(jnp.int32, (markers, markers), 0)
        == lax.broadcasted_iota(jnp.int32, (markers, markers), 1)
    ).astype(F32).astype(BF16)
    turned = lax.dot_general(eye, stacked, (((1,), (1,)), ((), ())), preferred_element_type=F32)
    out_ref[...] = turned.astype(BF16)


def solve_call(parts, comps, markers):
    return pl.pallas_call(
        functools.partial(solve_kernel, comps, markers),
        out_shape=jax.ShapeDtypeStruct((markers, coef_rows(comps)), BF16),
        compiler_params=pltpu.CompilerParams(vmem_limit_bytes=VMEM_LIMIT),
        name="solve",
    )(*parts)


def doubled_coef(coef):
    lanes = coef.shape[1]
    wide = coef.astype(F32)
    again = jnp.concatenate([wide[:, lanes // 2 :], wide[:, : lanes // 2]], axis=1)
    index = lax.broadcasted_iota(jnp.int32, wide.shape, 1)
    again = jnp.where(index < lanes // 2, wide, jnp.where(index < lanes // 4 * 3, again, 0.0))
    return jnp.concatenate([coef, again.astype(BF16)], axis=1)


def design_parts(x):
    d1, d2, d3 = split3(x)
    ones = jnp.ones(x.shape, BF16)
    return jnp.concatenate([d1, d1, d1, ones, d2, d2, d3, jnp.zeros(x.shape, BF16)], axis=0)


def factors(twice):
    twice = jnp.clip(twice, 0.02, 1.98)
    spread = twice * (2.0 - twice)
    return twice, spread * lax.rsqrt(spread)


def weigh(fitted, dosage, observed):
    twice, spread = factors(fitted)
    return observed * (dosage - twice), observed * spread


def parted(block, groups):
    block = block.astype(F32)
    height = block.shape[0] // (2 * groups)
    dosage = [block[2 * g * height : (2 * g + 1) * height] for g in range(groups)]
    present = [block[(2 * g + 1) * height : (2 * g + 2) * height] for g in range(groups)]
    if groups == 1:
        return dosage[0], present[0]
    return jnp.concatenate(dosage, axis=0), jnp.concatenate(present, axis=0)


def slot_of(source, plane, rows):
    ahead = lax.rem(source - plane + rows, rows)
    return jnp.where(lax.rem(plane, 2) == 0, ahead, lax.rem(rows - ahead, rows))


def by_even(slot, plane, rows):
    return jnp.where(lax.rem(plane, 2) == 0, plane < rows - slot, plane >= slot)


def early_kernel(rows, near, row_x_ref, col_x_ref, *refs):
    coef_refs, refs = refs[:rows], refs[rows:]
    held_ref, refs = refs[0], refs[1:]
    even, odd = refs[: rows - 2], refs[rows - 2 : 2 * rows - 4]
    piece_refs, refs = refs[2 * rows - 4 : 2 * rows - 4 + near], refs[2 * rows - 4 + near :]
    row_out, col_out, row_fit, col_fit, coef, fit = refs
    chip = coef_refs[0].shape[0]
    height = chip // rows
    space = coef.shape[0] // rows
    row = lax.axis_index("rows")
    plane = lax.axis_index("cols") // (lax.axis_size("cols") // rows)
    slots = [slot_of(plane ^ e, plane, rows) for e in range(rows)]

    @pl.when(pl.program_id(0) == 0)
    def _():
        if space != chip:
            coef[...] = jnp.zeros(coef.shape, BF16)
        for e in range(rows):
            place = pl.multiple_of(slots[e] * space, space)
            coef[pl.ds(place, chip), :] = doubled_coef(coef_refs[e][...])

    def fitted(x):
        return lax.dot_general(
            coef[...], design_parts(x), (((1,), (0,)), ((), ())), preferred_element_type=F32
        )

    if space != chip:
        row_out[...] = jnp.zeros(row_out.shape, BF16)
        col_out[...] = jnp.zeros(col_out.shape, BF16)
    fit_rows = fitted(row_x_ref[...])
    for slot in range(rows - 1):
        if slot == 0:
            block = held_ref[...]
        elif slot == 1:
            block = even[0][...]
        else:
            block = jnp.where(by_even(slot, plane, rows), even[slot - 1][...], odd[rows - slot - 1][...])
        resid, sdev = weigh(fit_rows[slot * space : slot * space + chip], *parted(block, rows))
        row_out[0, :, slot * space : slot * space + chip] = resid.astype(BF16).T
        row_out[1, :, slot * space : slot * space + chip] = sdev.astype(BF16).T
    row_fit[...] = fit_rows[(rows - 1) * space : (rows - 1) * space + chip]
    fit[...] = fitted(col_x_ref[...])
    for d in range(rows):
        for e in range(rows):
            place = pl.multiple_of(slots[e] * space + (row ^ d) * height, height)
            here = fit[pl.ds(place, height), :]
            if d < near:
                resid, sdev = weigh(here, *parted(piece_refs[d][e], 1))
                group = slots[e] * (space // height) + (row ^ d)
                col_out[0, group] = resid.astype(BF16)
                col_out[1, group] = sdev.astype(BF16)
            else:
                col_fit[e] = here


def early_call(rows, part, components, col_comps, coefs, held, even, odd, pieces):
    comps, width = col_comps.shape
    chip = coefs[0].shape[0]
    space = -(-chip // 128) * 128
    height = chip // rows
    wide = 256 if width % 256 == 0 else width
    whole = lambda i, at: (0, 0)
    block = pl.BlockSpec((2 * chip, wide), lambda i, at: (0, i))
    piece = pl.BlockSpec((rows, 2 * height, wide), lambda i, at: (0, 0, i))
    return pl.pallas_call(
        functools.partial(early_kernel_at, rows, len(pieces)),
        grid_spec=pltpu.PrefetchScalarGridSpec(
            num_scalar_prefetch=1,
            grid=(width // wide,),
            in_specs=[
                pl.BlockSpec((comps, wide), lambda i, at: (0, at[0] * (width // wide) + i)),
                pl.BlockSpec((comps, wide), lambda i, at: (0, i)),
            ]
            + [pl.BlockSpec(x.shape, whole) for x in coefs]
            + [block] * (1 + len(even) + len(odd))
            + [piece] * len(pieces),
            out_specs=(
                pl.BlockSpec((2, wide, rows * space), lambda i, at: (0, i, 0)),
                pl.BlockSpec((2, rows * space // height, height, wide), lambda i, at: (0, 0, 0, i)),
                pl.BlockSpec((chip, wide), lambda i, at: (0, i)),
                pl.BlockSpec((rows, height, wide), lambda i, at: (0, 0, i)),
            ),
            scratch_shapes=[
                pltpu.VMEM((rows * space, 2 * coefs[0].shape[1]), BF16),
                pltpu.VMEM((rows * space, wide), F32),
            ],
        ),
        out_shape=(
            jax.ShapeDtypeStruct((2, width, rows * space), BF16),
            jax.ShapeDtypeStruct((2, rows * space // height, height, width), BF16),
            jax.ShapeDtypeStruct((chip, width), F32),
            jax.ShapeDtypeStruct((rows, height, width), F32),
        ),
        compiler_params=pltpu.CompilerParams(vmem_limit_bytes=VMEM_ALL),
        name="early",
    )(part[None].astype(jnp.int32), components, col_comps, *coefs, held, *even, *odd, *pieces)


def early_kernel_at(rows, near, part_ref, *refs):
    early_kernel(rows, near, *refs)


def late_kernel(rows, group_ref, row_fit, col_fit, piece_ref, even_ref, odd_ref, *refs):
    row_out, col_out, block, row_part, col_part, block_sem, row_sems, col_sems = refs[2:]
    plane = lax.axis_index("cols") // (lax.axis_size("cols") // rows)
    last = by_even(rows - 1, plane, rows)

    @pl.when(last)
    def _():
        pltpu.make_async_copy(even_ref, block, block_sem).start()

    @pl.when(jnp.logical_not(last))
    def _():
        pltpu.make_async_copy(odd_ref, block, block_sem).start()

    copies = []
    for e in range(rows):
        resid, sdev = weigh(col_fit[e], *parted(piece_ref[e], 1))
        col_part[e, 0] = resid.astype(BF16)
        col_part[e, 1] = sdev.astype(BF16)
        for i in range(2):
            copies.append(
                pltpu.make_async_copy(col_part.at[e, i], col_out.at[i, group_ref[e]], col_sems.at[2 * e + i])
            )
            copies[-1].start()
    chip, width = row_fit.shape
    space = row_part.shape[2]
    if space != chip:
        row_part[...] = jnp.zeros(row_part.shape, BF16)
    pltpu.make_async_copy(odd_ref, block, block_sem).wait()
    wide = width // row_sems.shape[0]
    for at in range(0, width, wide):
        span = slice(at, at + wide)
        resid, sdev = weigh(row_fit[:, span], *parted(block[:, span], rows))
        row_part[0, span, 0:chip] = resid.astype(BF16).T
        row_part[1, span, 0:chip] = sdev.astype(BF16).T
        copies.append(
            pltpu.make_async_copy(
                row_part.at[:, span, :],
                row_out.at[:, span, (rows - 1) * space : rows * space],
                row_sems.at[at // wide],
            )
        )
        copies[-1].start()
    for copy in copies:
        copy.wait()


def late_call(rows, groups, row_fit, col_fit, even, odd, piece, row_panel, col_panel):
    chip, width = row_fit.shape
    height = chip // rows
    space = row_panel.shape[2] // rows
    wide = 256 if width % 256 == 0 else width
    anywhere = pl.BlockSpec(memory_space=pl.ANY)
    here = pl.BlockSpec(memory_space=pltpu.VMEM)
    return pl.pallas_call(
        functools.partial(late_kernel, rows),
        in_specs=[pl.BlockSpec(memory_space=pltpu.SMEM), here, here, here] + [anywhere] * 4,
        out_specs=(anywhere, anywhere),
        out_shape=(
            jax.ShapeDtypeStruct(row_panel.shape, BF16),
            jax.ShapeDtypeStruct(col_panel.shape, BF16),
        ),
        scratch_shapes=[
            pltpu.VMEM((2 * chip, width), BF16),
            pltpu.VMEM((2, width, space), BF16),
            pltpu.VMEM((rows, 2, height, width), BF16),
            pltpu.SemaphoreType.DMA,
            pltpu.SemaphoreType.DMA((width // wide,)),
            pltpu.SemaphoreType.DMA((2 * rows,)),
        ],
        input_output_aliases={6: 0, 7: 1},
        compiler_params=pltpu.CompilerParams(vmem_limit_bytes=VMEM_ALL),
        name="late",
    )(groups, row_fit, col_fit, piece, even, odd, row_panel, col_panel)


def quotient(numer, denom):
    inverse = pl.reciprocal(denom, approx=True)
    return numer * (inverse * (2.0 - denom * inverse))


def kin_kernel(part_ref, row_ref, col_ref, *refs):
    out_ref = refs[-1]
    numer = jnp.dot(row_ref[0], col_ref[0], preferred_element_type=F32)
    denom = jnp.dot(row_ref[1], col_ref[1], preferred_element_type=F32)
    out_ref[...] = quotient(numer, denom)


def kin_call(part, people, row_panel, col_panel, before):
    _, count, depth = row_panel.shape
    width = col_panel.shape[2]
    wide = 512 if width % 512 == 0 else width
    in_specs = [
        pl.BlockSpec((2, count, depth), lambda i, at: (0, 0, 0)),
        pl.BlockSpec((2, depth, wide), lambda i, at: (0, 0, i)),
    ]
    operands = [row_panel, col_panel]
    aliases = {}
    if before is not None:
        in_specs.append(pl.BlockSpec(memory_space=pl.ANY))
        operands.append(before)
        aliases = {len(operands): 0}
    return pl.pallas_call(
        kin_kernel,
        grid_spec=pltpu.PrefetchScalarGridSpec(
            num_scalar_prefetch=1,
            grid=(width // wide,),
            in_specs=in_specs,
            out_specs=pl.BlockSpec((count, wide), lambda i, at: (at[0], i)),
        ),
        out_shape=jax.ShapeDtypeStruct((people, width), F32),
        input_output_aliases=aliases,
        compiler_params=pltpu.CompilerParams(vmem_limit_bytes=VMEM_ALL),
        name="kinship",
    )(part[None].astype(jnp.int32), *operands)


def per_device(dosage, present, components):
    rows, cols = lax.axis_size("rows"), lax.axis_size("cols")
    ratio = cols // rows
    markers, people = dosage.shape
    comps = components.shape[0]
    width = people // ratio
    row = lax.axis_index("rows")
    col = lax.axis_index("cols")
    core, plane = col % ratio, col // ratio

    def pairs(hop):
        moves = [(z, c, *hop(z, c)) for z in range(rows) for c in range(ratio)]
        return [(z * ratio + c, y * ratio + b) for z, c, y, b in moves if 0 <= y < rows]

    def swap(x, k):
        return lax.ppermute(x, "cols", pairs(lambda z, c: (z, (c + k) % ratio))) if k else x

    def exchange(x, first):
        other = [z + 1 if (z - first) % 2 == 0 else z - 1 for z in range(rows)]
        other = [y if 0 <= y < rows else z for z, y in enumerate(other)]
        return lax.ppermute(x, "cols", pairs(lambda z, c: (other[z], c)))

    def beside(x, d):
        return lax.ppermute(x, "rows", [(i, i ^ d) for i in range(rows)]) if d else x

    def across(x, e):
        return lax.ppermute(x, "cols", pairs(lambda z, c: (z ^ e, c))) if e else x

    def by_core(parts):
        placed = []
        for p in range(ratio):
            chosen = parts[0]
            for k in range(1, ratio):
                chosen = jnp.where((core - p) % ratio == k, parts[k], chosen)
            placed.append(chosen)
        return jnp.concatenate(placed, axis=0)

    subs = rows // ratio
    fine = markers // subs
    halves = []
    for k in range(ratio):
        begin = (core + k) % ratio * width
        both = [
            lax.dynamic_slice_in_dim(x, begin, width, 1).astype(BF16).reshape(subs, 1, fine, width)
            for x in (dosage, present)
        ]
        halves.append(swap(jnp.concatenate(both, axis=1).reshape(2 * markers, width), k))
    held = by_core(halves)
    held, dosage, present = lax.optimization_barrier((held, dosage, present))
    odd = [exchange(held, 1)]
    even = [exchange(held, 0)]

    height = held.shape[0] // rows
    quarters = [beside(lax.dynamic_slice_in_dim(held, (row ^ d) * height, height, 0), d) for d in range(rows)]
    hops = [1 << i for i in range(rows.bit_length() - 1)]

    def doubled(x, hop):
        moves = [
            (r * cols + z * ratio + c, (r ^ hop) * cols + z * ratio + c)
            for z in range(rows)
            for r in range(rows)
            if (r ^ z) < hop
            for c in range(ratio)
        ]
        return jnp.where((row ^ plane) < hop, x, lax.ppermute(x, ("rows", "cols"), moves))

    gram = gram_call(dosage, present, components)
    col_comps = lax.dynamic_slice_in_dim(components, core * width, width, 1)
    quarters, gram, col_comps = lax.optimization_barrier((quarters, gram, col_comps))
    gram = gram + beside(gram, hops[0])
    col_comps = doubled(col_comps, hops[0])
    quarters, gram, col_comps, held, odd, even = lax.optimization_barrier(
        (jnp.stack(quarters), gram, col_comps, held, odd, even)
    )
    moved = [
        across(lax.dynamic_index_in_dim(quarters, row ^ plane ^ e, 0, keepdims=False), e) for e in range(rows)
    ]
    for hop in hops[1:-1]:
        gram = gram + beside(gram, hop)
    coef = solve_call([gram, beside(gram, hops[-1])], comps, markers)
    coef = by_core([swap(coef, k) for k in range(ratio)])
    for hop in hops[1:]:
        col_comps = doubled(col_comps, hop)
    coefs = [across(coef, e) for e in range(rows)]
    moved, coefs, col_comps, held, odd, even = lax.optimization_barrier(
        (jnp.stack(moved), coefs, col_comps, held, odd, even)
    )
    near = [moved]
    for step in range(rows - 3):
        odd, even = odd + [exchange(even[-1], 1)], even + [exchange(odd[-1], 0)]
        upto = rows - 1 if step == rows - 4 else min(rows - 1, 2 * step + 3)
        near += [beside(moved, d) for d in range(len(near), upto)]
        near, coefs, col_comps, held, odd, even = lax.optimization_barrier(
            (near, coefs, col_comps, held, odd, even)
        )
    last = exchange(odd[-1], 0)
    far = beside(near[0], rows - 1)
    row_panel, col_panel, row_fit, col_fit = early_call(
        rows, core, components, col_comps, coefs, held, even, odd, near
    )
    space = row_panel.shape[2] // rows
    groups = jnp.stack(
        [
            slot_of(plane ^ e, plane, rows) * (2 * space // height) + (row ^ (rows - 1))
            for e in range(rows)
        ]
    ).astype(jnp.int32)
    row_panel, col_panel = late_call(
        rows, groups, row_fit, col_fit, last, odd[0], far, row_panel, col_panel
    )
    col_panel = col_panel.reshape(2, rows * space, width)
    out = None
    for turn in range(ratio):
        out = kin_call((core + ratio - turn) % ratio, people, swap(row_panel, turn), col_panel, out)
    return out


def solution(mesh):
    placed = (P("cols", "rows"), P("cols", "rows"), P(None, "rows"))
    return jax.shard_map(
        per_device, mesh=mesh, in_specs=placed, out_specs=P("rows", "cols"), check_vma=False
    )
```

```python
import functools

import jax
import jax.numpy as jnp
from jax import lax
from jax.experimental import pallas as pl
from jax.experimental.pallas import tpu as pltpu
from jax.sharding import PartitionSpec as P

F32, BF16 = jnp.float32, jnp.bfloat16
VMEM_LIMIT = 56 * 1024 * 1024
VMEM_ALL = 63 * 1024 * 1024
SUB = 8


def split3(x):
    high = x.astype(BF16)
    rest = x - high.astype(F32)
    mid = rest.astype(BF16)
    low = (rest - mid.astype(F32)).astype(BF16)
    return high, mid, low


def group_starts(comps):
    starts, at = [], 0
    for j in range(comps):
        first = j // SUB * SUB
        starts.append((at, first))
        at += comps - first
    return starts, at


def gram_kernel(dosage_ref, present_ref, comps_ref, out_ref, lhs_ref):
    comps, people = comps_ref.shape
    markers = dosage_ref.shape[0]
    starts, total = group_starts(comps)
    chunk = 512 if people % 512 == 0 else people
    acc = None
    for at in range(0, people, chunk):
        span = slice(at, at + chunk)
        obs = present_ref[:, span].astype(F32)
        tgt = 0.5 * dosage_ref[:, span].astype(F32) * obs
        rhs = jnp.concatenate([obs, tgt], axis=0).astype(BF16)
        x = comps_ref[:, span]
        for j, (start, first) in enumerate(starts):
            lhs_ref[start : start + comps - first, :] = x[first:, :] * x[j : j + 1, :]
        lhs_ref[total : total + comps, :] = x
        tail = lhs_ref.shape[0] - total - comps
        lhs_ref[total + comps :, :] = jnp.ones((tail, chunk), F32)
        for part in split3(lhs_ref[...]):
            term = lax.dot_general(part, rhs, (((1,), (1,)), ((), ())), preferred_element_type=F32)
            acc = term if acc is None else acc + term
    half = total // 2
    out_ref[0:half, :] = jnp.concatenate([acc[0:half, 0:markers], acc[half:total, 0:markers]], axis=1)
    out_ref[half:, :] = acc[total : total + comps + SUB, :]


def gram_call(dosage, present, components):
    markers, people = dosage.shape
    comps = components.shape[0]
    total = group_starts(comps)[1]
    chunk = 512 if people % 512 == 0 else people
    return pl.pallas_call(
        gram_kernel,
        out_shape=jax.ShapeDtypeStruct((total // 2 + comps + SUB, 2 * markers), F32),
        scratch_shapes=[pltpu.VMEM((total + comps + 2 * SUB, chunk), F32)],
        compiler_params=pltpu.CompilerParams(vmem_limit_bytes=VMEM_LIMIT),
        name="gram",
    )(dosage, present, components)


def coef_rows(comps):
    return 4 * comps


def below(old, first, new):
    return new if first == 0 else jnp.concatenate([old[:first], new], axis=0)


def solve_kernel(comps, markers, *refs):
    out_ref = refs[-1]
    summed = refs[0][...]
    for ref in refs[1:-1]:
        summed = summed + ref[...]
    starts, total = group_starts(comps)
    half = total // 2
    left, right = summed[:, 0:markers], summed[:, markers : 2 * markers]

    def rows_of(start, count):
        if start + count <= half:
            return left[start : start + count]
        if start >= half:
            return right[start - half : start - half + count]
        return jnp.concatenate([left[start:half], right[0 : start + count - half]], axis=0)

    columns = [rows_of(start, comps - first) for start, first in starts]
    firsts = [first for _, first in starts]
    edge = left[half : half + comps]
    count = left[half + comps : half + comps + 1]
    moment = right[half : half + comps]
    moment_one = right[half + comps : half + comps + 1]
    factor, edge_f, moment_f = [], [], []
    for j in range(comps):
        first = firsts[j]
        column = columns[j]
        inv = 1.0 / column[j - first : j - first + 1]
        scaled = column * inv
        edge_j = edge[j : j + 1]
        moment_j = moment[j : j + 1]
        edge_s, moment_s = edge_j * inv, moment_j * inv
        row = lax.broadcasted_iota(jnp.int32, column.shape, 0) + first
        factor.append(jnp.where(row > j, scaled, 0.0))
        edge_f.append(edge_s)
        moment_f.append(moment_s)
        count = count - edge_s * edge_j
        moment_one = moment_one - edge_s * moment_j
        if j + 1 < comps:
            edge = below(edge, first, edge[first:] - column * edge_s)
            moment = below(moment, first, moment[first:] - column * moment_s)
        for k in range(j + 1, comps):
            offset = firsts[k] - first
            columns[k] = columns[k] - scaled[offset:] * column[k - first : k - first + 1]
    last = moment_one / count
    index = lax.broadcasted_iota(jnp.int32, (SUB, markers), 0)
    groups = [jnp.zeros((SUB, markers), F32) for _ in range(comps // SUB)]
    for j in range(comps - 1, -1, -1):
        first = firsts[j]
        value = moment_f[j] - edge_f[j] * last
        total_term = None
        for g in range(first // SUB, comps // SUB):
            term = factor[j][g * SUB - first : (g + 1) * SUB - first] * groups[g]
            total_term = term if total_term is None else total_term + term
        value = value - jnp.sum(total_term, axis=0, keepdims=True)
        g = j // SUB
        groups[g] = jnp.where(index == j - first, value, groups[g])
    coef = 2.0 * jnp.concatenate(groups, axis=0)
    last = 2.0 * last
    c1, c2, c3 = [part.astype(F32) for part in split3(coef)]
    l1, l2, l3 = [part.astype(F32) for part in split3(last)]
    index = lax.broadcasted_iota(jnp.int32, (comps, markers), 0)
    ones = jnp.where(index == 0, l1, jnp.where(index == 1, l2, jnp.where(index == 2, l3, 0.0)))
    stacked = jnp.concatenate([c1, c2, c3, ones], axis=0).astype(BF16)
    eye = (
        lax.broadcasted_iota(jnp.int32, (markers, markers), 0)
        == lax.broadcasted_iota(jnp.int32, (markers, markers), 1)
    ).astype(F32).astype(BF16)
    turned = lax.dot_general(eye, stacked, (((1,), (1,)), ((), ())), preferred_element_type=F32)
    out_ref[...] = turned.astype(BF16)


def solve_call(parts, comps, markers):
    return pl.pallas_call(
        functools.partial(solve_kernel, comps, markers),
        out_shape=jax.ShapeDtypeStruct((markers, coef_rows(comps)), BF16),
        compiler_params=pltpu.CompilerParams(vmem_limit_bytes=VMEM_LIMIT),
        name="solve",
    )(*parts)


def doubled_coef(coef):
    lanes = coef.shape[1]
    wide = coef.astype(F32)
    again = jnp.concatenate([wide[:, lanes // 2 :], wide[:, : lanes // 2]], axis=1)
    index = lax.broadcasted_iota(jnp.int32, wide.shape, 1)
    again = jnp.where(index < lanes // 2, wide, jnp.where(index < lanes // 4 * 3, again, 0.0))
    return jnp.concatenate([coef, again.astype(BF16)], axis=1)


def design_parts(x):
    d1, d2, d3 = split3(x)
    ones = jnp.ones(x.shape, BF16)
    return jnp.concatenate([d1, d1, d1, ones, d2, d2, d3, jnp.zeros(x.shape, BF16)], axis=0)


def factors(twice):
    twice = jnp.clip(twice, 0.02, 1.98)
    spread = twice * (2.0 - twice)
    return twice, spread * lax.rsqrt(spread)


def weigh(fitted, dosage, observed):
    twice, spread = factors(fitted)
    return observed * (dosage - twice), observed * spread


def parted(block, groups):
    block = block.astype(F32)
    height = block.shape[0] // (2 * groups)
    dosage = [block[2 * g * height : (2 * g + 1) * height] for g in range(groups)]
    present = [block[(2 * g + 1) * height : (2 * g + 2) * height] for g in range(groups)]
    if groups == 1:
        return dosage[0], present[0]
    return jnp.concatenate(dosage, axis=0), jnp.concatenate(present, axis=0)


def slot_of(source, plane, rows):
    ahead = lax.rem(source - plane + rows, rows)
    return jnp.where(lax.rem(plane, 2) == 0, ahead, lax.rem(rows - ahead, rows))


def by_even(slot, plane, rows):
    return jnp.where(lax.rem(plane, 2) == 0, plane < rows - slot, plane >= slot)


def early_kernel(rows, near, row_x_ref, col_x_ref, *refs):
    coef_refs, refs = refs[:rows], refs[rows:]
    held_ref, refs = refs[0], refs[1:]
    even, odd = refs[: rows - 2], refs[rows - 2 : 2 * rows - 4]
    piece_refs, refs = refs[2 * rows - 4 : 2 * rows - 4 + near], refs[2 * rows - 4 + near :]
    row_out, col_out, row_fit, col_fit, coef, fit = refs
    chip = coef_refs[0].shape[0]
    height = chip // rows
    space = coef.shape[0] // rows
    row = lax.axis_index("rows")
    plane = lax.axis_index("cols") // (lax.axis_size("cols") // rows)
    slots = [slot_of(plane ^ e, plane, rows) for e in range(rows)]

    @pl.when(pl.program_id(0) == 0)
    def _():
        if space != chip:
            coef[...] = jnp.zeros(coef.shape, BF16)
        for e in range(rows):
            place = pl.multiple_of(slots[e] * space, space)
            coef[pl.ds(place, chip), :] = doubled_coef(coef_refs[e][...])

    def fitted(x):
        return lax.dot_general(
            coef[...], design_parts(x), (((1,), (0,)), ((), ())), preferred_element_type=F32
        )

    if space != chip:
        row_out[...] = jnp.zeros(row_out.shape, BF16)
        col_out[...] = jnp.zeros(col_out.shape, BF16)
    fit_rows = fitted(row_x_ref[...])
    for slot in range(rows - 1):
        if slot == 0:
            block = held_ref[...]
        elif slot == 1:
            block = even[0][...]
        else:
            block = jnp.where(by_even(slot, plane, rows), even[slot - 1][...], odd[rows - slot - 1][...])
        resid, sdev = weigh(fit_rows[slot * space : slot * space + chip], *parted(block, rows))
        row_out[0, :, slot * space : slot * space + chip] = resid.astype(BF16).T
        row_out[1, :, slot * space : slot * space + chip] = sdev.astype(BF16).T
    row_fit[...] = fit_rows[(rows - 1) * space : (rows - 1) * space + chip]
    fit[...] = fitted(col_x_ref[...])
    for d in range(rows):
        for e in range(rows):
            place = pl.multiple_of(slots[e] * space + (row ^ d) * height, height)
            here = fit[pl.ds(place, height), :]
            if d < near:
                resid, sdev = weigh(here, *parted(piece_refs[d][e], 1))
                group = slots[e] * (space // height) + (row ^ d)
                col_out[0, group] = resid.astype(BF16)
                col_out[1, group] = sdev.astype(BF16)
            else:
                col_fit[e] = here


def early_call(rows, part, components, col_comps, coefs, held, even, odd, pieces):
    comps, width = col_comps.shape
    chip = coefs[0].shape[0]
    space = -(-chip // 128) * 128
    height = chip // rows
    wide = 256 if width % 256 == 0 else width
    whole = lambda i, at: (0, 0)
    block = pl.BlockSpec((2 * chip, wide), lambda i, at: (0, i))
    piece = pl.BlockSpec((rows, 2 * height, wide), lambda i, at: (0, 0, i))
    return pl.pallas_call(
        functools.partial(early_kernel_at, rows, len(pieces)),
        grid_spec=pltpu.PrefetchScalarGridSpec(
            num_scalar_prefetch=1,
            grid=(width // wide,),
            in_specs=[
                pl.BlockSpec((comps, wide), lambda i, at: (0, at[0] * (width // wide) + i)),
                pl.BlockSpec((comps, wide), lambda i, at: (0, i)),
            ]
            + [pl.BlockSpec(x.shape, whole) for x in coefs]
            + [block] * (1 + len(even) + len(odd))
            + [piece] * len(pieces),
            out_specs=(
                pl.BlockSpec((2, wide, rows * space), lambda i, at: (0, i, 0)),
                pl.BlockSpec((2, rows * space // height, height, wide), lambda i, at: (0, 0, 0, i)),
                pl.BlockSpec((chip, wide), lambda i, at: (0, i)),
                pl.BlockSpec((rows, height, wide), lambda i, at: (0, 0, i)),
            ),
            scratch_shapes=[
                pltpu.VMEM((rows * space, 2 * coefs[0].shape[1]), BF16),
                pltpu.VMEM((rows * space, wide), F32),
            ],
        ),
        out_shape=(
            jax.ShapeDtypeStruct((2, width, rows * space), BF16),
            jax.ShapeDtypeStruct((2, rows * space // height, height, width), BF16),
            jax.ShapeDtypeStruct((chip, width), F32),
            jax.ShapeDtypeStruct((rows, height, width), F32),
        ),
        compiler_params=pltpu.CompilerParams(vmem_limit_bytes=VMEM_ALL),
        name="early",
    )(part[None].astype(jnp.int32), components, col_comps, *coefs, held, *even, *odd, *pieces)


def early_kernel_at(rows, near, part_ref, *refs):
    early_kernel(rows, near, *refs)


def late_kernel(rows, group_ref, row_fit, col_fit, piece_ref, even_ref, odd_ref, *refs):
    row_out, col_out, block, row_part, col_part, block_sem, row_sems, col_sems = refs[2:]
    plane = lax.axis_index("cols") // (lax.axis_size("cols") // rows)
    last = by_even(rows - 1, plane, rows)

    @pl.when(last)
    def _():
        pltpu.make_async_copy(even_ref, block, block_sem).start()

    @pl.when(jnp.logical_not(last))
    def _():
        pltpu.make_async_copy(odd_ref, block, block_sem).start()

    copies = []
    for e in range(rows):
        resid, sdev = weigh(col_fit[e], *parted(piece_ref[e], 1))
        col_part[e, 0] = resid.astype(BF16)
        col_part[e, 1] = sdev.astype(BF16)
        for i in range(2):
            copies.append(
                pltpu.make_async_copy(col_part.at[e, i], col_out.at[i, group_ref[e]], col_sems.at[2 * e + i])
            )
            copies[-1].start()
    chip, width = row_fit.shape
    space = row_part.shape[2]
    if space != chip:
        row_part[...] = jnp.zeros(row_part.shape, BF16)
    pltpu.make_async_copy(odd_ref, block, block_sem).wait()
    wide = width // row_sems.shape[0]
    for at in range(0, width, wide):
        span = slice(at, at + wide)
        resid, sdev = weigh(row_fit[:, span], *parted(block[:, span], rows))
        row_part[0, span, 0:chip] = resid.astype(BF16).T
        row_part[1, span, 0:chip] = sdev.astype(BF16).T
        copies.append(
            pltpu.make_async_copy(
                row_part.at[:, span, :],
                row_out.at[:, span, (rows - 1) * space : rows * space],
                row_sems.at[at // wide],
            )
        )
        copies[-1].start()
    for copy in copies:
        copy.wait()


def late_call(rows, groups, row_fit, col_fit, even, odd, piece, row_panel, col_panel):
    chip, width = row_fit.shape
    height = chip // rows
    space = row_panel.shape[2] // rows
    wide = 256 if width % 256 == 0 else width
    anywhere = pl.BlockSpec(memory_space=pl.ANY)
    here = pl.BlockSpec(memory_space=pltpu.VMEM)
    return pl.pallas_call(
        functools.partial(late_kernel, rows),
        in_specs=[pl.BlockSpec(memory_space=pltpu.SMEM), here, here, here] + [anywhere] * 4,
        out_specs=(anywhere, anywhere),
        out_shape=(
            jax.ShapeDtypeStruct(row_panel.shape, BF16),
            jax.ShapeDtypeStruct(col_panel.shape, BF16),
        ),
        scratch_shapes=[
            pltpu.VMEM((2 * chip, width), BF16),
            pltpu.VMEM((2, width, space), BF16),
            pltpu.VMEM((rows, 2, height, width), BF16),
            pltpu.SemaphoreType.DMA,
            pltpu.SemaphoreType.DMA((width // wide,)),
            pltpu.SemaphoreType.DMA((2 * rows,)),
        ],
        input_output_aliases={6: 0, 7: 1},
        compiler_params=pltpu.CompilerParams(vmem_limit_bytes=VMEM_ALL),
        name="late",
    )(groups, row_fit, col_fit, piece, even, odd, row_panel, col_panel)


def quotient(numer, denom):
    inverse = pl.reciprocal(denom, approx=True)
    return numer * (inverse * (2.0 - denom * inverse))


def kin_kernel(part_ref, row_ref, col_ref, *refs):
    out_ref = refs[-1]
    numer = jnp.dot(row_ref[0], col_ref[0], preferred_element_type=F32)
    denom = jnp.dot(row_ref[1], col_ref[1], preferred_element_type=F32)
    out_ref[...] = quotient(numer, denom)


def kin_call(part, people, row_panel, col_panel, before):
    _, count, depth = row_panel.shape
    width = col_panel.shape[2]
    wide = 512 if width % 512 == 0 else width
    in_specs = [
        pl.BlockSpec((2, count, depth), lambda i, at: (0, 0, 0)),
        pl.BlockSpec((2, depth, wide), lambda i, at: (0, 0, i)),
    ]
    operands = [row_panel, col_panel]
    aliases = {}
    if before is not None:
        in_specs.append(pl.BlockSpec(memory_space=pl.ANY))
        operands.append(before)
        aliases = {len(operands): 0}
    return pl.pallas_call(
        kin_kernel,
        grid_spec=pltpu.PrefetchScalarGridSpec(
            num_scalar_prefetch=1,
            grid=(width // wide,),
            in_specs=in_specs,
            out_specs=pl.BlockSpec((count, wide), lambda i, at: (at[0], i)),
        ),
        out_shape=jax.ShapeDtypeStruct((people, width), F32),
        input_output_aliases=aliases,
        compiler_params=pltpu.CompilerParams(vmem_limit_bytes=VMEM_ALL),
        name="kinship",
    )(part[None].astype(jnp.int32), *operands)


def per_device(dosage, present, components):
    rows, cols = lax.axis_size("rows"), lax.axis_size("cols")
    ratio = cols // rows
    markers, people = dosage.shape
    comps = components.shape[0]
    width = people // ratio
    row = lax.axis_index("rows")
    col = lax.axis_index("cols")
    core, plane = col % ratio, col // ratio

    def pairs(hop):
        moves = [(z, c, *hop(z, c)) for z in range(rows) for c in range(ratio)]
        return [(z * ratio + c, y * ratio + b) for z, c, y, b in moves if 0 <= y < rows]

    def swap(x, k):
        return lax.ppermute(x, "cols", pairs(lambda z, c: (z, (c + k) % ratio))) if k else x

    def exchange(x, first):
        other = [z + 1 if (z - first) % 2 == 0 else z - 1 for z in range(rows)]
        other = [y if 0 <= y < rows else z for z, y in enumerate(other)]
        return lax.ppermute(x, "cols", pairs(lambda z, c: (other[z], c)))

    def beside(x, d):
        return lax.ppermute(x, "rows", [(i, i ^ d) for i in range(rows)]) if d else x

    def across(x, e):
        return lax.ppermute(x, "cols", pairs(lambda z, c: (z ^ e, c))) if e else x

    def by_core(parts):
        placed = []
        for p in range(ratio):
            chosen = parts[0]
            for k in range(1, ratio):
                chosen = jnp.where((core - p) % ratio == k, parts[k], chosen)
            placed.append(chosen)
        return jnp.concatenate(placed, axis=0)

    subs = rows // ratio
    fine = markers // subs
    halves = []
    for k in range(ratio):
        begin = (core + k) % ratio * width
        both = [
            lax.dynamic_slice_in_dim(x, begin, width, 1).astype(BF16).reshape(subs, 1, fine, width)
            for x in (dosage, present)
        ]
        halves.append(swap(jnp.concatenate(both, axis=1).reshape(2 * markers, width), k))
    held = by_core(halves)
    held, dosage, present = lax.optimization_barrier((held, dosage, present))
    odd = [exchange(held, 1)]
    even = [exchange(held, 0)]

    height = held.shape[0] // rows
    quarters = [beside(lax.dynamic_slice_in_dim(held, (row ^ d) * height, height, 0), d) for d in range(rows)]
    hops = [1 << i for i in range(rows.bit_length() - 1)]

    def doubled(x, hop):
        return jnp.where((row ^ plane) < hop, x, beside(x, hop))

    gram = gram_call(dosage, present, components)
    col_comps = lax.dynamic_slice_in_dim(components, core * width, width, 1)
    quarters, gram, col_comps = lax.optimization_barrier((quarters, gram, col_comps))
    gram = gram + beside(gram, hops[0])
    col_comps = doubled(col_comps, hops[0])
    quarters, gram, col_comps, held, odd, even = lax.optimization_barrier(
        (jnp.stack(quarters), gram, col_comps, held, odd, even)
    )
    moved = [
        across(lax.dynamic_index_in_dim(quarters, row ^ plane ^ e, 0, keepdims=False), e) for e in range(rows)
    ]
    for hop in hops[1:-1]:
        gram = gram + beside(gram, hop)
    coef = solve_call([gram, beside(gram, hops[-1])], comps, markers)
    coef = by_core([swap(coef, k) for k in range(ratio)])
    for hop in hops[1:]:
        col_comps = doubled(col_comps, hop)
    coefs = [across(coef, e) for e in range(rows)]
    moved, coefs, col_comps, held, odd, even = lax.optimization_barrier(
        (jnp.stack(moved), coefs, col_comps, held, odd, even)
    )
    near = [moved]
    for step in range(rows - 3):
        odd, even = odd + [exchange(even[-1], 1)], even + [exchange(odd[-1], 0)]
        upto = rows - 1 if step == rows - 4 else min(rows - 1, 2 * step + 3)
        near += [beside(moved, d) for d in range(len(near), upto)]
        near, coefs, col_comps, held, odd, even = lax.optimization_barrier(
            (near, coefs, col_comps, held, odd, even)
        )
    last = exchange(odd[-1], 0)
    far = beside(near[0], rows - 1)
    row_panel, col_panel, row_fit, col_fit = early_call(
        rows, core, components, col_comps, coefs, held, even, odd, near
    )
    space = row_panel.shape[2] // rows
    groups = jnp.stack(
        [
            slot_of(plane ^ e, plane, rows) * (2 * space // height) + (row ^ (rows - 1))
            for e in range(rows)
        ]
    ).astype(jnp.int32)
    row_panel, col_panel = late_call(
        rows, groups, row_fit, col_fit, last, odd[0], far, row_panel, col_panel
    )
    col_panel = col_panel.reshape(2, rows * space, width)
    out = None
    for turn in range(ratio):
        out = kin_call((core + ratio - turn) % ratio, people, swap(row_panel, turn), col_panel, out)
    return out


def solution(mesh):
    placed = (P("cols", "rows"), P("cols", "rows"), P(None, "rows"))
    return jax.shard_map(
        per_device, mesh=mesh, in_specs=placed, out_specs=P("rows", "cols"), check_vma=False
    )
```

```python
import functools

import jax
import jax.numpy as jnp
from jax import lax
from jax.experimental import pallas as pl
from jax.experimental.pallas import tpu as pltpu
from jax.sharding import PartitionSpec as P

F32, BF16 = jnp.float32, jnp.bfloat16
VMEM_LIMIT = 56 * 1024 * 1024
VMEM_ALL = 63 * 1024 * 1024
SUB = 8


def split3(x):
    high = x.astype(BF16)
    rest = x - high.astype(F32)
    mid = rest.astype(BF16)
    low = (rest - mid.astype(F32)).astype(BF16)
    return high, mid, low


def group_starts(comps):
    starts, at = [], 0
    for j in range(comps):
        first = j // SUB * SUB
        starts.append((at, first))
        at += comps - first
    return starts, at


def gram_kernel(dosage_ref, present_ref, comps_ref, out_ref, lhs_ref):
    comps, people = comps_ref.shape
    markers = dosage_ref.shape[0]
    starts, total = group_starts(comps)
    chunk = 512 if people % 512 == 0 else people
    acc = None
    for at in range(0, people, chunk):
        span = slice(at, at + chunk)
        obs = present_ref[:, span].astype(F32)
        tgt = 0.5 * dosage_ref[:, span].astype(F32) * obs
        rhs = jnp.concatenate([obs, tgt], axis=0).astype(BF16)
        x = comps_ref[:, span]
        for j, (start, first) in enumerate(starts):
            lhs_ref[start : start + comps - first, :] = x[first:, :] * x[j : j + 1, :]
        lhs_ref[total : total + comps, :] = x
        tail = lhs_ref.shape[0] - total - comps
        lhs_ref[total + comps :, :] = jnp.ones((tail, chunk), F32)
        for part in split3(lhs_ref[...]):
            term = lax.dot_general(part, rhs, (((1,), (1,)), ((), ())), preferred_element_type=F32)
            acc = term if acc is None else acc + term
    half = total // 2
    out_ref[0:half, :] = jnp.concatenate([acc[0:half, 0:markers], acc[half:total, 0:markers]], axis=1)
    out_ref[half:, :] = acc[total : total + comps + SUB, :]


def gram_call(dosage, present, components):
    markers, people = dosage.shape
    comps = components.shape[0]
    total = group_starts(comps)[1]
    chunk = 512 if people % 512 == 0 else people
    return pl.pallas_call(
        gram_kernel,
        out_shape=jax.ShapeDtypeStruct((total // 2 + comps + SUB, 2 * markers), F32),
        scratch_shapes=[pltpu.VMEM((total + comps + 2 * SUB, chunk), F32)],
        compiler_params=pltpu.CompilerParams(vmem_limit_bytes=VMEM_LIMIT),
        name="gram",
    )(dosage, present, components)


def coef_rows(comps):
    return 4 * comps


def below(old, first, new):
    return new if first == 0 else jnp.concatenate([old[:first], new], axis=0)


def solve_kernel(comps, markers, *refs):
    out_ref = refs[-1]
    summed = refs[0][...]
    for ref in refs[1:-1]:
        summed = summed + ref[...]
    starts, total = group_starts(comps)
    half = total // 2
    left, right = summed[:, 0:markers], summed[:, markers : 2 * markers]

    def rows_of(start, count):
        if start + count <= half:
            return left[start : start + count]
        if start >= half:
            return right[start - half : start - half + count]
        return jnp.concatenate([left[start:half], right[0 : start + count - half]], axis=0)

    columns = [rows_of(start, comps - first) for start, first in starts]
    firsts = [first for _, first in starts]
    edge = left[half : half + comps]
    count = left[half + comps : half + comps + 1]
    moment = right[half : half + comps]
    moment_one = right[half + comps : half + comps + 1]
    factor, edge_f, moment_f = [], [], []
    for j in range(comps):
        first = firsts[j]
        column = columns[j]
        inv = 1.0 / column[j - first : j - first + 1]
        scaled = column * inv
        edge_j = edge[j : j + 1]
        moment_j = moment[j : j + 1]
        edge_s, moment_s = edge_j * inv, moment_j * inv
        row = lax.broadcasted_iota(jnp.int32, column.shape, 0) + first
        factor.append(jnp.where(row > j, scaled, 0.0))
        edge_f.append(edge_s)
        moment_f.append(moment_s)
        count = count - edge_s * edge_j
        moment_one = moment_one - edge_s * moment_j
        if j + 1 < comps:
            edge = below(edge, first, edge[first:] - column * edge_s)
            moment = below(moment, first, moment[first:] - column * moment_s)
        for k in range(j + 1, comps):
            offset = firsts[k] - first
            columns[k] = columns[k] - scaled[offset:] * column[k - first : k - first + 1]
    last = moment_one / count
    index = lax.broadcasted_iota(jnp.int32, (SUB, markers), 0)
    groups = [jnp.zeros((SUB, markers), F32) for _ in range(comps // SUB)]
    for j in range(comps - 1, -1, -1):
        first = firsts[j]
        value = moment_f[j] - edge_f[j] * last
        total_term = None
        for g in range(first // SUB, comps // SUB):
            term = factor[j][g * SUB - first : (g + 1) * SUB - first] * groups[g]
            total_term = term if total_term is None else total_term + term
        value = value - jnp.sum(total_term, axis=0, keepdims=True)
        g = j // SUB
        groups[g] = jnp.where(index == j - first, value, groups[g])
    coef = 2.0 * jnp.concatenate(groups, axis=0)
    last = 2.0 * last
    c1, c2, c3 = [part.astype(F32) for part in split3(coef)]
    l1, l2, l3 = [part.astype(F32) for part in split3(last)]
    index = lax.broadcasted_iota(jnp.int32, (comps, markers), 0)
    ones = jnp.where(index == 0, l1, jnp.where(index == 1, l2, jnp.where(index == 2, l3, 0.0)))
    stacked = jnp.concatenate([c1, c2, c3, ones], axis=0).astype(BF16)
    eye = (
        lax.broadcasted_iota(jnp.int32, (markers, markers), 0)
        == lax.broadcasted_iota(jnp.int32, (markers, markers), 1)
    ).astype(F32).astype(BF16)
    turned = lax.dot_general(eye, stacked, (((1,), (1,)), ((), ())), preferred_element_type=F32)
    out_ref[...] = turned.astype(BF16)


def solve_call(parts, comps, markers):
    return pl.pallas_call(
        functools.partial(solve_kernel, comps, markers),
        out_shape=jax.ShapeDtypeStruct((markers, coef_rows(comps)), BF16),
        compiler_params=pltpu.CompilerParams(vmem_limit_bytes=VMEM_LIMIT),
        name="solve",
    )(*parts)


def doubled_coef(coef):
    lanes = coef.shape[1]
    wide = coef.astype(F32)
    again = jnp.concatenate([wide[:, lanes // 2 :], wide[:, : lanes // 2]], axis=1)
    index = lax.broadcasted_iota(jnp.int32, wide.shape, 1)
    again = jnp.where(index < lanes // 2, wide, jnp.where(index < lanes // 4 * 3, again, 0.0))
    return jnp.concatenate([coef, again.astype(BF16)], axis=1)


def design_parts(x):
    d1, d2, d3 = split3(x)
    ones = jnp.ones(x.shape, BF16)
    return jnp.concatenate([d1, d1, d1, ones, d2, d2, d3, jnp.zeros(x.shape, BF16)], axis=0)


def factors(twice):
    twice = jnp.clip(twice, 0.02, 1.98)
    spread = twice * (2.0 - twice)
    return twice, spread * lax.rsqrt(spread)


def weigh(fitted, dosage, observed):
    twice, spread = factors(fitted)
    return observed * (dosage - twice), observed * spread


def parted(block, groups):
    block = block.astype(F32)
    height = block.shape[0] // (2 * groups)
    dosage = [block[2 * g * height : (2 * g + 1) * height] for g in range(groups)]
    present = [block[(2 * g + 1) * height : (2 * g + 2) * height] for g in range(groups)]
    if groups == 1:
        return dosage[0], present[0]
    return jnp.concatenate(dosage, axis=0), jnp.concatenate(present, axis=0)


def slot_of(source, plane, rows):
    ahead = lax.rem(source - plane + rows, rows)
    return jnp.where(lax.rem(plane, 2) == 0, ahead, lax.rem(rows - ahead, rows))


def by_even(slot, plane, rows):
    return jnp.where(lax.rem(plane, 2) == 0, plane < rows - slot, plane >= slot)


def early_kernel(rows, near, row_x_ref, col_x_ref, *refs):
    coef_refs, refs = refs[:rows], refs[rows:]
    held_ref, refs = refs[0], refs[1:]
    even, odd = refs[: rows - 2], refs[rows - 2 : 2 * rows - 4]
    piece_refs, refs = refs[2 * rows - 4 : 2 * rows - 4 + near], refs[2 * rows - 4 + near :]
    row_out, col_out, row_fit, col_fit, coef, fit = refs
    chip = coef_refs[0].shape[0]
    height = chip // rows
    space = coef.shape[0] // rows
    row = lax.axis_index("rows")
    plane = lax.axis_index("cols") // (lax.axis_size("cols") // rows)
    slots = [slot_of(plane ^ e, plane, rows) for e in range(rows)]

    @pl.when(pl.program_id(0) == 0)
    def _():
        if space != chip:
            coef[...] = jnp.zeros(coef.shape, BF16)
        for e in range(rows):
            place = pl.multiple_of(slots[e] * space, space)
            coef[pl.ds(place, chip), :] = doubled_coef(coef_refs[e][...])

    def fitted(x):
        return lax.dot_general(
            coef[...], design_parts(x), (((1,), (0,)), ((), ())), preferred_element_type=F32
        )

    if space != chip:
        row_out[...] = jnp.zeros(row_out.shape, BF16)
        col_out[...] = jnp.zeros(col_out.shape, BF16)
    fit_rows = fitted(row_x_ref[...])
    for slot in range(rows - 1):
        if slot == 0:
            block = held_ref[...]
        elif slot == 1:
            block = even[0][...]
        else:
            block = jnp.where(by_even(slot, plane, rows), even[slot - 1][...], odd[rows - slot - 1][...])
        resid, sdev = weigh(fit_rows[slot * space : slot * space + chip], *parted(block, rows))
        row_out[0, :, slot * space : slot * space + chip] = resid.astype(BF16).T
        row_out[1, :, slot * space : slot * space + chip] = sdev.astype(BF16).T
    row_fit[...] = fit_rows[(rows - 1) * space : (rows - 1) * space + chip]
    fit[...] = fitted(col_x_ref[...])
    for d in range(rows):
        for e in range(rows):
            place = pl.multiple_of(slots[e] * space + (row ^ d) * height, height)
            here = fit[pl.ds(place, height), :]
            if d < near:
                resid, sdev = weigh(here, *parted(piece_refs[d][e], 1))
                group = slots[e] * (space // height) + (row ^ d)
                col_out[0, group] = resid.astype(BF16)
                col_out[1, group] = sdev.astype(BF16)
            else:
                col_fit[e] = here


def early_call(rows, part, components, col_comps, coefs, held, even, odd, pieces):
    comps, width = col_comps.shape
    chip = coefs[0].shape[0]
    space = -(-chip // 128) * 128
    height = chip // rows
    wide = 256 if width % 256 == 0 else width
    whole = lambda i, at: (0, 0)
    block = pl.BlockSpec((2 * chip, wide), lambda i, at: (0, i))
    piece = pl.BlockSpec((rows, 2 * height, wide), lambda i, at: (0, 0, i))
    return pl.pallas_call(
        functools.partial(early_kernel_at, rows, len(pieces)),
        grid_spec=pltpu.PrefetchScalarGridSpec(
            num_scalar_prefetch=1,
            grid=(width // wide,),
            in_specs=[
                pl.BlockSpec((comps, wide), lambda i, at: (0, at[0] * (width // wide) + i)),
                pl.BlockSpec((comps, wide), lambda i, at: (0, i)),
            ]
            + [pl.BlockSpec(x.shape, whole) for x in coefs]
            + [block] * (1 + len(even) + len(odd))
            + [piece] * len(pieces),
            out_specs=(
                pl.BlockSpec((2, wide, rows * space), lambda i, at: (0, i, 0)),
                pl.BlockSpec((2, rows * space // height, height, wide), lambda i, at: (0, 0, 0, i)),
                pl.BlockSpec((chip, wide), lambda i, at: (0, i)),
                pl.BlockSpec((rows, height, wide), lambda i, at: (0, 0, i)),
            ),
            scratch_shapes=[
                pltpu.VMEM((rows * space, 2 * coefs[0].shape[1]), BF16),
                pltpu.VMEM((rows * space, wide), F32),
            ],
        ),
        out_shape=(
            jax.ShapeDtypeStruct((2, width, rows * space), BF16),
            jax.ShapeDtypeStruct((2, rows * space // height, height, width), BF16),
            jax.ShapeDtypeStruct((chip, width), F32),
            jax.ShapeDtypeStruct((rows, height, width), F32),
        ),
        compiler_params=pltpu.CompilerParams(vmem_limit_bytes=VMEM_ALL),
        name="early",
    )(part[None].astype(jnp.int32), components, col_comps, *coefs, held, *even, *odd, *pieces)


def early_kernel_at(rows, near, part_ref, *refs):
    early_kernel(rows, near, *refs)


def late_kernel(rows, group_ref, row_fit, col_fit, piece_ref, even_ref, odd_ref, *refs):
    row_out, col_out, block, row_part, col_part, block_sem, row_sems, col_sems = refs[2:]
    plane = lax.axis_index("cols") // (lax.axis_size("cols") // rows)
    last = by_even(rows - 1, plane, rows)

    @pl.when(last)
    def _():
        pltpu.make_async_copy(even_ref, block, block_sem).start()

    @pl.when(jnp.logical_not(last))
    def _():
        pltpu.make_async_copy(odd_ref, block, block_sem).start()

    copies = []
    for e in range(rows):
        resid, sdev = weigh(col_fit[e], *parted(piece_ref[e], 1))
        col_part[e, 0] = resid.astype(BF16)
        col_part[e, 1] = sdev.astype(BF16)
        for i in range(2):
            copies.append(
                pltpu.make_async_copy(col_part.at[e, i], col_out.at[i, group_ref[e]], col_sems.at[2 * e + i])
            )
            copies[-1].start()
    chip, width = row_fit.shape
    space = row_part.shape[2]
    if space != chip:
        row_part[...] = jnp.zeros(row_part.shape, BF16)
    pltpu.make_async_copy(odd_ref, block, block_sem).wait()
    wide = width // row_sems.shape[0]
    for at in range(0, width, wide):
        span = slice(at, at + wide)
        resid, sdev = weigh(row_fit[:, span], *parted(block[:, span], rows))
        row_part[0, span, 0:chip] = resid.astype(BF16).T
        row_part[1, span, 0:chip] = sdev.astype(BF16).T
        copies.append(
            pltpu.make_async_copy(
                row_part.at[:, span, :],
                row_out.at[:, span, (rows - 1) * space : rows * space],
                row_sems.at[at // wide],
            )
        )
        copies[-1].start()
    for copy in copies:
        copy.wait()


def late_call(rows, groups, row_fit, col_fit, even, odd, piece, row_panel, col_panel):
    chip, width = row_fit.shape
    height = chip // rows
    space = row_panel.shape[2] // rows
    wide = 256 if width % 256 == 0 else width
    anywhere = pl.BlockSpec(memory_space=pl.ANY)
    here = pl.BlockSpec(memory_space=pltpu.VMEM)
    return pl.pallas_call(
        functools.partial(late_kernel, rows),
        in_specs=[pl.BlockSpec(memory_space=pltpu.SMEM), here, here, here] + [anywhere] * 4,
        out_specs=(anywhere, anywhere),
        out_shape=(
            jax.ShapeDtypeStruct(row_panel.shape, BF16),
            jax.ShapeDtypeStruct(col_panel.shape, BF16),
        ),
        scratch_shapes=[
            pltpu.VMEM((2 * chip, width), BF16),
            pltpu.VMEM((2, width, space), BF16),
            pltpu.VMEM((rows, 2, height, width), BF16),
            pltpu.SemaphoreType.DMA,
            pltpu.SemaphoreType.DMA((width // wide,)),
            pltpu.SemaphoreType.DMA((2 * rows,)),
        ],
        input_output_aliases={6: 0, 7: 1},
        compiler_params=pltpu.CompilerParams(vmem_limit_bytes=VMEM_ALL),
        name="late",
    )(groups, row_fit, col_fit, piece, even, odd, row_panel, col_panel)


def quotient(numer, denom):
    inverse = pl.reciprocal(denom, approx=True)
    return numer * (inverse * (2.0 - denom * inverse))


def kin_kernel(part_ref, row_ref, col_ref, *refs):
    out_ref = refs[-1]
    numer = jnp.dot(row_ref[0], col_ref[0], preferred_element_type=F32)
    denom = jnp.dot(row_ref[1], col_ref[1], preferred_element_type=F32)
    out_ref[...] = quotient(numer, denom)


def kin_call(part, people, row_panel, col_panel, before):
    _, count, depth = row_panel.shape
    width = col_panel.shape[2]
    wide = 512 if width % 512 == 0 else width
    in_specs = [
        pl.BlockSpec((2, count, depth), lambda i, at: (0, 0, 0)),
        pl.BlockSpec((2, depth, wide), lambda i, at: (0, 0, i)),
    ]
    operands = [row_panel, col_panel]
    aliases = {}
    if before is not None:
        in_specs.append(pl.BlockSpec(memory_space=pl.ANY))
        operands.append(before)
        aliases = {len(operands): 0}
    return pl.pallas_call(
        kin_kernel,
        grid_spec=pltpu.PrefetchScalarGridSpec(
            num_scalar_prefetch=1,
            grid=(width // wide,),
            in_specs=in_specs,
            out_specs=pl.BlockSpec((count, wide), lambda i, at: (at[0], i)),
        ),
        out_shape=jax.ShapeDtypeStruct((people, width), F32),
        input_output_aliases=aliases,
        compiler_params=pltpu.CompilerParams(vmem_limit_bytes=VMEM_ALL),
        name="kinship",
    )(part[None].astype(jnp.int32), *operands)


def per_device(dosage, present, components):
    rows, cols = lax.axis_size("rows"), lax.axis_size("cols")
    ratio = cols // rows
    markers, people = dosage.shape
    comps = components.shape[0]
    width = people // ratio
    row = lax.axis_index("rows")
    col = lax.axis_index("cols")
    core, plane = col % ratio, col // ratio

    def pairs(hop):
        moves = [(z, c, *hop(z, c)) for z in range(rows) for c in range(ratio)]
        return [(z * ratio + c, y * ratio + b) for z, c, y, b in moves if 0 <= y < rows]

    def swap(x, k):
        return lax.ppermute(x, "cols", pairs(lambda z, c: (z, (c + k) % ratio))) if k else x

    def exchange(x, first):
        other = [z + 1 if (z - first) % 2 == 0 else z - 1 for z in range(rows)]
        other = [y if 0 <= y < rows else z for z, y in enumerate(other)]
        return lax.ppermute(x, "cols", pairs(lambda z, c: (other[z], c)))

    def beside(x, d):
        return lax.ppermute(x, "rows", [(i, i ^ d) for i in range(rows)]) if d else x

    def across(x, e):
        return lax.ppermute(x, "cols", pairs(lambda z, c: (z ^ e, c))) if e else x

    def by_core(parts):
        placed = []
        for p in range(ratio):
            chosen = parts[0]
            for k in range(1, ratio):
                chosen = jnp.where((core - p) % ratio == k, parts[k], chosen)
            placed.append(chosen)
        return jnp.concatenate(placed, axis=0)

    subs = rows // ratio
    fine = markers // subs
    halves = []
    for k in range(ratio):
        begin = (core + k) % ratio * width
        both = [
            lax.dynamic_slice_in_dim(x, begin, width, 1).astype(BF16).reshape(subs, 1, fine, width)
            for x in (dosage, present)
        ]
        halves.append(swap(jnp.concatenate(both, axis=1).reshape(2 * markers, width), k))
    held = by_core(halves)
    held, dosage, present = lax.optimization_barrier((held, dosage, present))
    odd = [exchange(held, 1)]
    even = [exchange(held, 0)]

    height = held.shape[0] // rows
    quarters = [beside(lax.dynamic_slice_in_dim(held, (row ^ d) * height, height, 0), d) for d in range(rows)]
    hops = [1 << i for i in range(rows.bit_length() - 1)]

    def doubled(x, hop):
        return jnp.where(((row ^ plane) & hop) == 0, x, beside(x, hop))

    gram = gram_call(dosage, present, components)
    col_comps = lax.dynamic_slice_in_dim(components, core * width, width, 1)
    quarters, gram, col_comps = lax.optimization_barrier((quarters, gram, col_comps))
    gram = gram + beside(gram, hops[0])
    col_comps = doubled(col_comps, hops[-1])
    quarters, gram, col_comps, held, odd, even = lax.optimization_barrier(
        (jnp.stack(quarters), gram, col_comps, held, odd, even)
    )
    moved = [
        across(lax.dynamic_index_in_dim(quarters, row ^ plane ^ e, 0, keepdims=False), e) for e in range(rows)
    ]
    for hop in hops[1:-1]:
        gram = gram + beside(gram, hop)
    coef = solve_call([gram, beside(gram, hops[-1])], comps, markers)
    coef = by_core([swap(coef, k) for k in range(ratio)])
    for hop in hops[:-1]:
        col_comps = doubled(col_comps, hop)
    coefs = [across(coef, e) for e in range(rows)]
    moved, coefs, col_comps, held, odd, even = lax.optimization_barrier(
        (jnp.stack(moved), coefs, col_comps, held, odd, even)
    )
    near = [moved]
    for step in range(rows - 3):
        odd, even = odd + [exchange(even[-1], 1)], even + [exchange(odd[-1], 0)]
        upto = rows - 1 if step == rows - 4 else min(rows - 1, 2 * step + 3)
        near += [beside(moved, d) for d in range(len(near), upto)]
        near, coefs, col_comps, held, odd, even = lax.optimization_barrier(
            (near, coefs, col_comps, held, odd, even)
        )
    last = exchange(odd[-1], 0)
    far = beside(near[0], rows - 1)
    row_panel, col_panel, row_fit, col_fit = early_call(
        rows, core, components, col_comps, coefs, held, even, odd, near
    )
    space = row_panel.shape[2] // rows
    groups = jnp.stack(
        [
            slot_of(plane ^ e, plane, rows) * (2 * space // height) + (row ^ (rows - 1))
            for e in range(rows)
        ]
    ).astype(jnp.int32)
    row_panel, col_panel = late_call(
        rows, groups, row_fit, col_fit, last, odd[0], far, row_panel, col_panel
    )
    col_panel = col_panel.reshape(2, rows * space, width)
    out = None
    for turn in range(ratio):
        out = kin_call((core + ratio - turn) % ratio, people, swap(row_panel, turn), col_panel, out)
    return out


def solution(mesh):
    placed = (P("cols", "rows"), P("cols", "rows"), P(None, "rows"))
    return jax.shard_map(
        per_device, mesh=mesh, in_specs=placed, out_specs=P("rows", "cols"), check_vma=False
    )
```

```python
import functools

import jax
import jax.numpy as jnp
from jax import lax
from jax.experimental import pallas as pl
from jax.experimental.pallas import tpu as pltpu
from jax.sharding import PartitionSpec as P

F32, BF16 = jnp.float32, jnp.bfloat16
VMEM_LIMIT = 56 * 1024 * 1024
VMEM_ALL = 63 * 1024 * 1024
SUB = 8


def split3(x):
    high = x.astype(BF16)
    rest = x - high.astype(F32)
    mid = rest.astype(BF16)
    low = (rest - mid.astype(F32)).astype(BF16)
    return high, mid, low


def group_starts(comps):
    starts, at = [], 0
    for j in range(comps):
        first = j // SUB * SUB
        starts.append((at, first))
        at += comps - first
    return starts, at


def gram_kernel(dosage_ref, present_ref, comps_ref, out_ref, lhs_ref):
    comps, people = comps_ref.shape
    markers = dosage_ref.shape[0]
    starts, total = group_starts(comps)
    chunk = 512 if people % 512 == 0 else people
    acc = None
    for at in range(0, people, chunk):
        span = slice(at, at + chunk)
        obs = present_ref[:, span].astype(F32)
        tgt = 0.5 * dosage_ref[:, span].astype(F32) * obs
        rhs = jnp.concatenate([obs, tgt], axis=0).astype(BF16)
        x = comps_ref[:, span]
        for j, (start, first) in enumerate(starts):
            lhs_ref[start : start + comps - first, :] = x[first:, :] * x[j : j + 1, :]
        lhs_ref[total : total + comps, :] = x
        tail = lhs_ref.shape[0] - total - comps
        lhs_ref[total + comps :, :] = jnp.ones((tail, chunk), F32)
        for part in split3(lhs_ref[...]):
            term = lax.dot_general(part, rhs, (((1,), (1,)), ((), ())), preferred_element_type=F32)
            acc = term if acc is None else acc + term
    half = total // 2
    out_ref[0:half, :] = jnp.concatenate([acc[0:half, 0:markers], acc[half:total, 0:markers]], axis=1)
    out_ref[half:, :] = acc[total : total + comps + SUB, :]


def gram_call(dosage, present, components):
    markers, people = dosage.shape
    comps = components.shape[0]
    total = group_starts(comps)[1]
    chunk = 512 if people % 512 == 0 else people
    return pl.pallas_call(
        gram_kernel,
        out_shape=jax.ShapeDtypeStruct((total // 2 + comps + SUB, 2 * markers), F32),
        scratch_shapes=[pltpu.VMEM((total + comps + 2 * SUB, chunk), F32)],
        compiler_params=pltpu.CompilerParams(vmem_limit_bytes=VMEM_LIMIT),
        name="gram",
    )(dosage, present, components)


def coef_rows(comps):
    return 4 * comps


def below(old, first, new):
    return new if first == 0 else jnp.concatenate([old[:first], new], axis=0)


def solve_kernel(comps, markers, *refs):
    out_ref = refs[-1]
    summed = refs[0][...]
    for ref in refs[1:-1]:
        summed = summed + ref[...]
    starts, total = group_starts(comps)
    half = total // 2
    left, right = summed[:, 0:markers], summed[:, markers : 2 * markers]

    def rows_of(start, count):
        if start + count <= half:
            return left[start : start + count]
        if start >= half:
            return right[start - half : start - half + count]
        return jnp.concatenate([left[start:half], right[0 : start + count - half]], axis=0)

    columns = [rows_of(start, comps - first) for start, first in starts]
    firsts = [first for _, first in starts]
    edge = left[half : half + comps]
    count = left[half + comps : half + comps + 1]
    moment = right[half : half + comps]
    moment_one = right[half + comps : half + comps + 1]
    factor, edge_f, moment_f = [], [], []
    for j in range(comps):
        first = firsts[j]
        column = columns[j]
        inv = 1.0 / column[j - first : j - first + 1]
        scaled = column * inv
        edge_j = edge[j : j + 1]
        moment_j = moment[j : j + 1]
        edge_s, moment_s = edge_j * inv, moment_j * inv
        row = lax.broadcasted_iota(jnp.int32, column.shape, 0) + first
        factor.append(jnp.where(row > j, scaled, 0.0))
        edge_f.append(edge_s)
        moment_f.append(moment_s)
        count = count - edge_s * edge_j
        moment_one = moment_one - edge_s * moment_j
        if j + 1 < comps:
            edge = below(edge, first, edge[first:] - column * edge_s)
            moment = below(moment, first, moment[first:] - column * moment_s)
        for k in range(j + 1, comps):
            offset = firsts[k] - first
            columns[k] = columns[k] - scaled[offset:] * column[k - first : k - first + 1]
    last = moment_one / count
    index = lax.broadcasted_iota(jnp.int32, (SUB, markers), 0)
    groups = [jnp.zeros((SUB, markers), F32) for _ in range(comps // SUB)]
    for j in range(comps - 1, -1, -1):
        first = firsts[j]
        value = moment_f[j] - edge_f[j] * last
        total_term = None
        for g in range(first // SUB, comps // SUB):
            term = factor[j][g * SUB - first : (g + 1) * SUB - first] * groups[g]
            total_term = term if total_term is None else total_term + term
        value = value - jnp.sum(total_term, axis=0, keepdims=True)
        g = j // SUB
        groups[g] = jnp.where(index == j - first, value, groups[g])
    coef = 2.0 * jnp.concatenate(groups, axis=0)
    last = 2.0 * last
    c1, c2, c3 = [part.astype(F32) for part in split3(coef)]
    l1, l2, l3 = [part.astype(F32) for part in split3(last)]
    index = lax.broadcasted_iota(jnp.int32, (comps, markers), 0)
    ones = jnp.where(index == 0, l1, jnp.where(index == 1, l2, jnp.where(index == 2, l3, 0.0)))
    stacked = jnp.concatenate([c1, c2, c3, ones], axis=0).astype(BF16)
    eye = (
        lax.broadcasted_iota(jnp.int32, (markers, markers), 0)
        == lax.broadcasted_iota(jnp.int32, (markers, markers), 1)
    ).astype(F32).astype(BF16)
    turned = lax.dot_general(eye, stacked, (((1,), (1,)), ((), ())), preferred_element_type=F32)
    out_ref[...] = turned.astype(BF16)


def solve_call(parts, comps, markers):
    return pl.pallas_call(
        functools.partial(solve_kernel, comps, markers),
        out_shape=jax.ShapeDtypeStruct((markers, coef_rows(comps)), BF16),
        compiler_params=pltpu.CompilerParams(vmem_limit_bytes=VMEM_LIMIT),
        name="solve",
    )(*parts)


def doubled_coef(coef):
    lanes = coef.shape[1]
    wide = coef.astype(F32)
    again = jnp.concatenate([wide[:, lanes // 2 :], wide[:, : lanes // 2]], axis=1)
    index = lax.broadcasted_iota(jnp.int32, wide.shape, 1)
    again = jnp.where(index < lanes // 2, wide, jnp.where(index < lanes // 4 * 3, again, 0.0))
    return jnp.concatenate([coef, again.astype(BF16)], axis=1)


def design_parts(x):
    d1, d2, d3 = split3(x)
    ones = jnp.ones(x.shape, BF16)
    return jnp.concatenate([d1, d1, d1, ones, d2, d2, d3, jnp.zeros(x.shape, BF16)], axis=0)


def factors(twice):
    twice = jnp.clip(twice, 0.02, 1.98)
    spread = twice * (2.0 - twice)
    return twice, spread * lax.rsqrt(spread)


def weigh(fitted, dosage, observed):
    twice, spread = factors(fitted)
    return observed * (dosage - twice), observed * spread


def parted(block, groups):
    block = block.astype(F32)
    height = block.shape[0] // (2 * groups)
    dosage = [block[2 * g * height : (2 * g + 1) * height] for g in range(groups)]
    present = [block[(2 * g + 1) * height : (2 * g + 2) * height] for g in range(groups)]
    if groups == 1:
        return dosage[0], present[0]
    return jnp.concatenate(dosage, axis=0), jnp.concatenate(present, axis=0)


def slot_of(source, plane, rows):
    ahead = lax.rem(source - plane + rows, rows)
    return jnp.where(lax.rem(plane, 2) == 0, ahead, lax.rem(rows - ahead, rows))


def by_even(slot, plane, rows):
    return jnp.where(lax.rem(plane, 2) == 0, plane < rows - slot, plane >= slot)


def early_kernel(rows, near, row_x_ref, col_x_ref, *refs):
    coef_refs, refs = refs[:rows], refs[rows:]
    held_ref, refs = refs[0], refs[1:]
    even, odd = refs[: rows - 2], refs[rows - 2 : 2 * rows - 4]
    piece_refs, refs = refs[2 * rows - 4 : 2 * rows - 4 + near], refs[2 * rows - 4 + near :]
    row_out, col_out, row_fit, col_fit, coef, fit = refs
    chip = coef_refs[0].shape[0]
    height = chip // rows
    space = coef.shape[0] // rows
    row = lax.axis_index("rows")
    plane = lax.axis_index("cols") // (lax.axis_size("cols") // rows)
    slots = [slot_of(plane ^ e, plane, rows) for e in range(rows)]

    @pl.when(pl.program_id(0) == 0)
    def _():
        if space != chip:
            coef[...] = jnp.zeros(coef.shape, BF16)
        for e in range(rows):
            place = pl.multiple_of(slots[e] * space, space)
            coef[pl.ds(place, chip), :] = doubled_coef(coef_refs[e][...])

    def fitted(x):
        return lax.dot_general(
            coef[...], design_parts(x), (((1,), (0,)), ((), ())), preferred_element_type=F32
        )

    if space != chip:
        row_out[...] = jnp.zeros(row_out.shape, BF16)
        col_out[...] = jnp.zeros(col_out.shape, BF16)
    fit_rows = fitted(row_x_ref[...])
    for slot in range(rows - 1):
        if slot == 0:
            block = held_ref[...]
        elif slot == 1:
            block = even[0][...]
        else:
            block = jnp.where(by_even(slot, plane, rows), even[slot - 1][...], odd[rows - slot - 1][...])
        resid, sdev = weigh(fit_rows[slot * space : slot * space + chip], *parted(block, rows))
        row_out[0, :, slot * space : slot * space + chip] = resid.astype(BF16).T
        row_out[1, :, slot * space : slot * space + chip] = sdev.astype(BF16).T
    row_fit[...] = fit_rows[(rows - 1) * space : (rows - 1) * space + chip]
    fit[...] = fitted(col_x_ref[...])
    for d in range(rows):
        for e in range(rows):
            place = pl.multiple_of(slots[e] * space + (row ^ d) * height, height)
            here = fit[pl.ds(place, height), :]
            if d < near:
                resid, sdev = weigh(here, *parted(piece_refs[d][e], 1))
                group = slots[e] * (space // height) + (row ^ d)
                col_out[0, group] = resid.astype(BF16)
                col_out[1, group] = sdev.astype(BF16)
            else:
                col_fit[e] = here


def early_call(rows, part, components, col_comps, coefs, held, even, odd, pieces):
    comps, width = col_comps.shape
    chip = coefs[0].shape[0]
    space = -(-chip // 128) * 128
    height = chip // rows
    wide = 256 if width % 256 == 0 else width
    whole = lambda i, at: (0, 0)
    block = pl.BlockSpec((2 * chip, wide), lambda i, at: (0, i))
    piece = pl.BlockSpec((rows, 2 * height, wide), lambda i, at: (0, 0, i))
    return pl.pallas_call(
        functools.partial(early_kernel_at, rows, len(pieces)),
        grid_spec=pltpu.PrefetchScalarGridSpec(
            num_scalar_prefetch=1,
            grid=(width // wide,),
            in_specs=[
                pl.BlockSpec((comps, wide), lambda i, at: (0, at[0] * (width // wide) + i)),
                pl.BlockSpec((comps, wide), lambda i, at: (0, i)),
            ]
            + [pl.BlockSpec(x.shape, whole) for x in coefs]
            + [block] * (1 + len(even) + len(odd))
            + [piece] * len(pieces),
            out_specs=(
                pl.BlockSpec((2, wide, rows * space), lambda i, at: (0, i, 0)),
                pl.BlockSpec((2, rows * space // height, height, wide), lambda i, at: (0, 0, 0, i)),
                pl.BlockSpec((chip, wide), lambda i, at: (0, i)),
                pl.BlockSpec((rows, height, wide), lambda i, at: (0, 0, i)),
            ),
            scratch_shapes=[
                pltpu.VMEM((rows * space, 2 * coefs[0].shape[1]), BF16),
                pltpu.VMEM((rows * space, wide), F32),
            ],
        ),
        out_shape=(
            jax.ShapeDtypeStruct((2, width, rows * space), BF16),
            jax.ShapeDtypeStruct((2, rows * space // height, height, width), BF16),
            jax.ShapeDtypeStruct((chip, width), F32),
            jax.ShapeDtypeStruct((rows, height, width), F32),
        ),
        compiler_params=pltpu.CompilerParams(vmem_limit_bytes=VMEM_ALL),
        name="early",
    )(part[None].astype(jnp.int32), components, col_comps, *coefs, held, *even, *odd, *pieces)


def early_kernel_at(rows, near, part_ref, *refs):
    early_kernel(rows, near, *refs)


def late_kernel(rows, group_ref, row_fit, col_fit, piece_ref, even_ref, odd_ref, *refs):
    row_out, col_out, block, row_part, col_part, block_sem, row_sems, col_sems = refs[2:]
    plane = lax.axis_index("cols") // (lax.axis_size("cols") // rows)
    last = by_even(rows - 1, plane, rows)

    @pl.when(last)
    def _():
        pltpu.make_async_copy(even_ref, block, block_sem).start()

    @pl.when(jnp.logical_not(last))
    def _():
        pltpu.make_async_copy(odd_ref, block, block_sem).start()

    copies = []
    for e in range(rows):
        resid, sdev = weigh(col_fit[e], *parted(piece_ref[e], 1))
        col_part[e, 0] = resid.astype(BF16)
        col_part[e, 1] = sdev.astype(BF16)
        for i in range(2):
            copies.append(
                pltpu.make_async_copy(col_part.at[e, i], col_out.at[i, group_ref[e]], col_sems.at[2 * e + i])
            )
            copies[-1].start()
    chip, width = row_fit.shape
    space = row_part.shape[2]
    if space != chip:
        row_part[...] = jnp.zeros(row_part.shape, BF16)
    pltpu.make_async_copy(odd_ref, block, block_sem).wait()
    wide = width // row_sems.shape[0]
    for at in range(0, width, wide):
        span = slice(at, at + wide)
        resid, sdev = weigh(row_fit[:, span], *parted(block[:, span], rows))
        row_part[0, span, 0:chip] = resid.astype(BF16).T
        row_part[1, span, 0:chip] = sdev.astype(BF16).T
        copies.append(
            pltpu.make_async_copy(
                row_part.at[:, span, :],
                row_out.at[:, span, (rows - 1) * space : rows * space],
                row_sems.at[at // wide],
            )
        )
        copies[-1].start()
    for copy in copies:
        copy.wait()


def late_call(rows, groups, row_fit, col_fit, even, odd, piece, row_panel, col_panel):
    chip, width = row_fit.shape
    height = chip // rows
    space = row_panel.shape[2] // rows
    wide = 256 if width % 256 == 0 else width
    anywhere = pl.BlockSpec(memory_space=pl.ANY)
    here = pl.BlockSpec(memory_space=pltpu.VMEM)
    return pl.pallas_call(
        functools.partial(late_kernel, rows),
        in_specs=[pl.BlockSpec(memory_space=pltpu.SMEM), here, here, here] + [anywhere] * 4,
        out_specs=(anywhere, anywhere),
        out_shape=(
            jax.ShapeDtypeStruct(row_panel.shape, BF16),
            jax.ShapeDtypeStruct(col_panel.shape, BF16),
        ),
        scratch_shapes=[
            pltpu.VMEM((2 * chip, width), BF16),
            pltpu.VMEM((2, width, space), BF16),
            pltpu.VMEM((rows, 2, height, width), BF16),
            pltpu.SemaphoreType.DMA,
            pltpu.SemaphoreType.DMA((width // wide,)),
            pltpu.SemaphoreType.DMA((2 * rows,)),
        ],
        input_output_aliases={6: 0, 7: 1},
        compiler_params=pltpu.CompilerParams(vmem_limit_bytes=VMEM_ALL),
        name="late",
    )(groups, row_fit, col_fit, piece, even, odd, row_panel, col_panel)


def quotient(numer, denom):
    inverse = pl.reciprocal(denom, approx=True)
    return numer * (inverse * (2.0 - denom * inverse))


def kin_kernel(part_ref, row_ref, col_ref, *refs):
    out_ref = refs[-1]
    numer = jnp.dot(row_ref[0], col_ref[0], preferred_element_type=F32)
    denom = jnp.dot(row_ref[1], col_ref[1], preferred_element_type=F32)
    out_ref[...] = quotient(numer, denom)


def kin_call(part, people, row_panel, col_panel, before):
    _, count, depth = row_panel.shape
    width = col_panel.shape[2]
    wide = 512 if width % 512 == 0 else width
    in_specs = [
        pl.BlockSpec((2, count, depth), lambda i, at: (0, 0, 0)),
        pl.BlockSpec((2, depth, wide), lambda i, at: (0, 0, i)),
    ]
    operands = [row_panel, col_panel]
    aliases = {}
    if before is not None:
        in_specs.append(pl.BlockSpec(memory_space=pl.ANY))
        operands.append(before)
        aliases = {len(operands): 0}
    return pl.pallas_call(
        kin_kernel,
        grid_spec=pltpu.PrefetchScalarGridSpec(
            num_scalar_prefetch=1,
            grid=(width // wide,),
            in_specs=in_specs,
            out_specs=pl.BlockSpec((count, wide), lambda i, at: (at[0], i)),
        ),
        out_shape=jax.ShapeDtypeStruct((people, width), F32),
        input_output_aliases=aliases,
        compiler_params=pltpu.CompilerParams(vmem_limit_bytes=VMEM_ALL),
        name="kinship",
    )(part[None].astype(jnp.int32), *operands)


def per_device(dosage, present, components):
    rows, cols = lax.axis_size("rows"), lax.axis_size("cols")
    ratio = cols // rows
    markers, people = dosage.shape
    comps = components.shape[0]
    width = people // ratio
    row = lax.axis_index("rows")
    col = lax.axis_index("cols")
    core, plane = col % ratio, col // ratio

    def pairs(hop):
        moves = [(z, c, *hop(z, c)) for z in range(rows) for c in range(ratio)]
        return [(z * ratio + c, y * ratio + b) for z, c, y, b in moves if 0 <= y < rows]

    def swap(x, k):
        return lax.ppermute(x, "cols", pairs(lambda z, c: (z, (c + k) % ratio))) if k else x

    def exchange(x, first):
        other = [z + 1 if (z - first) % 2 == 0 else z - 1 for z in range(rows)]
        other = [y if 0 <= y < rows else z for z, y in enumerate(other)]
        return lax.ppermute(x, "cols", pairs(lambda z, c: (other[z], c)))

    def beside(x, d):
        return lax.ppermute(x, "rows", [(i, i ^ d) for i in range(rows)]) if d else x

    def across(x, e):
        return lax.ppermute(x, "cols", pairs(lambda z, c: (z ^ e, c))) if e else x

    def by_core(parts):
        placed = []
        for p in range(ratio):
            chosen = parts[0]
            for k in range(1, ratio):
                chosen = jnp.where((core - p) % ratio == k, parts[k], chosen)
            placed.append(chosen)
        return jnp.concatenate(placed, axis=0)

    subs = rows // ratio
    fine = markers // subs
    halves = []
    for k in range(ratio):
        begin = (core + k) % ratio * width
        both = [
            lax.dynamic_slice_in_dim(x, begin, width, 1).astype(BF16).reshape(subs, 1, fine, width)
            for x in (dosage, present)
        ]
        halves.append(swap(jnp.concatenate(both, axis=1).reshape(2 * markers, width), k))
    held = by_core(halves)
    held, dosage, present = lax.optimization_barrier((held, dosage, present))
    odd = [exchange(held, 1)]
    even = [exchange(held, 0)]

    height = held.shape[0] // rows
    quarters = [beside(lax.dynamic_slice_in_dim(held, (row ^ d) * height, height, 0), d) for d in range(rows)]
    hops = [1 << i for i in range(rows.bit_length() - 1)]

    def doubled(x, hop):
        return jnp.where(((row ^ plane) & hop) == 0, x, beside(x, hop))

    gram = gram_call(dosage, present, components)
    col_comps = lax.dynamic_slice_in_dim(components, core * width, width, 1)
    quarters[1], gram, col_comps = lax.optimization_barrier((quarters[1], gram, col_comps))
    gram = gram + beside(gram, hops[0])
    col_comps = doubled(col_comps, hops[-1])
    quarters, gram, col_comps, held, odd, even = lax.optimization_barrier(
        (jnp.stack(quarters), gram, col_comps, held, odd, even)
    )
    moved = [
        across(lax.dynamic_index_in_dim(quarters, row ^ plane ^ e, 0, keepdims=False), e) for e in range(rows)
    ]
    for hop in hops[1:-1]:
        gram = gram + beside(gram, hop)
    coef = solve_call([gram, beside(gram, hops[-1])], comps, markers)
    coef = by_core([swap(coef, k) for k in range(ratio)])
    for hop in hops[:-1]:
        col_comps = doubled(col_comps, hop)
    coefs = [across(coef, e) for e in range(rows)]
    moved, coefs, col_comps, held, odd, even = lax.optimization_barrier(
        (jnp.stack(moved), coefs, col_comps, held, odd, even)
    )
    near = [moved]
    for step in range(rows - 3):
        odd, even = odd + [exchange(even[-1], 1)], even + [exchange(odd[-1], 0)]
        upto = rows - 1 if step == rows - 4 else min(rows - 1, 2 * step + 3)
        near += [beside(moved, d) for d in range(len(near), upto)]
        near, coefs, col_comps, held, odd, even = lax.optimization_barrier(
            (near, coefs, col_comps, held, odd, even)
        )
    last = exchange(odd[-1], 0)
    far = beside(near[0], rows - 1)
    row_panel, col_panel, row_fit, col_fit = early_call(
        rows, core, components, col_comps, coefs, held, even, odd, near
    )
    space = row_panel.shape[2] // rows
    groups = jnp.stack(
        [
            slot_of(plane ^ e, plane, rows) * (2 * space // height) + (row ^ (rows - 1))
            for e in range(rows)
        ]
    ).astype(jnp.int32)
    row_panel, col_panel = late_call(
        rows, groups, row_fit, col_fit, last, odd[0], far, row_panel, col_panel
    )
    col_panel = col_panel.reshape(2, rows * space, width)
    out = None
    for turn in range(ratio):
        out = kin_call((core + ratio - turn) % ratio, people, swap(row_panel, turn), col_panel, out)
    return out


def solution(mesh):
    placed = (P("cols", "rows"), P("cols", "rows"), P(None, "rows"))
    return jax.shard_map(
        per_device, mesh=mesh, in_specs=placed, out_specs=P("rows", "cols"), check_vma=False
    )
```

```python
import functools

import jax
import jax.numpy as jnp
from jax import lax
from jax.experimental import pallas as pl
from jax.experimental.pallas import tpu as pltpu
from jax.sharding import PartitionSpec as P

F32, BF16 = jnp.float32, jnp.bfloat16
VMEM_LIMIT = 56 * 1024 * 1024
VMEM_ALL = 63 * 1024 * 1024
SUB = 8


def split3(x):
    high = x.astype(BF16)
    rest = x - high.astype(F32)
    mid = rest.astype(BF16)
    low = (rest - mid.astype(F32)).astype(BF16)
    return high, mid, low


def group_starts(comps):
    starts, at = [], 0
    for j in range(comps):
        first = j // SUB * SUB
        starts.append((at, first))
        at += comps - first
    return starts, at


def gram_kernel(dosage_ref, present_ref, comps_ref, out_ref, lhs_ref):
    comps, people = comps_ref.shape
    markers = dosage_ref.shape[0]
    starts, total = group_starts(comps)
    chunk = 512 if people % 512 == 0 else people
    acc = None
    for at in range(0, people, chunk):
        span = slice(at, at + chunk)
        obs = present_ref[:, span].astype(F32)
        tgt = 0.5 * dosage_ref[:, span].astype(F32) * obs
        rhs = jnp.concatenate([obs, tgt], axis=0).astype(BF16)
        x = comps_ref[:, span]
        for j, (start, first) in enumerate(starts):
            lhs_ref[start : start + comps - first, :] = x[first:, :] * x[j : j + 1, :]
        lhs_ref[total : total + comps, :] = x
        tail = lhs_ref.shape[0] - total - comps
        lhs_ref[total + comps :, :] = jnp.ones((tail, chunk), F32)
        for part in split3(lhs_ref[...]):
            term = lax.dot_general(part, rhs, (((1,), (1,)), ((), ())), preferred_element_type=F32)
            acc = term if acc is None else acc + term
    half = total // 2
    out_ref[0:half, :] = jnp.concatenate([acc[0:half, 0:markers], acc[half:total, 0:markers]], axis=1)
    out_ref[half:, :] = acc[total : total + comps + SUB, :]


def gram_call(dosage, present, components):
    markers, people = dosage.shape
    comps = components.shape[0]
    total = group_starts(comps)[1]
    chunk = 512 if people % 512 == 0 else people
    return pl.pallas_call(
        gram_kernel,
        out_shape=jax.ShapeDtypeStruct((total // 2 + comps + SUB, 2 * markers), F32),
        scratch_shapes=[pltpu.VMEM((total + comps + 2 * SUB, chunk), F32)],
        compiler_params=pltpu.CompilerParams(vmem_limit_bytes=VMEM_LIMIT),
        name="gram",
    )(dosage, present, components)


def coef_rows(comps):
    return 4 * comps


def below(old, first, new):
    return new if first == 0 else jnp.concatenate([old[:first], new], axis=0)


def solve_kernel(comps, markers, *refs):
    out_ref = refs[-1]
    summed = refs[0][...]
    for ref in refs[1:-1]:
        summed = summed + ref[...]
    starts, total = group_starts(comps)
    half = total // 2
    left, right = summed[:, 0:markers], summed[:, markers : 2 * markers]

    def rows_of(start, count):
        if start + count <= half:
            return left[start : start + count]
        if start >= half:
            return right[start - half : start - half + count]
        return jnp.concatenate([left[start:half], right[0 : start + count - half]], axis=0)

    columns = [rows_of(start, comps - first) for start, first in starts]
    firsts = [first for _, first in starts]
    edge = left[half : half + comps]
    count = left[half + comps : half + comps + 1]
    moment = right[half : half + comps]
    moment_one = right[half + comps : half + comps + 1]
    factor, edge_f, moment_f = [], [], []
    for j in range(comps):
        first = firsts[j]
        column = columns[j]
        inv = 1.0 / column[j - first : j - first + 1]
        scaled = column * inv
        edge_j = edge[j : j + 1]
        moment_j = moment[j : j + 1]
        edge_s, moment_s = edge_j * inv, moment_j * inv
        row = lax.broadcasted_iota(jnp.int32, column.shape, 0) + first
        factor.append(jnp.where(row > j, scaled, 0.0))
        edge_f.append(edge_s)
        moment_f.append(moment_s)
        count = count - edge_s * edge_j
        moment_one = moment_one - edge_s * moment_j
        if j + 1 < comps:
            edge = below(edge, first, edge[first:] - column * edge_s)
            moment = below(moment, first, moment[first:] - column * moment_s)
        for k in range(j + 1, comps):
            offset = firsts[k] - first
            columns[k] = columns[k] - scaled[offset:] * column[k - first : k - first + 1]
    last = moment_one / count
    index = lax.broadcasted_iota(jnp.int32, (SUB, markers), 0)
    groups = [jnp.zeros((SUB, markers), F32) for _ in range(comps // SUB)]
    for j in range(comps - 1, -1, -1):
        first = firsts[j]
        value = moment_f[j] - edge_f[j] * last
        total_term = None
        for g in range(first // SUB, comps // SUB):
            term = factor[j][g * SUB - first : (g + 1) * SUB - first] * groups[g]
            total_term = term if total_term is None else total_term + term
        value = value - jnp.sum(total_term, axis=0, keepdims=True)
        g = j // SUB
        groups[g] = jnp.where(index == j - first, value, groups[g])
    coef = 2.0 * jnp.concatenate(groups, axis=0)
    last = 2.0 * last
    c1, c2, c3 = [part.astype(F32) for part in split3(coef)]
    l1, l2, l3 = [part.astype(F32) for part in split3(last)]
    index = lax.broadcasted_iota(jnp.int32, (comps, markers), 0)
    ones = jnp.where(index == 0, l1, jnp.where(index == 1, l2, jnp.where(index == 2, l3, 0.0)))
    stacked = jnp.concatenate([c1, c2, c3, ones], axis=0).astype(BF16)
    eye = (
        lax.broadcasted_iota(jnp.int32, (markers, markers), 0)
        == lax.broadcasted_iota(jnp.int32, (markers, markers), 1)
    ).astype(F32).astype(BF16)
    turned = lax.dot_general(eye, stacked, (((1,), (1,)), ((), ())), preferred_element_type=F32)
    out_ref[...] = turned.astype(BF16)


def solve_call(parts, comps, markers):
    return pl.pallas_call(
        functools.partial(solve_kernel, comps, markers),
        out_shape=jax.ShapeDtypeStruct((markers, coef_rows(comps)), BF16),
        compiler_params=pltpu.CompilerParams(vmem_limit_bytes=VMEM_LIMIT),
        name="solve",
    )(*parts)


def doubled_coef(coef):
    lanes = coef.shape[1]
    wide = coef.astype(F32)
    again = jnp.concatenate([wide[:, lanes // 2 :], wide[:, : lanes // 2]], axis=1)
    index = lax.broadcasted_iota(jnp.int32, wide.shape, 1)
    again = jnp.where(index < lanes // 2, wide, jnp.where(index < lanes // 4 * 3, again, 0.0))
    return jnp.concatenate([coef, again.astype(BF16)], axis=1)


def design_parts(x):
    d1, d2, d3 = split3(x)
    ones = jnp.ones(x.shape, BF16)
    return jnp.concatenate([d1, d1, d1, ones, d2, d2, d3, jnp.zeros(x.shape, BF16)], axis=0)


def factors(twice):
    twice = jnp.clip(twice, 0.02, 1.98)
    spread = twice * (2.0 - twice)
    return twice, spread * lax.rsqrt(spread)


def weigh(fitted, dosage, observed):
    twice, spread = factors(fitted)
    return observed * (dosage - twice), observed * spread


def parted(block, groups):
    block = block.astype(F32)
    height = block.shape[0] // (2 * groups)
    dosage = [block[2 * g * height : (2 * g + 1) * height] for g in range(groups)]
    present = [block[(2 * g + 1) * height : (2 * g + 2) * height] for g in range(groups)]
    if groups == 1:
        return dosage[0], present[0]
    return jnp.concatenate(dosage, axis=0), jnp.concatenate(present, axis=0)


def slot_of(source, plane, rows):
    ahead = lax.rem(source - plane + rows, rows)
    return jnp.where(lax.rem(plane, 2) == 0, ahead, lax.rem(rows - ahead, rows))


def by_even(slot, plane, rows):
    return jnp.where(lax.rem(plane, 2) == 0, plane < rows - slot, plane >= slot)


def early_kernel(rows, near, row_x_ref, col_x_ref, *refs):
    coef_refs, refs = refs[:rows], refs[rows:]
    held_ref, refs = refs[0], refs[1:]
    even, odd = refs[: rows - 2], refs[rows - 2 : 2 * rows - 4]
    piece_refs, refs = refs[2 * rows - 4 : 2 * rows - 4 + near], refs[2 * rows - 4 + near :]
    row_out, col_out, row_fit, col_fit, coef, fit = refs
    chip = coef_refs[0].shape[0]
    height = chip // rows
    space = coef.shape[0] // rows
    row = lax.axis_index("rows")
    plane = lax.axis_index("cols") // (lax.axis_size("cols") // rows)
    slots = [slot_of(plane ^ e, plane, rows) for e in range(rows)]

    @pl.when(pl.program_id(0) == 0)
    def _():
        if space != chip:
            coef[...] = jnp.zeros(coef.shape, BF16)
        for e in range(rows):
            place = pl.multiple_of(slots[e] * space, space)
            coef[pl.ds(place, chip), :] = doubled_coef(coef_refs[e][...])

    def fitted(x):
        return lax.dot_general(
            coef[...], design_parts(x), (((1,), (0,)), ((), ())), preferred_element_type=F32
        )

    if space != chip:
        row_out[...] = jnp.zeros(row_out.shape, BF16)
        col_out[...] = jnp.zeros(col_out.shape, BF16)
    fit_rows = fitted(row_x_ref[...])
    for slot in range(rows - 1):
        if slot == 0:
            block = held_ref[...]
        elif slot == 1:
            block = even[0][...]
        else:
            block = jnp.where(by_even(slot, plane, rows), even[slot - 1][...], odd[rows - slot - 1][...])
        resid, sdev = weigh(fit_rows[slot * space : slot * space + chip], *parted(block, rows))
        row_out[0, :, slot * space : slot * space + chip] = resid.astype(BF16).T
        row_out[1, :, slot * space : slot * space + chip] = sdev.astype(BF16).T
    row_fit[...] = fit_rows[(rows - 1) * space : (rows - 1) * space + chip]
    fit[...] = fitted(col_x_ref[...])
    for d in range(rows):
        for e in range(rows):
            place = pl.multiple_of(slots[e] * space + (row ^ d) * height, height)
            here = fit[pl.ds(place, height), :]
            if d < near:
                resid, sdev = weigh(here, *parted(piece_refs[d][e], 1))
                group = slots[e] * (space // height) + (row ^ d)
                col_out[0, group] = resid.astype(BF16)
                col_out[1, group] = sdev.astype(BF16)
            else:
                col_fit[e] = here


def early_call(rows, part, components, col_comps, coefs, held, even, odd, pieces):
    comps, width = col_comps.shape
    chip = coefs[0].shape[0]
    space = -(-chip // 128) * 128
    height = chip // rows
    wide = 256 if width % 256 == 0 else width
    whole = lambda i, at: (0, 0)
    block = pl.BlockSpec((2 * chip, wide), lambda i, at: (0, i))
    piece = pl.BlockSpec((rows, 2 * height, wide), lambda i, at: (0, 0, i))
    return pl.pallas_call(
        functools.partial(early_kernel_at, rows, len(pieces)),
        grid_spec=pltpu.PrefetchScalarGridSpec(
            num_scalar_prefetch=1,
            grid=(width // wide,),
            in_specs=[
                pl.BlockSpec((comps, wide), lambda i, at: (0, at[0] * (width // wide) + i)),
                pl.BlockSpec((comps, wide), lambda i, at: (0, i)),
            ]
            + [pl.BlockSpec(x.shape, whole) for x in coefs]
            + [block] * (1 + len(even) + len(odd))
            + [piece] * len(pieces),
            out_specs=(
                pl.BlockSpec((2, wide, rows * space), lambda i, at: (0, i, 0)),
                pl.BlockSpec((2, rows * space // height, height, wide), lambda i, at: (0, 0, 0, i)),
                pl.BlockSpec((chip, wide), lambda i, at: (0, i)),
                pl.BlockSpec((rows, height, wide), lambda i, at: (0, 0, i)),
            ),
            scratch_shapes=[
                pltpu.VMEM((rows * space, 2 * coefs[0].shape[1]), BF16),
                pltpu.VMEM((rows * space, wide), F32),
            ],
        ),
        out_shape=(
            jax.ShapeDtypeStruct((2, width, rows * space), BF16),
            jax.ShapeDtypeStruct((2, rows * space // height, height, width), BF16),
            jax.ShapeDtypeStruct((chip, width), F32),
            jax.ShapeDtypeStruct((rows, height, width), F32),
        ),
        compiler_params=pltpu.CompilerParams(vmem_limit_bytes=VMEM_ALL),
        name="early",
    )(part[None].astype(jnp.int32), components, col_comps, *coefs, held, *even, *odd, *pieces)


def early_kernel_at(rows, near, part_ref, *refs):
    early_kernel(rows, near, *refs)


def late_kernel(rows, group_ref, row_fit, col_fit, piece_ref, even_ref, odd_ref, *refs):
    row_out, col_out, block, row_part, col_part, block_sem, row_sems, col_sems = refs[2:]
    plane = lax.axis_index("cols") // (lax.axis_size("cols") // rows)
    last = by_even(rows - 1, plane, rows)

    @pl.when(last)
    def _():
        pltpu.make_async_copy(even_ref, block, block_sem).start()

    @pl.when(jnp.logical_not(last))
    def _():
        pltpu.make_async_copy(odd_ref, block, block_sem).start()

    copies = []
    for e in range(rows):
        resid, sdev = weigh(col_fit[e], *parted(piece_ref[e], 1))
        col_part[e, 0] = resid.astype(BF16)
        col_part[e, 1] = sdev.astype(BF16)
        for i in range(2):
            copies.append(
                pltpu.make_async_copy(col_part.at[e, i], col_out.at[i, group_ref[e]], col_sems.at[2 * e + i])
            )
            copies[-1].start()
    chip, width = row_fit.shape
    space = row_part.shape[2]
    if space != chip:
        row_part[...] = jnp.zeros(row_part.shape, BF16)
    pltpu.make_async_copy(odd_ref, block, block_sem).wait()
    wide = width // row_sems.shape[0]
    for at in range(0, width, wide):
        span = slice(at, at + wide)
        resid, sdev = weigh(row_fit[:, span], *parted(block[:, span], rows))
        row_part[0, span, 0:chip] = resid.astype(BF16).T
        row_part[1, span, 0:chip] = sdev.astype(BF16).T
        copies.append(
            pltpu.make_async_copy(
                row_part.at[:, span, :],
                row_out.at[:, span, (rows - 1) * space : rows * space],
                row_sems.at[at // wide],
            )
        )
        copies[-1].start()
    for copy in copies:
        copy.wait()


def late_call(rows, groups, row_fit, col_fit, even, odd, piece, row_panel, col_panel):
    chip, width = row_fit.shape
    height = chip // rows
    space = row_panel.shape[2] // rows
    wide = 256 if width % 256 == 0 else width
    anywhere = pl.BlockSpec(memory_space=pl.ANY)
    here = pl.BlockSpec(memory_space=pltpu.VMEM)
    return pl.pallas_call(
        functools.partial(late_kernel, rows),
        in_specs=[pl.BlockSpec(memory_space=pltpu.SMEM), here, here, here] + [anywhere] * 4,
        out_specs=(anywhere, anywhere),
        out_shape=(
            jax.ShapeDtypeStruct(row_panel.shape, BF16),
            jax.ShapeDtypeStruct(col_panel.shape, BF16),
        ),
        scratch_shapes=[
            pltpu.VMEM((2 * chip, width), BF16),
            pltpu.VMEM((2, width, space), BF16),
            pltpu.VMEM((rows, 2, height, width), BF16),
            pltpu.SemaphoreType.DMA,
            pltpu.SemaphoreType.DMA((width // wide,)),
            pltpu.SemaphoreType.DMA((2 * rows,)),
        ],
        input_output_aliases={6: 0, 7: 1},
        compiler_params=pltpu.CompilerParams(vmem_limit_bytes=VMEM_ALL),
        name="late",
    )(groups, row_fit, col_fit, piece, even, odd, row_panel, col_panel)


def quotient(numer, denom):
    inverse = pl.reciprocal(denom, approx=True)
    return numer * (inverse * (2.0 - denom * inverse))


def kin_kernel(part_ref, row_ref, col_ref, *refs):
    out_ref = refs[-1]
    numer = jnp.dot(row_ref[0], col_ref[0], preferred_element_type=F32)
    denom = jnp.dot(row_ref[1], col_ref[1], preferred_element_type=F32)
    out_ref[...] = quotient(numer, denom)


def kin_call(part, people, row_panel, col_panel, before):
    _, count, depth = row_panel.shape
    width = col_panel.shape[2]
    wide = 512 if width % 512 == 0 else width
    in_specs = [
        pl.BlockSpec((2, count, depth), lambda i, at: (0, 0, 0)),
        pl.BlockSpec((2, depth, wide), lambda i, at: (0, 0, i)),
    ]
    operands = [row_panel, col_panel]
    aliases = {}
    if before is not None:
        in_specs.append(pl.BlockSpec(memory_space=pl.ANY))
        operands.append(before)
        aliases = {len(operands): 0}
    return pl.pallas_call(
        kin_kernel,
        grid_spec=pltpu.PrefetchScalarGridSpec(
            num_scalar_prefetch=1,
            grid=(width // wide,),
            in_specs=in_specs,
            out_specs=pl.BlockSpec((count, wide), lambda i, at: (at[0], i)),
        ),
        out_shape=jax.ShapeDtypeStruct((people, width), F32),
        input_output_aliases=aliases,
        compiler_params=pltpu.CompilerParams(vmem_limit_bytes=VMEM_ALL),
        name="kinship",
    )(part[None].astype(jnp.int32), *operands)


def per_device(dosage, present, components):
    rows, cols = lax.axis_size("rows"), lax.axis_size("cols")
    ratio = cols // rows
    markers, people = dosage.shape
    comps = components.shape[0]
    width = people // ratio
    row = lax.axis_index("rows")
    col = lax.axis_index("cols")
    core, plane = col % ratio, col // ratio

    def pairs(hop):
        moves = [(z, c, *hop(z, c)) for z in range(rows) for c in range(ratio)]
        return [(z * ratio + c, y * ratio + b) for z, c, y, b in moves if 0 <= y < rows]

    def swap(x, k):
        return lax.ppermute(x, "cols", pairs(lambda z, c: (z, (c + k) % ratio))) if k else x

    def exchange(x, first):
        other = [z + 1 if (z - first) % 2 == 0 else z - 1 for z in range(rows)]
        other = [y if 0 <= y < rows else z for z, y in enumerate(other)]
        return lax.ppermute(x, "cols", pairs(lambda z, c: (other[z], c)))

    def beside(x, d):
        return lax.ppermute(x, "rows", [(i, i ^ d) for i in range(rows)]) if d else x

    def across(x, e):
        return lax.ppermute(x, "cols", pairs(lambda z, c: (z ^ e, c))) if e else x

    def by_core(parts):
        placed = []
        for p in range(ratio):
            chosen = parts[0]
            for k in range(1, ratio):
                chosen = jnp.where((core - p) % ratio == k, parts[k], chosen)
            placed.append(chosen)
        return jnp.concatenate(placed, axis=0)

    subs = rows // ratio
    fine = markers // subs
    halves = []
    for k in range(ratio):
        begin = (core + k) % ratio * width
        both = [
            lax.dynamic_slice_in_dim(x, begin, width, 1).astype(BF16).reshape(subs, 1, fine, width)
            for x in (dosage, present)
        ]
        halves.append(swap(jnp.concatenate(both, axis=1).reshape(2 * markers, width), k))
    held = by_core(halves)
    held, dosage, present = lax.optimization_barrier((held, dosage, present))
    odd = [exchange(held, 1)]
    even = [exchange(held, 0)]

    height = held.shape[0] // rows
    quarters = [beside(lax.dynamic_slice_in_dim(held, (row ^ d) * height, height, 0), d) for d in range(rows)]
    hops = [1 << i for i in range(rows.bit_length() - 1)]

    def doubled(x, hop):
        return jnp.where(((row ^ plane) & hop) == 0, x, beside(x, hop))

    gram = gram_call(dosage, present, components)
    col_comps = lax.dynamic_slice_in_dim(components, core * width, width, 1)
    quarters[1], gram, col_comps = lax.optimization_barrier((quarters[1], gram, col_comps))
    gram = gram + beside(gram, hops[0])
    col_comps = doubled(col_comps, hops[-1])
    quarters, gram, col_comps, held, odd, even = lax.optimization_barrier(
        (jnp.stack(quarters), gram, col_comps, held, odd, even)
    )
    moved = [
        across(lax.dynamic_index_in_dim(quarters, row ^ plane ^ e, 0, keepdims=False), e) for e in range(rows)
    ]
    for hop in hops[1:-1]:
        gram = gram + beside(gram, hop)
    coef = solve_call([gram, beside(gram, hops[-1])], comps, markers)
    for hop in hops[:-1]:
        col_comps = doubled(col_comps, hop)
    shares = [across(coef, e) for e in range(rows)]
    moved, shares, col_comps, held, odd, even = lax.optimization_barrier(
        (jnp.stack(moved), shares, col_comps, held, odd, even)
    )
    shares = jnp.concatenate(shares, axis=0)
    shares = [swap(shares, k) for k in range(ratio)]
    coefs = [by_core([x[e * markers : (e + 1) * markers] for x in shares]) for e in range(rows)]
    near = [moved]
    for step in range(rows - 3):
        odd, even = odd + [exchange(even[-1], 1)], even + [exchange(odd[-1], 0)]
        upto = rows - 1 if step == rows - 4 else min(rows - 1, 2 * step + 3)
        near += [beside(moved, d) for d in range(len(near), upto)]
        near, coefs, col_comps, held, odd, even = lax.optimization_barrier(
            (near, coefs, col_comps, held, odd, even)
        )
    last = exchange(odd[-1], 0)
    far = beside(near[0], rows - 1)
    row_panel, col_panel, row_fit, col_fit = early_call(
        rows, core, components, col_comps, coefs, held, even, odd, near
    )
    space = row_panel.shape[2] // rows
    groups = jnp.stack(
        [
            slot_of(plane ^ e, plane, rows) * (2 * space // height) + (row ^ (rows - 1))
            for e in range(rows)
        ]
    ).astype(jnp.int32)
    row_panel, col_panel = late_call(
        rows, groups, row_fit, col_fit, last, odd[0], far, row_panel, col_panel
    )
    col_panel = col_panel.reshape(2, rows * space, width)
    out = None
    for turn in range(ratio):
        out = kin_call((core + ratio - turn) % ratio, people, swap(row_panel, turn), col_panel, out)
    return out


def solution(mesh):
    placed = (P("cols", "rows"), P("cols", "rows"), P(None, "rows"))
    return jax.shard_map(
        per_device, mesh=mesh, in_specs=placed, out_specs=P("rows", "cols"), check_vma=False
    )
```

```python
import functools

import jax
import jax.numpy as jnp
from jax import lax
from jax.experimental import pallas as pl
from jax.experimental.pallas import tpu as pltpu
from jax.sharding import PartitionSpec as P

F32, BF16 = jnp.float32, jnp.bfloat16
VMEM_LIMIT = 56 * 1024 * 1024
VMEM_ALL = 63 * 1024 * 1024
SUB = 8


def split3(x):
    high = x.astype(BF16)
    rest = x - high.astype(F32)
    mid = rest.astype(BF16)
    low = (rest - mid.astype(F32)).astype(BF16)
    return high, mid, low


def group_starts(comps):
    starts, at = [], 0
    for j in range(comps):
        first = j // SUB * SUB
        starts.append((at, first))
        at += comps - first
    return starts, at


def gram_kernel(dosage_ref, present_ref, comps_ref, out_ref, lhs_ref):
    comps, people = comps_ref.shape
    markers = dosage_ref.shape[0]
    starts, total = group_starts(comps)
    chunk = 512 if people % 512 == 0 else people
    acc = None
    for at in range(0, people, chunk):
        span = slice(at, at + chunk)
        obs = present_ref[:, span].astype(F32)
        tgt = 0.5 * dosage_ref[:, span].astype(F32) * obs
        rhs = jnp.concatenate([obs, tgt], axis=0).astype(BF16)
        x = comps_ref[:, span]
        for j, (start, first) in enumerate(starts):
            lhs_ref[start : start + comps - first, :] = x[first:, :] * x[j : j + 1, :]
        lhs_ref[total : total + comps, :] = x
        tail = lhs_ref.shape[0] - total - comps
        lhs_ref[total + comps :, :] = jnp.ones((tail, chunk), F32)
        for part in split3(lhs_ref[...]):
            term = lax.dot_general(part, rhs, (((1,), (1,)), ((), ())), preferred_element_type=F32)
            acc = term if acc is None else acc + term
    half = total // 2
    out_ref[0:half, :] = jnp.concatenate([acc[0:half, 0:markers], acc[half:total, 0:markers]], axis=1)
    out_ref[half:, :] = acc[total : total + comps + SUB, :]


def gram_call(dosage, present, components):
    markers, people = dosage.shape
    comps = components.shape[0]
    total = group_starts(comps)[1]
    chunk = 512 if people % 512 == 0 else people
    return pl.pallas_call(
        gram_kernel,
        out_shape=jax.ShapeDtypeStruct((total // 2 + comps + SUB, 2 * markers), F32),
        scratch_shapes=[pltpu.VMEM((total + comps + 2 * SUB, chunk), F32)],
        compiler_params=pltpu.CompilerParams(vmem_limit_bytes=VMEM_LIMIT),
        name="gram",
    )(dosage, present, components)


def coef_rows(comps):
    return 4 * comps


def below(old, first, new):
    return new if first == 0 else jnp.concatenate([old[:first], new], axis=0)


def solve_kernel(comps, markers, *refs):
    out_ref = refs[-1]
    summed = refs[0][...]
    for ref in refs[1:-1]:
        summed = summed + ref[...]
    starts, total = group_starts(comps)
    half = total // 2
    left, right = summed[:, 0:markers], summed[:, markers : 2 * markers]

    def rows_of(start, count):
        if start + count <= half:
            return left[start : start + count]
        if start >= half:
            return right[start - half : start - half + count]
        return jnp.concatenate([left[start:half], right[0 : start + count - half]], axis=0)

    columns = [rows_of(start, comps - first) for start, first in starts]
    firsts = [first for _, first in starts]
    edge = left[half : half + comps]
    count = left[half + comps : half + comps + 1]
    moment = right[half : half + comps]
    moment_one = right[half + comps : half + comps + 1]
    factor, edge_f, moment_f = [], [], []
    for j in range(comps):
        first = firsts[j]
        column = columns[j]
        inv = 1.0 / column[j - first : j - first + 1]
        scaled = column * inv
        edge_j = edge[j : j + 1]
        moment_j = moment[j : j + 1]
        edge_s, moment_s = edge_j * inv, moment_j * inv
        row = lax.broadcasted_iota(jnp.int32, column.shape, 0) + first
        factor.append(jnp.where(row > j, scaled, 0.0))
        edge_f.append(edge_s)
        moment_f.append(moment_s)
        count = count - edge_s * edge_j
        moment_one = moment_one - edge_s * moment_j
        if j + 1 < comps:
            edge = below(edge, first, edge[first:] - column * edge_s)
            moment = below(moment, first, moment[first:] - column * moment_s)
        for k in range(j + 1, comps):
            offset = firsts[k] - first
            columns[k] = columns[k] - scaled[offset:] * column[k - first : k - first + 1]
    last = moment_one / count
    index = lax.broadcasted_iota(jnp.int32, (SUB, markers), 0)
    groups = [jnp.zeros((SUB, markers), F32) for _ in range(comps // SUB)]
    for j in range(comps - 1, -1, -1):
        first = firsts[j]
        value = moment_f[j] - edge_f[j] * last
        total_term = None
        for g in range(first // SUB, comps // SUB):
            term = factor[j][g * SUB - first : (g + 1) * SUB - first] * groups[g]
            total_term = term if total_term is None else total_term + term
        value = value - jnp.sum(total_term, axis=0, keepdims=True)
        g = j // SUB
        groups[g] = jnp.where(index == j - first, value, groups[g])
    coef = 2.0 * jnp.concatenate(groups, axis=0)
    last = 2.0 * last
    c1, c2, c3 = [part.astype(F32) for part in split3(coef)]
    l1, l2, l3 = [part.astype(F32) for part in split3(last)]
    index = lax.broadcasted_iota(jnp.int32, (comps, markers), 0)
    ones = jnp.where(index == 0, l1, jnp.where(index == 1, l2, jnp.where(index == 2, l3, 0.0)))
    stacked = jnp.concatenate([c1, c2, c3, ones], axis=0).astype(BF16)
    eye = (
        lax.broadcasted_iota(jnp.int32, (markers, markers), 0)
        == lax.broadcasted_iota(jnp.int32, (markers, markers), 1)
    ).astype(F32).astype(BF16)
    turned = lax.dot_general(eye, stacked, (((1,), (1,)), ((), ())), preferred_element_type=F32)
    out_ref[...] = turned.astype(BF16)


def solve_call(parts, comps, markers):
    return pl.pallas_call(
        functools.partial(solve_kernel, comps, markers),
        out_shape=jax.ShapeDtypeStruct((markers, coef_rows(comps)), BF16),
        compiler_params=pltpu.CompilerParams(vmem_limit_bytes=VMEM_LIMIT),
        name="solve",
    )(*parts)


def doubled_coef(coef):
    lanes = coef.shape[1]
    wide = coef.astype(F32)
    again = jnp.concatenate([wide[:, lanes // 2 :], wide[:, : lanes // 2]], axis=1)
    index = lax.broadcasted_iota(jnp.int32, wide.shape, 1)
    again = jnp.where(index < lanes // 2, wide, jnp.where(index < lanes // 4 * 3, again, 0.0))
    return jnp.concatenate([coef, again.astype(BF16)], axis=1)


def design_parts(x):
    d1, d2, d3 = split3(x)
    ones = jnp.ones(x.shape, BF16)
    return jnp.concatenate([d1, d1, d1, ones, d2, d2, d3, jnp.zeros(x.shape, BF16)], axis=0)


def factors(twice):
    twice = jnp.clip(twice, 0.02, 1.98)
    spread = twice * (2.0 - twice)
    return twice, spread * lax.rsqrt(spread)


def weigh(fitted, dosage, observed):
    twice, spread = factors(fitted)
    return observed * (dosage - twice), observed * spread


def parted(block, groups):
    block = block.astype(F32)
    height = block.shape[0] // (2 * groups)
    dosage = [block[2 * g * height : (2 * g + 1) * height] for g in range(groups)]
    present = [block[(2 * g + 1) * height : (2 * g + 2) * height] for g in range(groups)]
    if groups == 1:
        return dosage[0], present[0]
    return jnp.concatenate(dosage, axis=0), jnp.concatenate(present, axis=0)


def slot_of(source, plane, rows):
    ahead = lax.rem(source - plane + rows, rows)
    return jnp.where(lax.rem(plane, 2) == 0, ahead, lax.rem(rows - ahead, rows))


def by_even(slot, plane, rows):
    return jnp.where(lax.rem(plane, 2) == 0, plane < rows - slot, plane >= slot)


def early_kernel(rows, near, row_x_ref, col_x_ref, *refs):
    coef_refs, refs = refs[:rows], refs[rows:]
    held_ref, refs = refs[0], refs[1:]
    even, odd = refs[: rows - 2], refs[rows - 2 : 2 * rows - 4]
    piece_refs, refs = refs[2 * rows - 4 : 2 * rows - 4 + near], refs[2 * rows - 4 + near :]
    row_out, col_out, row_fit, col_fit, coef, fit = refs
    chip = coef_refs[0].shape[0]
    height = chip // rows
    space = coef.shape[0] // rows
    row = lax.axis_index("rows")
    plane = lax.axis_index("cols") // (lax.axis_size("cols") // rows)
    slots = [slot_of(plane ^ e, plane, rows) for e in range(rows)]

    @pl.when(pl.program_id(0) == 0)
    def _():
        if space != chip:
            coef[...] = jnp.zeros(coef.shape, BF16)
        for e in range(rows):
            place = pl.multiple_of(slots[e] * space, space)
            coef[pl.ds(place, chip), :] = doubled_coef(coef_refs[e][...])

    def fitted(x):
        return lax.dot_general(
            coef[...], design_parts(x), (((1,), (0,)), ((), ())), preferred_element_type=F32
        )

    if space != chip:
        row_out[...] = jnp.zeros(row_out.shape, BF16)
        col_out[...] = jnp.zeros(col_out.shape, BF16)
    fit_rows = fitted(row_x_ref[...])
    for slot in range(rows - 1):
        if slot == 0:
            block = held_ref[...]
        elif slot == 1:
            block = even[0][...]
        else:
            block = jnp.where(by_even(slot, plane, rows), even[slot - 1][...], odd[rows - slot - 1][...])
        resid, sdev = weigh(fit_rows[slot * space : slot * space + chip], *parted(block, rows))
        row_out[0, :, slot * space : slot * space + chip] = resid.astype(BF16).T
        row_out[1, :, slot * space : slot * space + chip] = sdev.astype(BF16).T
    row_fit[...] = fit_rows[(rows - 1) * space : (rows - 1) * space + chip]
    fit[...] = fitted(col_x_ref[...])
    for d in range(rows):
        for e in range(rows):
            place = pl.multiple_of(slots[e] * space + (row ^ d) * height, height)
            here = fit[pl.ds(place, height), :]
            if d < near:
                resid, sdev = weigh(here, *parted(piece_refs[d][e], 1))
                group = slots[e] * (space // height) + (row ^ d)
                col_out[0, group] = resid.astype(BF16)
                col_out[1, group] = sdev.astype(BF16)
            else:
                col_fit[e] = here


def early_call(rows, part, components, col_comps, coefs, held, even, odd, pieces):
    comps, width = col_comps.shape
    chip = coefs[0].shape[0]
    space = -(-chip // 128) * 128
    height = chip // rows
    wide = 256 if width % 256 == 0 else width
    whole = lambda i, at: (0, 0)
    block = pl.BlockSpec((2 * chip, wide), lambda i, at: (0, i))
    piece = pl.BlockSpec((rows, 2 * height, wide), lambda i, at: (0, 0, i))
    return pl.pallas_call(
        functools.partial(early_kernel_at, rows, len(pieces)),
        grid_spec=pltpu.PrefetchScalarGridSpec(
            num_scalar_prefetch=1,
            grid=(width // wide,),
            in_specs=[
                pl.BlockSpec((comps, wide), lambda i, at: (0, at[0] * (width // wide) + i)),
                pl.BlockSpec((comps, wide), lambda i, at: (0, i)),
            ]
            + [pl.BlockSpec(x.shape, whole) for x in coefs]
            + [block] * (1 + len(even) + len(odd))
            + [piece] * len(pieces),
            out_specs=(
                pl.BlockSpec((2, wide, rows * space), lambda i, at: (0, i, 0)),
                pl.BlockSpec((2, rows * space // height, height, wide), lambda i, at: (0, 0, 0, i)),
                pl.BlockSpec((chip, wide), lambda i, at: (0, i)),
                pl.BlockSpec((rows, height, wide), lambda i, at: (0, 0, i)),
            ),
            scratch_shapes=[
                pltpu.VMEM((rows * space, 2 * coefs[0].shape[1]), BF16),
                pltpu.VMEM((rows * space, wide), F32),
            ],
        ),
        out_shape=(
            jax.ShapeDtypeStruct((2, width, rows * space), BF16),
            jax.ShapeDtypeStruct((2, rows * space // height, height, width), BF16),
            jax.ShapeDtypeStruct((chip, width), F32),
            jax.ShapeDtypeStruct((rows, height, width), F32),
        ),
        compiler_params=pltpu.CompilerParams(vmem_limit_bytes=VMEM_ALL),
        name="early",
    )(part[None].astype(jnp.int32), components, col_comps, *coefs, held, *even, *odd, *pieces)


def early_kernel_at(rows, near, part_ref, *refs):
    early_kernel(rows, near, *refs)


def late_kernel(rows, group_ref, row_fit, col_fit, piece_ref, even_ref, odd_ref, *refs):
    row_out, col_out, block, row_part, col_part, block_sem, row_sems, col_sems = refs[2:]
    plane = lax.axis_index("cols") // (lax.axis_size("cols") // rows)
    last = by_even(rows - 1, plane, rows)

    @pl.when(last)
    def _():
        pltpu.make_async_copy(even_ref, block, block_sem).start()

    @pl.when(jnp.logical_not(last))
    def _():
        pltpu.make_async_copy(odd_ref, block, block_sem).start()

    copies = []
    for e in range(rows):
        resid, sdev = weigh(col_fit[e], *parted(piece_ref[e], 1))
        col_part[e, 0] = resid.astype(BF16)
        col_part[e, 1] = sdev.astype(BF16)
        for i in range(2):
            copies.append(
                pltpu.make_async_copy(col_part.at[e, i], col_out.at[i, group_ref[e]], col_sems.at[2 * e + i])
            )
            copies[-1].start()
    chip, width = row_fit.shape
    space = row_part.shape[2]
    if space != chip:
        row_part[...] = jnp.zeros(row_part.shape, BF16)
    pltpu.make_async_copy(odd_ref, block, block_sem).wait()
    wide = width // row_sems.shape[0]
    for at in range(0, width, wide):
        span = slice(at, at + wide)
        resid, sdev = weigh(row_fit[:, span], *parted(block[:, span], rows))
        row_part[0, span, 0:chip] = resid.astype(BF16).T
        row_part[1, span, 0:chip] = sdev.astype(BF16).T
        copies.append(
            pltpu.make_async_copy(
                row_part.at[:, span, :],
                row_out.at[:, span, (rows - 1) * space : rows * space],
                row_sems.at[at // wide],
            )
        )
        copies[-1].start()
    for copy in copies:
        copy.wait()


def late_call(rows, groups, row_fit, col_fit, even, odd, piece, row_panel, col_panel):
    chip, width = row_fit.shape
    height = chip // rows
    space = row_panel.shape[2] // rows
    wide = 256 if width % 256 == 0 else width
    anywhere = pl.BlockSpec(memory_space=pl.ANY)
    here = pl.BlockSpec(memory_space=pltpu.VMEM)
    return pl.pallas_call(
        functools.partial(late_kernel, rows),
        in_specs=[pl.BlockSpec(memory_space=pltpu.SMEM), here, here, here] + [anywhere] * 4,
        out_specs=(anywhere, anywhere),
        out_shape=(
            jax.ShapeDtypeStruct(row_panel.shape, BF16),
            jax.ShapeDtypeStruct(col_panel.shape, BF16),
        ),
        scratch_shapes=[
            pltpu.VMEM((2 * chip, width), BF16),
            pltpu.VMEM((2, width, space), BF16),
            pltpu.VMEM((rows, 2, height, width), BF16),
            pltpu.SemaphoreType.DMA,
            pltpu.SemaphoreType.DMA((width // wide,)),
            pltpu.SemaphoreType.DMA((2 * rows,)),
        ],
        input_output_aliases={6: 0, 7: 1},
        compiler_params=pltpu.CompilerParams(vmem_limit_bytes=VMEM_ALL),
        name="late",
    )(groups, row_fit, col_fit, piece, even, odd, row_panel, col_panel)


def quotient(numer, denom):
    inverse = pl.reciprocal(denom, approx=True)
    return numer * (inverse * (2.0 - denom * inverse))


def kin_kernel(part_ref, row_ref, col_ref, *refs):
    out_ref = refs[-1]
    numer = jnp.dot(row_ref[0], col_ref[0], preferred_element_type=F32)
    denom = jnp.dot(row_ref[1], col_ref[1], preferred_element_type=F32)
    out_ref[...] = quotient(numer, denom)


def kin_call(part, people, row_panel, col_panel, before):
    _, count, depth = row_panel.shape
    width = col_panel.shape[2]
    wide = 768 if width % 768 == 0 else width
    in_specs = [
        pl.BlockSpec((2, count, depth), lambda i, at: (0, 0, 0)),
        pl.BlockSpec((2, depth, wide), lambda i, at: (0, 0, i)),
    ]
    operands = [row_panel, col_panel]
    aliases = {}
    if before is not None:
        in_specs.append(pl.BlockSpec(memory_space=pl.ANY))
        operands.append(before)
        aliases = {len(operands): 0}
    return pl.pallas_call(
        kin_kernel,
        grid_spec=pltpu.PrefetchScalarGridSpec(
            num_scalar_prefetch=1,
            grid=(width // wide,),
            in_specs=in_specs,
            out_specs=pl.BlockSpec((count, wide), lambda i, at: (at[0], i)),
        ),
        out_shape=jax.ShapeDtypeStruct((people, width), F32),
        input_output_aliases=aliases,
        compiler_params=pltpu.CompilerParams(vmem_limit_bytes=VMEM_ALL),
        name="kinship",
    )(part[None].astype(jnp.int32), *operands)


def per_device(dosage, present, components):
    rows, cols = lax.axis_size("rows"), lax.axis_size("cols")
    ratio = cols // rows
    markers, people = dosage.shape
    comps = components.shape[0]
    width = people // ratio
    row = lax.axis_index("rows")
    col = lax.axis_index("cols")
    core, plane = col % ratio, col // ratio

    def pairs(hop):
        moves = [(z, c, *hop(z, c)) for z in range(rows) for c in range(ratio)]
        return [(z * ratio + c, y * ratio + b) for z, c, y, b in moves if 0 <= y < rows]

    def swap(x, k):
        return lax.ppermute(x, "cols", pairs(lambda z, c: (z, (c + k) % ratio))) if k else x

    def exchange(x, first):
        other = [z + 1 if (z - first) % 2 == 0 else z - 1 for z in range(rows)]
        other = [y if 0 <= y < rows else z for z, y in enumerate(other)]
        return lax.ppermute(x, "cols", pairs(lambda z, c: (other[z], c)))

    def beside(x, d):
        return lax.ppermute(x, "rows", [(i, i ^ d) for i in range(rows)]) if d else x

    def across(x, e):
        return lax.ppermute(x, "cols", pairs(lambda z, c: (z ^ e, c))) if e else x

    def by_core(parts):
        placed = []
        for p in range(ratio):
            chosen = parts[0]
            for k in range(1, ratio):
                chosen = jnp.where((core - p) % ratio == k, parts[k], chosen)
            placed.append(chosen)
        return jnp.concatenate(placed, axis=0)

    subs = rows // ratio
    fine = markers // subs
    halves = []
    for k in range(ratio):
        begin = (core + k) % ratio * width
        both = [
            lax.dynamic_slice_in_dim(x, begin, width, 1).astype(BF16).reshape(subs, 1, fine, width)
            for x in (dosage, present)
        ]
        halves.append(swap(jnp.concatenate(both, axis=1).reshape(2 * markers, width), k))
    held = by_core(halves)
    held, dosage, present = lax.optimization_barrier((held, dosage, present))
    odd = [exchange(held, 1)]
    even = [exchange(held, 0)]

    height = held.shape[0] // rows
    quarters = [beside(lax.dynamic_slice_in_dim(held, (row ^ d) * height, height, 0), d) for d in range(rows)]
    hops = [1 << i for i in range(rows.bit_length() - 1)]

    def doubled(x, hop):
        return jnp.where(((row ^ plane) & hop) == 0, x, beside(x, hop))

    gram = gram_call(dosage, present, components)
    col_comps = lax.dynamic_slice_in_dim(components, core * width, width, 1)
    quarters[1], gram, col_comps = lax.optimization_barrier((quarters[1], gram, col_comps))
    gram = gram + beside(gram, hops[0])
    col_comps = doubled(col_comps, hops[-1])
    quarters, gram, col_comps, held, odd, even = lax.optimization_barrier(
        (jnp.stack(quarters), gram, col_comps, held, odd, even)
    )
    moved = [
        across(lax.dynamic_index_in_dim(quarters, row ^ plane ^ e, 0, keepdims=False), e) for e in range(rows)
    ]
    for hop in hops[1:-1]:
        gram = gram + beside(gram, hop)
    coef = solve_call([gram, beside(gram, hops[-1])], comps, markers)
    for hop in hops[:-1]:
        col_comps = doubled(col_comps, hop)
    shares = [across(coef, e) for e in range(rows)]
    moved, shares, col_comps, held, odd, even = lax.optimization_barrier(
        (jnp.stack(moved), shares, col_comps, held, odd, even)
    )
    shares = jnp.concatenate(shares, axis=0)
    shares = [swap(shares, k) for k in range(ratio)]
    coefs = [by_core([x[e * markers : (e + 1) * markers] for x in shares]) for e in range(rows)]
    near = [moved]
    for step in range(rows - 3):
        odd, even = odd + [exchange(even[-1], 1)], even + [exchange(odd[-1], 0)]
        upto = rows - 1 if step == rows - 4 else min(rows - 1, 2 * step + 3)
        near += [beside(moved, d) for d in range(len(near), upto)]
        near, coefs, col_comps, held, odd, even = lax.optimization_barrier(
            (near, coefs, col_comps, held, odd, even)
        )
    last = exchange(odd[-1], 0)
    far = beside(near[0], rows - 1)
    row_panel, col_panel, row_fit, col_fit = early_call(
        rows, core, components, col_comps, coefs, held, even, odd, near
    )
    space = row_panel.shape[2] // rows
    groups = jnp.stack(
        [
            slot_of(plane ^ e, plane, rows) * (2 * space // height) + (row ^ (rows - 1))
            for e in range(rows)
        ]
    ).astype(jnp.int32)
    row_panel, col_panel = late_call(
        rows, groups, row_fit, col_fit, last, odd[0], far, row_panel, col_panel
    )
    col_panel = col_panel.reshape(2, rows * space, width)
    out = None
    for turn in range(ratio):
        out = kin_call((core + ratio - turn) % ratio, people, swap(row_panel, turn), col_panel, out)
    return out


def solution(mesh):
    placed = (P("cols", "rows"), P("cols", "rows"), P(None, "rows"))
    return jax.shard_map(
        per_device, mesh=mesh, in_specs=placed, out_specs=P("rows", "cols"), check_vma=False
    )
```

```python
import functools

import jax
import jax.numpy as jnp
from jax import lax
from jax.experimental import pallas as pl
from jax.experimental.pallas import tpu as pltpu
from jax.sharding import PartitionSpec as P

F32, BF16 = jnp.float32, jnp.bfloat16
VMEM_LIMIT = 56 * 1024 * 1024
VMEM_ALL = 63 * 1024 * 1024
SUB = 8


def split3(x):
    high = x.astype(BF16)
    rest = x - high.astype(F32)
    mid = rest.astype(BF16)
    low = (rest - mid.astype(F32)).astype(BF16)
    return high, mid, low


def group_starts(comps):
    starts, at = [], 0
    for j in range(comps):
        first = j // SUB * SUB
        starts.append((at, first))
        at += comps - first
    return starts, at


def gram_kernel(dosage_ref, present_ref, comps_ref, out_ref, lhs_ref):
    comps, people = comps_ref.shape
    markers = dosage_ref.shape[0]
    starts, total = group_starts(comps)
    chunk = 512 if people % 512 == 0 else people
    acc = None
    for at in range(0, people, chunk):
        span = slice(at, at + chunk)
        obs = present_ref[:, span].astype(F32)
        tgt = 0.5 * dosage_ref[:, span].astype(F32) * obs
        rhs = jnp.concatenate([obs, tgt], axis=0).astype(BF16)
        x = comps_ref[:, span]
        for j, (start, first) in enumerate(starts):
            lhs_ref[start : start + comps - first, :] = x[first:, :] * x[j : j + 1, :]
        lhs_ref[total : total + comps, :] = x
        tail = lhs_ref.shape[0] - total - comps
        lhs_ref[total + comps :, :] = jnp.ones((tail, chunk), F32)
        for part in split3(lhs_ref[...]):
            term = lax.dot_general(part, rhs, (((1,), (1,)), ((), ())), preferred_element_type=F32)
            acc = term if acc is None else acc + term
    half = total // 2
    out_ref[0:half, :] = jnp.concatenate([acc[0:half, 0:markers], acc[half:total, 0:markers]], axis=1)
    out_ref[half:, :] = acc[total : total + comps + SUB, :]


def gram_call(dosage, present, components):
    markers, people = dosage.shape
    comps = components.shape[0]
    total = group_starts(comps)[1]
    chunk = 512 if people % 512 == 0 else people
    return pl.pallas_call(
        gram_kernel,
        out_shape=jax.ShapeDtypeStruct((total // 2 + comps + SUB, 2 * markers), F32),
        scratch_shapes=[pltpu.VMEM((total + comps + 2 * SUB, chunk), F32)],
        compiler_params=pltpu.CompilerParams(vmem_limit_bytes=VMEM_LIMIT),
        name="gram",
    )(dosage, present, components)


def coef_rows(comps):
    return 4 * comps


def below(old, first, new):
    return new if first == 0 else jnp.concatenate([old[:first], new], axis=0)


def solve_kernel(comps, markers, *refs):
    out_ref = refs[-1]
    summed = refs[0][...]
    for ref in refs[1:-1]:
        summed = summed + ref[...]
    starts, total = group_starts(comps)
    half = total // 2
    left, right = summed[:, 0:markers], summed[:, markers : 2 * markers]

    def rows_of(start, count):
        if start + count <= half:
            return left[start : start + count]
        if start >= half:
            return right[start - half : start - half + count]
        return jnp.concatenate([left[start:half], right[0 : start + count - half]], axis=0)

    columns = [rows_of(start, comps - first) for start, first in starts]
    firsts = [first for _, first in starts]
    edge = left[half : half + comps]
    count = left[half + comps : half + comps + 1]
    moment = right[half : half + comps]
    moment_one = right[half + comps : half + comps + 1]
    factor, edge_f, moment_f = [], [], []
    for j in range(comps):
        first = firsts[j]
        column = columns[j]
        pivot = column[j - first : j - first + 1]
        inv = pl.reciprocal(pivot, approx=True)
        for _ in range(2):
            inv = inv * (2.0 - pivot * inv)
        scaled = column * inv
        edge_j = edge[j : j + 1]
        moment_j = moment[j : j + 1]
        edge_s, moment_s = edge_j * inv, moment_j * inv
        row = lax.broadcasted_iota(jnp.int32, column.shape, 0) + first
        factor.append(jnp.where(row > j, scaled, 0.0))
        edge_f.append(edge_s)
        moment_f.append(moment_s)
        count = count - edge_s * edge_j
        moment_one = moment_one - edge_s * moment_j
        if j + 1 < comps:
            edge = below(edge, first, edge[first:] - column * edge_s)
            moment = below(moment, first, moment[first:] - column * moment_s)
        for k in range(j + 1, comps):
            offset = firsts[k] - first
            columns[k] = columns[k] - scaled[offset:] * column[k - first : k - first + 1]
    last = moment_one / count
    index = lax.broadcasted_iota(jnp.int32, (SUB, markers), 0)
    groups = [jnp.zeros((SUB, markers), F32) for _ in range(comps // SUB)]
    for j in range(comps - 1, -1, -1):
        first = firsts[j]
        value = moment_f[j] - edge_f[j] * last
        total_term = None
        for g in range(first // SUB, comps // SUB):
            term = factor[j][g * SUB - first : (g + 1) * SUB - first] * groups[g]
            total_term = term if total_term is None else total_term + term
        value = value - jnp.sum(total_term, axis=0, keepdims=True)
        g = j // SUB
        groups[g] = jnp.where(index == j - first, value, groups[g])
    coef = 2.0 * jnp.concatenate(groups, axis=0)
    last = 2.0 * last
    c1, c2, c3 = [part.astype(F32) for part in split3(coef)]
    l1, l2, l3 = [part.astype(F32) for part in split3(last)]
    index = lax.broadcasted_iota(jnp.int32, (comps, markers), 0)
    ones = jnp.where(index == 0, l1, jnp.where(index == 1, l2, jnp.where(index == 2, l3, 0.0)))
    stacked = jnp.concatenate([c1, c2, c3, ones], axis=0).astype(BF16)
    eye = (
        lax.broadcasted_iota(jnp.int32, (markers, markers), 0)
        == lax.broadcasted_iota(jnp.int32, (markers, markers), 1)
    ).astype(F32).astype(BF16)
    turned = lax.dot_general(eye, stacked, (((1,), (1,)), ((), ())), preferred_element_type=F32)
    out_ref[...] = turned.astype(BF16)


def solve_call(parts, comps, markers):
    return pl.pallas_call(
        functools.partial(solve_kernel, comps, markers),
        out_shape=jax.ShapeDtypeStruct((markers, coef_rows(comps)), BF16),
        compiler_params=pltpu.CompilerParams(vmem_limit_bytes=VMEM_LIMIT),
        name="solve",
    )(*parts)


def doubled_coef(coef):
    lanes = coef.shape[1]
    wide = coef.astype(F32)
    again = jnp.concatenate([wide[:, lanes // 2 :], wide[:, : lanes // 2]], axis=1)
    index = lax.broadcasted_iota(jnp.int32, wide.shape, 1)
    again = jnp.where(index < lanes // 2, wide, jnp.where(index < lanes // 4 * 3, again, 0.0))
    return jnp.concatenate([coef, again.astype(BF16)], axis=1)


def design_parts(x):
    d1, d2, d3 = split3(x)
    ones = jnp.ones(x.shape, BF16)
    return jnp.concatenate([d1, d1, d1, ones, d2, d2, d3, jnp.zeros(x.shape, BF16)], axis=0)


def factors(twice):
    twice = jnp.clip(twice, 0.02, 1.98)
    spread = twice * (2.0 - twice)
    return twice, spread * lax.rsqrt(spread)


def weigh(fitted, dosage, observed):
    twice, spread = factors(fitted)
    return observed * (dosage - twice), observed * spread


def parted(block, groups):
    block = block.astype(F32)
    height = block.shape[0] // (2 * groups)
    dosage = [block[2 * g * height : (2 * g + 1) * height] for g in range(groups)]
    present = [block[(2 * g + 1) * height : (2 * g + 2) * height] for g in range(groups)]
    if groups == 1:
        return dosage[0], present[0]
    return jnp.concatenate(dosage, axis=0), jnp.concatenate(present, axis=0)


def slot_of(source, plane, rows):
    ahead = lax.rem(source - plane + rows, rows)
    return jnp.where(lax.rem(plane, 2) == 0, ahead, lax.rem(rows - ahead, rows))


def by_even(slot, plane, rows):
    return jnp.where(lax.rem(plane, 2) == 0, plane < rows - slot, plane >= slot)


def early_kernel(rows, near, row_x_ref, col_x_ref, *refs):
    coef_refs, refs = refs[:rows], refs[rows:]
    held_ref, refs = refs[0], refs[1:]
    even, odd = refs[: rows - 2], refs[rows - 2 : 2 * rows - 4]
    piece_refs, refs = refs[2 * rows - 4 : 2 * rows - 4 + near], refs[2 * rows - 4 + near :]
    row_out, col_out, row_fit, col_fit, coef, fit = refs
    chip = coef_refs[0].shape[0]
    height = chip // rows
    space = coef.shape[0] // rows
    row = lax.axis_index("rows")
    plane = lax.axis_index("cols") // (lax.axis_size("cols") // rows)
    slots = [slot_of(plane ^ e, plane, rows) for e in range(rows)]

    @pl.when(pl.program_id(0) == 0)
    def _():
        if space != chip:
            coef[...] = jnp.zeros(coef.shape, BF16)
        for e in range(rows):
            place = pl.multiple_of(slots[e] * space, space)
            coef[pl.ds(place, chip), :] = doubled_coef(coef_refs[e][...])

    def fitted(x):
        return lax.dot_general(
            coef[...], design_parts(x), (((1,), (0,)), ((), ())), preferred_element_type=F32
        )

    if space != chip:
        row_out[...] = jnp.zeros(row_out.shape, BF16)
        col_out[...] = jnp.zeros(col_out.shape, BF16)
    fit_rows = fitted(row_x_ref[...])
    for slot in range(rows - 1):
        if slot == 0:
            block = held_ref[...]
        elif slot == 1:
            block = even[0][...]
        else:
            block = jnp.where(by_even(slot, plane, rows), even[slot - 1][...], odd[rows - slot - 1][...])
        resid, sdev = weigh(fit_rows[slot * space : slot * space + chip], *parted(block, rows))
        row_out[0, :, slot * space : slot * space + chip] = resid.astype(BF16).T
        row_out[1, :, slot * space : slot * space + chip] = sdev.astype(BF16).T
    row_fit[...] = fit_rows[(rows - 1) * space : (rows - 1) * space + chip]
    fit[...] = fitted(col_x_ref[...])
    for d in range(rows):
        for e in range(rows):
            place = pl.multiple_of(slots[e] * space + (row ^ d) * height, height)
            here = fit[pl.ds(place, height), :]
            if d < near:
                resid, sdev = weigh(here, *parted(piece_refs[d][e], 1))
                group = slots[e] * (space // height) + (row ^ d)
                col_out[0, group] = resid.astype(BF16)
                col_out[1, group] = sdev.astype(BF16)
            else:
                col_fit[e] = here


def early_call(rows, part, components, col_comps, coefs, held, even, odd, pieces):
    comps, width = col_comps.shape
    chip = coefs[0].shape[0]
    space = -(-chip // 128) * 128
    height = chip // rows
    wide = 256 if width % 256 == 0 else width
    whole = lambda i, at: (0, 0)
    block = pl.BlockSpec((2 * chip, wide), lambda i, at: (0, i))
    piece = pl.BlockSpec((rows, 2 * height, wide), lambda i, at: (0, 0, i))
    return pl.pallas_call(
        functools.partial(early_kernel_at, rows, len(pieces)),
        grid_spec=pltpu.PrefetchScalarGridSpec(
            num_scalar_prefetch=1,
            grid=(width // wide,),
            in_specs=[
                pl.BlockSpec((comps, wide), lambda i, at: (0, at[0] * (width // wide) + i)),
                pl.BlockSpec((comps, wide), lambda i, at: (0, i)),
            ]
            + [pl.BlockSpec(x.shape, whole) for x in coefs]
            + [block] * (1 + len(even) + len(odd))
            + [piece] * len(pieces),
            out_specs=(
                pl.BlockSpec((2, wide, rows * space), lambda i, at: (0, i, 0)),
                pl.BlockSpec((2, rows * space // height, height, wide), lambda i, at: (0, 0, 0, i)),
                pl.BlockSpec((chip, wide), lambda i, at: (0, i)),
                pl.BlockSpec((rows, height, wide), lambda i, at: (0, 0, i)),
            ),
            scratch_shapes=[
                pltpu.VMEM((rows * space, 2 * coefs[0].shape[1]), BF16),
                pltpu.VMEM((rows * space, wide), F32),
            ],
        ),
        out_shape=(
            jax.ShapeDtypeStruct((2, width, rows * space), BF16),
            jax.ShapeDtypeStruct((2, rows * space // height, height, width), BF16),
            jax.ShapeDtypeStruct((chip, width), F32),
            jax.ShapeDtypeStruct((rows, height, width), F32),
        ),
        compiler_params=pltpu.CompilerParams(vmem_limit_bytes=VMEM_ALL),
        name="early",
    )(part[None].astype(jnp.int32), components, col_comps, *coefs, held, *even, *odd, *pieces)


def early_kernel_at(rows, near, part_ref, *refs):
    early_kernel(rows, near, *refs)


def late_kernel(rows, group_ref, row_fit, col_fit, piece_ref, even_ref, odd_ref, *refs):
    row_out, col_out, block, row_part, col_part, block_sem, row_sems, col_sems = refs[2:]
    plane = lax.axis_index("cols") // (lax.axis_size("cols") // rows)
    last = by_even(rows - 1, plane, rows)

    @pl.when(last)
    def _():
        pltpu.make_async_copy(even_ref, block, block_sem).start()

    @pl.when(jnp.logical_not(last))
    def _():
        pltpu.make_async_copy(odd_ref, block, block_sem).start()

    copies = []
    for e in range(rows):
        resid, sdev = weigh(col_fit[e], *parted(piece_ref[e], 1))
        col_part[e, 0] = resid.astype(BF16)
        col_part[e, 1] = sdev.astype(BF16)
        for i in range(2):
            copies.append(
                pltpu.make_async_copy(col_part.at[e, i], col_out.at[i, group_ref[e]], col_sems.at[2 * e + i])
            )
            copies[-1].start()
    chip, width = row_fit.shape
    space = row_part.shape[2]
    if space != chip:
        row_part[...] = jnp.zeros(row_part.shape, BF16)
    pltpu.make_async_copy(odd_ref, block, block_sem).wait()
    wide = width // row_sems.shape[0]
    for at in range(0, width, wide):
        span = slice(at, at + wide)
        resid, sdev = weigh(row_fit[:, span], *parted(block[:, span], rows))
        row_part[0, span, 0:chip] = resid.astype(BF16).T
        row_part[1, span, 0:chip] = sdev.astype(BF16).T
        copies.append(
            pltpu.make_async_copy(
                row_part.at[:, span, :],
                row_out.at[:, span, (rows - 1) * space : rows * space],
                row_sems.at[at // wide],
            )
        )
        copies[-1].start()
    for copy in copies:
        copy.wait()


def late_call(rows, groups, row_fit, col_fit, even, odd, piece, row_panel, col_panel):
    chip, width = row_fit.shape
    height = chip // rows
    space = row_panel.shape[2] // rows
    wide = 256 if width % 256 == 0 else width
    anywhere = pl.BlockSpec(memory_space=pl.ANY)
    here = pl.BlockSpec(memory_space=pltpu.VMEM)
    return pl.pallas_call(
        functools.partial(late_kernel, rows),
        in_specs=[pl.BlockSpec(memory_space=pltpu.SMEM), here, here, here] + [anywhere] * 4,
        out_specs=(anywhere, anywhere),
        out_shape=(
            jax.ShapeDtypeStruct(row_panel.shape, BF16),
            jax.ShapeDtypeStruct(col_panel.shape, BF16),
        ),
        scratch_shapes=[
            pltpu.VMEM((2 * chip, width), BF16),
            pltpu.VMEM((2, width, space), BF16),
            pltpu.VMEM((rows, 2, height, width), BF16),
            pltpu.SemaphoreType.DMA,
            pltpu.SemaphoreType.DMA((width // wide,)),
            pltpu.SemaphoreType.DMA((2 * rows,)),
        ],
        input_output_aliases={6: 0, 7: 1},
        compiler_params=pltpu.CompilerParams(vmem_limit_bytes=VMEM_ALL),
        name="late",
    )(groups, row_fit, col_fit, piece, even, odd, row_panel, col_panel)


def quotient(numer, denom):
    inverse = pl.reciprocal(denom, approx=True)
    return numer * (inverse * (2.0 - denom * inverse))


def kin_kernel(part_ref, row_ref, col_ref, *refs):
    out_ref = refs[-1]
    numer = jnp.dot(row_ref[0], col_ref[0], preferred_element_type=F32)
    denom = jnp.dot(row_ref[1], col_ref[1], preferred_element_type=F32)
    out_ref[...] = quotient(numer, denom)


def kin_call(part, people, row_panel, col_panel, before):
    _, count, depth = row_panel.shape
    width = col_panel.shape[2]
    wide = 512 if width % 512 == 0 else width
    in_specs = [
        pl.BlockSpec((2, count, depth), lambda i, at: (0, 0, 0)),
        pl.BlockSpec((2, depth, wide), lambda i, at: (0, 0, i)),
    ]
    operands = [row_panel, col_panel]
    aliases = {}
    if before is not None:
        in_specs.append(pl.BlockSpec(memory_space=pl.ANY))
        operands.append(before)
        aliases = {len(operands): 0}
    return pl.pallas_call(
        kin_kernel,
        grid_spec=pltpu.PrefetchScalarGridSpec(
            num_scalar_prefetch=1,
            grid=(width // wide,),
            in_specs=in_specs,
            out_specs=pl.BlockSpec((count, wide), lambda i, at: (at[0], i)),
        ),
        out_shape=jax.ShapeDtypeStruct((people, width), F32),
        input_output_aliases=aliases,
        compiler_params=pltpu.CompilerParams(vmem_limit_bytes=VMEM_ALL),
        name="kinship",
    )(part[None].astype(jnp.int32), *operands)


def per_device(dosage, present, components):
    rows, cols = lax.axis_size("rows"), lax.axis_size("cols")
    ratio = cols // rows
    markers, people = dosage.shape
    comps = components.shape[0]
    width = people // ratio
    row = lax.axis_index("rows")
    col = lax.axis_index("cols")
    core, plane = col % ratio, col // ratio

    def pairs(hop):
        moves = [(z, c, *hop(z, c)) for z in range(rows) for c in range(ratio)]
        return [(z * ratio + c, y * ratio + b) for z, c, y, b in moves if 0 <= y < rows]

    def swap(x, k):
        return lax.ppermute(x, "cols", pairs(lambda z, c: (z, (c + k) % ratio))) if k else x

    def exchange(x, first):
        other = [z + 1 if (z - first) % 2 == 0 else z - 1 for z in range(rows)]
        other = [y if 0 <= y < rows else z for z, y in enumerate(other)]
        return lax.ppermute(x, "cols", pairs(lambda z, c: (other[z], c)))

    def beside(x, d):
        return lax.ppermute(x, "rows", [(i, i ^ d) for i in range(rows)]) if d else x

    def across(x, e):
        return lax.ppermute(x, "cols", pairs(lambda z, c: (z ^ e, c))) if e else x

    def by_core(parts):
        placed = []
        for p in range(ratio):
            chosen = parts[0]
            for k in range(1, ratio):
                chosen = jnp.where((core - p) % ratio == k, parts[k], chosen)
            placed.append(chosen)
        return jnp.concatenate(placed, axis=0)

    subs = rows // ratio
    fine = markers // subs
    halves = []
    for k in range(ratio):
        begin = (core + k) % ratio * width
        both = [
            lax.dynamic_slice_in_dim(x, begin, width, 1).astype(BF16).reshape(subs, 1, fine, width)
            for x in (dosage, present)
        ]
        halves.append(swap(jnp.concatenate(both, axis=1).reshape(2 * markers, width), k))
    held = by_core(halves)
    held, dosage, present = lax.optimization_barrier((held, dosage, present))
    odd = [exchange(held, 1)]
    even = [exchange(held, 0)]

    height = held.shape[0] // rows
    quarters = [beside(lax.dynamic_slice_in_dim(held, (row ^ d) * height, height, 0), d) for d in range(rows)]
    hops = [1 << i for i in range(rows.bit_length() - 1)]

    def doubled(x, hop):
        return jnp.where(((row ^ plane) & hop) == 0, x, beside(x, hop))

    gram = gram_call(dosage, present, components)
    col_comps = lax.dynamic_slice_in_dim(components, core * width, width, 1)
    quarters[1], gram, col_comps = lax.optimization_barrier((quarters[1], gram, col_comps))
    gram = gram + beside(gram, hops[0])
    col_comps = doubled(col_comps, hops[-1])
    quarters, gram, col_comps, held, odd, even = lax.optimization_barrier(
        (jnp.stack(quarters), gram, col_comps, held, odd, even)
    )
    moved = [
        across(lax.dynamic_index_in_dim(quarters, row ^ plane ^ e, 0, keepdims=False), e) for e in range(rows)
    ]
    for hop in hops[1:-1]:
        gram = gram + beside(gram, hop)
    coef = solve_call([gram, beside(gram, hops[-1])], comps, markers)
    for hop in hops[:-1]:
        col_comps = doubled(col_comps, hop)
    shares = [across(coef, e) for e in range(rows)]
    moved, shares, col_comps, held, odd, even = lax.optimization_barrier(
        (jnp.stack(moved), shares, col_comps, held, odd, even)
    )
    shares = jnp.concatenate(shares, axis=0)
    shares = [swap(shares, k) for k in range(ratio)]
    coefs = [by_core([x[e * markers : (e + 1) * markers] for x in shares]) for e in range(rows)]
    near = [moved]
    for step in range(rows - 3):
        odd, even = odd + [exchange(even[-1], 1)], even + [exchange(odd[-1], 0)]
        upto = rows - 1 if step == rows - 4 else min(rows - 1, 2 * step + 3)
        near += [beside(moved, d) for d in range(len(near), upto)]
        near, coefs, col_comps, held, odd, even = lax.optimization_barrier(
            (near, coefs, col_comps, held, odd, even)
        )
    last = exchange(odd[-1], 0)
    far = beside(near[0], rows - 1)
    row_panel, col_panel, row_fit, col_fit = early_call(
        rows, core, components, col_comps, coefs, held, even, odd, near
    )
    space = row_panel.shape[2] // rows
    groups = jnp.stack(
        [
            slot_of(plane ^ e, plane, rows) * (2 * space // height) + (row ^ (rows - 1))
            for e in range(rows)
        ]
    ).astype(jnp.int32)
    row_panel, col_panel = late_call(
        rows, groups, row_fit, col_fit, last, odd[0], far, row_panel, col_panel
    )
    col_panel = col_panel.reshape(2, rows * space, width)
    out = None
    for turn in range(ratio):
        out = kin_call((core + ratio - turn) % ratio, people, swap(row_panel, turn), col_panel, out)
    return out


def solution(mesh):
    placed = (P("cols", "rows"), P("cols", "rows"), P(None, "rows"))
    return jax.shard_map(
        per_device, mesh=mesh, in_specs=placed, out_specs=P("rows", "cols"), check_vma=False
    )
```
